32 devices in a mesh: band: 4 (over y, core), slab: 8 (over z, x).
Axes of the slice: x: 2, y: 2, z: 4, core: 2. Of those that a mesh axis runs over, the one named last changes fastest.
Arguments:
- bands: float32 [2, 256, 32768], P(None, ('band', 'slab')), may hold values from -6 to 6
- projectors: float32 [4096, 512], P('slab'), may hold values from -0.625 to 0.625
- slot_atom: int32 [4096], P('slab'), may hold values from -1 to 767, as said below
- slot_box: int32 [4096], P('slab'), may hold values from 0 to 63
- channels: int32 [768], replicated, may hold values from 1 to 8
- coupling: float32 [8, 8, 768], replicated, may hold values from -2 to 2
Outputs:
- applied: float32 [2, 256, 32768], P(None, ('band', 'slab'))
The draws below stay inside these ranges and needn't reach their ends.
Inputs may be any that keep to these rules, and one draw needn't show every extreme that they name: `slot_atom`: atom a is owned by slab a // 96. A live slot k names an atom owned by slab k // 512 or by the slab before it, cyclically. In each slab's 512 slots the live ones come first; some slab has all of its slots live.
All inputs are finite; a program needn't handle non-finite values.
Results may differ from the reference program's by a relative error of at most 0.0003.
Values sent between devices are 32-bit elements; how exact they have to be, the bound alone decides.
No kernel may reach another device: no remote copies, remote signals or barrier semaphores. Data moves between devices by JAX's collectives and lax.ppermute only.
A program may use at most 128 MiB of HBM per device.

```python
import jax
import jax.numpy as jnp
from jax import lax

NBLOCK = 2
BANDS = 256
CH = 8
BOXPTS = 64
BOX_DEV = 64
ATOM_DEV = 96
BLK_DEV = 512
NBLK = 4096
NATOM = 768
NGRID = 32768
N_SLAB = 8


def slot_tables(key):
    slabs = NBLK // BLK_DEV
    keys = jax.random.split(key, 6)
    full = jax.random.randint(keys[0], (), 0, slabs)
    lowest = BLK_DEV // 8
    spread = BLK_DEV - lowest
    first_draw = jax.random.randint(keys[1], (slabs,), 0, spread + 1)
    second_draw = jax.random.randint(keys[2], (slabs,), 0, spread + 1)
    live_count = lowest + first_draw * second_draw // spread
    slab_ids = jnp.arange(slabs, dtype=jnp.int32)
    live_count = jnp.where(slab_ids == full, BLK_DEV, live_count)
    live_count = jnp.where(slab_ids == (full + 1) % slabs, lowest, live_count)
    slot = jnp.arange(NBLK, dtype=jnp.int32)
    slab_of = slot // BLK_DEV
    position = slot % BLK_DEV
    backward = jax.random.randint(keys[3], (NBLK,), 0, 2)
    within = jax.random.randint(keys[4], (NBLK,), 0, ATOM_DEV)
    atom = (slab_of - backward) % slabs * ATOM_DEV + within
    boxes = jax.random.randint(keys[5], (NBLK,), 0, BOX_DEV)
    marked = slot == NBLK - BLK_DEV
    atom = jnp.where(marked, NATOM - 1, atom)
    boxes = jnp.where(marked, BOX_DEV - 1, boxes)
    live = position < live_count[slab_of]
    atom = jnp.where(live, atom, -1)
    return (atom.astype(jnp.int32), boxes.astype(jnp.int32))


def draw_slot_atom(key, part):
    return slot_tables(jax.random.fold_in(key, 7))[0]


def draw_slot_box(key, part):
    return slot_tables(jax.random.fold_in(key, 7))[1]


def touch_ends(drawn, key, smallest, high):
    index_at = [jax.random.randint(jax.random.fold_in(key, axis), (), 0, length) for axis, length in enumerate(drawn.shape)]
    longest = drawn.shape.index(max(drawn.shape))
    beside = index_at[:longest] + [(index_at[longest] + 1) % drawn.shape[longest]] + index_at[longest + 1:]
    return drawn.at[tuple(index_at)].set(smallest).at[tuple(beside)].set(high)


def shard_levels(rng, shape, cuts, least, high):
    def one(dim, parts):
        heights = jax.random.uniform(jax.random.fold_in(jax.random.fold_in(rng, 6), dim), (parts,), jnp.float32, least / len(cuts), high / len(cuts))
        return jnp.repeat(jnp.exp(heights), shape[dim] // parts).reshape((-1,) + (1,) * (len(shape) - dim - 1))

    loudness = one(*cuts[0])
    for cut in cuts[1:]:
        loudness = loudness * one(*cut)
    return loudness


def gaussian(own_key, dims, deviation, most, cuts=(), kind=jnp.bfloat16):
    level = shard_levels(own_key, dims, cuts, -0.22, 0.18) if cuts else 1.0
    values = jax.random.normal(own_key, dims, jnp.float32) * deviation * level
    return jnp.minimum(jnp.maximum(values, -most), most).astype(kind)


def setup_inputs(seed: int = 0) -> dict:
    key_list = jax.random.split(jax.random.key(seed), 7)
    return {
        "bands": gaussian(key_list[0], (NBLOCK, BANDS, NGRID), 1.0, 6.0, ((1, 32),), jnp.float32),
        "projectors": gaussian(key_list[1], (NBLK, CH * BOXPTS), 0.1, 0.625, ((0, 8),), jnp.float32),
        "slot_atom": draw_slot_atom(jax.random.fold_in(key_list[6], 71), 0),
        "slot_box": draw_slot_box(jax.random.fold_in(key_list[6], 71), 0),
        "channels": touch_ends(jax.random.randint(key_list[4], (NATOM,), 1, CH + 1), jax.random.fold_in(key_list[4], 1), 1, CH).astype(jnp.int32),
        "coupling": gaussian(key_list[5], (CH, CH, NATOM), 0.35, 2.0, (), jnp.float32),
    }


def reference(bands, projectors, slot_atom, slot_box, channels, coupling):
    nblock, nband, ngrid = bands.shape
    highest = lax.Precision.HIGHEST
    slab_bands = bands.reshape(nblock, nband, N_SLAB, BOX_DEV, BOXPTS).transpose(2, 0, 1, 3, 4)
    beta_all = projectors.reshape(N_SLAB, BLK_DEV, CH, BOXPTS)
    atoms_all = slot_atom.reshape(N_SLAB, BLK_DEV)
    boxes_all = slot_box.reshape(N_SLAB, BLK_DEV).astype(jnp.int32)

    def project(carry, inputs):
        slab, beta, atoms, boxes = inputs
        live = (atoms >= 0).astype(slab.dtype)
        safe = jnp.where(atoms >= 0, atoms, 0).astype(jnp.int32)
        patches = jnp.take(slab, boxes, axis=2)
        term = jnp.einsum('nbkg,kcg->kncb', patches, beta, precision=highest)
        term = term * live[:, None, None, None]
        return carry + jax.ops.segment_sum(term, safe, num_segments=NATOM), None

    start = jnp.zeros((NATOM, nblock, CH, nband), bands.dtype)
    proj, _ = lax.scan(project, start, (slab_bands, beta_all, atoms_all, boxes_all))
    mask = (jnp.arange(CH, dtype=jnp.int32)[None, :] < channels[:, None]).astype(bands.dtype)
    masked = proj * mask[:, None, :, None]
    coef = jnp.einsum('cea,aneb->ancb', coupling, masked, precision=highest) * mask[:, None, :, None]

    def apply(inputs):
        beta, atoms, boxes = inputs
        live = (atoms >= 0).astype(bands.dtype)
        safe = jnp.where(atoms >= 0, atoms, 0).astype(jnp.int32)
        per_slot = jnp.take(coef, safe, axis=0) * live[:, None, None, None]
        contrib = jnp.einsum('kncb,kcg->nbkg', per_slot, beta, precision=highest)
        out = jnp.zeros((nblock, nband, BOX_DEV, BOXPTS), bands.dtype)
        return out.at[:, :, boxes, :].add(contrib)

    slabs_out = lax.map(apply, (beta_all, atoms_all, boxes_all))
    return slabs_out.transpose(1, 2, 0, 3, 4).reshape(nblock, nband, ngrid)
```

```python
import functools
import math

import jax
import jax.numpy as jnp
import numpy as np
from jax import lax
from jax.experimental import pallas as pl
from jax.experimental.pallas import tpu as pltpu
from jax.sharding import PartitionSpec as P

BOXPTS = 64
GROUP = 16
AXES = ("band", "slab")
MIB = 1 << 20


def round_up(value, step):
    return (value + step - 1) // step * step


def cycle_tables(nslab):
    order = list(range(0, nslab, 2)) + list(range(nslab - 1 - nslab % 2, 0, -2))
    place = {s: i for i, s in enumerate(order)}
    return order, place


def params(limit):
    return pltpu.CompilerParams(vmem_limit_bytes=limit)


VMEM = pl.BlockSpec(memory_space=pltpu.VMEM)
SMEM = pl.BlockSpec(memory_space=pltpu.SMEM)
ANY = pl.BlockSpec(memory_space=pl.ANY)


def split_bands_kernel(x_ref, out_ref):
    rows = x_ref.shape[0]
    low_half = lax.broadcasted_iota(jnp.int32, (rows, 128), 1) < BOXPTS
    zero = jnp.zeros((rows, 128), jnp.float32)

    def step(pair, carry):
        x = x_ref[:, pl.ds(pl.multiple_of(pair * 128, 128), 128)]
        high = x.astype(jnp.bfloat16).astype(jnp.float32)
        low = x - high
        high_turned = pltpu.roll(high, BOXPTS, 1)
        low_turned = pltpu.roll(low, BOXPTS, 1)
        out_ref[2 * pair, :, 0:128] = jnp.where(low_half, high, high_turned).astype(jnp.bfloat16)
        out_ref[2 * pair, :, 128:256] = jnp.where(low_half, low, zero).astype(jnp.bfloat16)
        out_ref[2 * pair + 1, :, 0:128] = jnp.where(low_half, high_turned, high).astype(jnp.bfloat16)
        out_ref[2 * pair + 1, :, 128:256] = jnp.where(low_half, low_turned, zero).astype(jnp.bfloat16)
        return carry

    lax.fori_loop(0, x_ref.shape[1] // 128, step, 0, unroll=4)


def split_bands(x):
    rows, ngrid = x.shape
    shape = (ngrid // BOXPTS, rows, 256)
    return pl.pallas_call(
        split_bands_kernel,
        out_shape=jax.ShapeDtypeStruct(shape, jnp.bfloat16),
        in_specs=[VMEM],
        out_specs=VMEM,
        compiler_params=params(40 * MIB),
        cost_estimate=pl.CostEstimate(flops=8 * x.size, bytes_accessed=12 * x.size, transcendentals=0),
        name="split_bands",
    )(x)


def split_slots(values, low_half):
    parts = []
    for t in range(values.shape[1] // 128):
        x = values[:, t * 128 : (t + 1) * 128]
        high = x.astype(jnp.bfloat16).astype(jnp.float32)
        low = x - high
        parts.append(jnp.where(low_half, high, pltpu.roll(low, BOXPTS, 1)).astype(jnp.bfloat16))
        parts.append(jnp.where(low_half, pltpu.roll(high, BOXPTS, 1), low).astype(jnp.bfloat16))
    return jnp.concatenate(parts, axis=0)


def high_only(tile):
    lanes = lax.broadcasted_iota(jnp.int32, tile.shape, 1)
    return jnp.where(lanes < BOXPTS, tile.astype(jnp.float32), 0.0).astype(jnp.bfloat16)


def live_groups(live, start, length):
    return lax.div(jnp.clip(live - start, 0, length) + (GROUP - 1), GROUP)


def project_kernel(slots, npiece, first, place_ref, live_ref, box_ref, x_ref, *refs):
    pieces, outs = refs[:npiece], refs[npiece:]
    rows = x_ref.shape[1]
    boxes = x_ref.shape[0] // live_ref.shape[0]
    width = pieces[0].shape[1] // BOXPTS * GROUP
    low_half = lax.broadcasted_iota(jnp.int32, (GROUP, 128), 1) < BOXPTS
    lane_slot = lax.broadcasted_iota(jnp.int32, (rows, width), 1) % GROUP
    for i, (piece, out) in enumerate(zip(pieces, outs)):
        slab = place_ref[2 * (first + i)]
        start = place_ref[2 * (first + i) + 1]
        count = live_groups(live_ref[slab], start, piece.shape[0])
        slot_base = slab * slots + start
        box_base = slab * boxes
        out[...] = jnp.zeros(out.shape, jnp.float32)

        def step(g, carry):
            values = piece[pl.ds(pl.multiple_of(g * GROUP, GROUP), GROUP), :]
            tile = split_slots(values, low_half)
            weights = jnp.concatenate([tile, high_only(tile)], axis=1)
            patches = jnp.concatenate(
                [x_ref[box_base + box_ref[slot_base + g * GROUP + s]] for s in range(GROUP)], axis=0
            )
            product = lax.dot_general(
                patches, weights, (((1,), (1,)), ((), ())), preferred_element_type=jnp.float32
            )
            total = product[0:rows]
            for s in range(1, GROUP):
                total = jnp.where(lane_slot == s, product[s * rows : (s + 1) * rows], total)
            out[g] = total
            return carry

        lax.fori_loop(0, count, step, 0)


def project(pieces, first, place, live, box, x, slots):
    width = pieces[0].shape[1] // BOXPTS * GROUP
    shapes = [
        jax.ShapeDtypeStruct((p.shape[0] // GROUP, x.shape[1], width), jnp.float32) for p in pieces
    ]
    work = sum(p.size for p in pieces)
    return pl.pallas_call(
        functools.partial(project_kernel, slots, len(pieces), first),
        out_shape=shapes,
        in_specs=[SMEM, SMEM, SMEM, VMEM] + [VMEM] * len(pieces),
        out_specs=[VMEM] * len(pieces),
        compiler_params=params(40 * MIB),
        cost_estimate=pl.CostEstimate(
            flops=2 * 16 * work, bytes_accessed=4 * work + 2 * x.size, transcendentals=0
        ),
        name="project",
    )(place, live, box, x, *pieces)


def swap_blocks(tiles, lane_block, width):
    tiles = list(tiles)
    bit = 1
    while bit < len(tiles):
        upper = (lane_block & bit) != 0
        for i in range(len(tiles)):
            if not i & bit:
                a, b = tiles[i], tiles[i | bit]
                tiles[i] = jnp.where(upper, pltpu.roll(b, GROUP * bit, 1), a)
                tiles[i | bit] = jnp.where(upper, b, pltpu.roll(a, width - GROUP * bit, 1))
        bit *= 2
    return tiles


def stacked_split(value):
    high = value.astype(jnp.bfloat16)
    low = (value - high.astype(jnp.float32)).astype(jnp.bfloat16)
    return jnp.concatenate([high, low], axis=0)


def apply_kernel(
    nslab, slots, npiece, place_ref, live_ref, box_ref, column_ref, coupling_ref, *refs
):
    pieces, projections = refs[:npiece], refs[npiece : 2 * npiece]
    out_ref = refs[2 * npiece]
    beta, proj, parts, sums, beta_sem, proj_sem, out_sem = refs[2 * npiece + 1 :]
    groups = slots // GROUP
    rows, width = proj.shape[1], proj.shape[2]
    channel = width // GROUP
    lanes = parts.shape[2] // 2
    boxes = out_ref.shape[1] // BOXPTS // nslab
    chunk = width // GROUP
    copies = []
    for i in range(npiece):
        slab, start = place_ref[2 * i], place_ref[2 * i + 1]
        first = slab * groups + lax.div(start, GROUP)
        count = projections[i].shape[0]
        copies.append(
            pltpu.make_async_copy(projections[i], proj.at[pl.ds(first, count)], proj_sem.at[i])
        )
        copies[-1].start()
    beta_copies = []
    for i in range(npiece):
        slab, start = place_ref[2 * i], place_ref[2 * i + 1]
        count = pieces[i].shape[0]
        first = pl.multiple_of(slab * slots + start, GROUP)
        beta_copies.append(
            pltpu.make_async_copy(pieces[i], beta.at[pl.ds(first, count), :], beta_sem.at[i])
        )
        beta_copies[-1].start()
    for c in copies:
        c.wait()

    lane_block = lax.broadcasted_iota(jnp.int32, (rows, width), 1) // GROUP
    atom_row = lax.broadcasted_iota(jnp.int32, (2 * lanes, slots), 0)

    def selector(slab):
        column = jnp.broadcast_to(column_ref[slab], (2 * lanes, slots))
        return jnp.where(column == atom_row, 1.0, 0.0).astype(jnp.bfloat16)

    def sum_by_atom(slab, carry):
        by_channel = [[] for _ in range(channel)]
        for k in range(groups // chunk):
            tiles = [proj[slab * groups + k * chunk + i] for i in range(chunk)]
            for c, tile in enumerate(swap_blocks(tiles, lane_block, width)):
                by_channel[c].append(tile)
        value = jnp.concatenate([jnp.concatenate(t, axis=1) for t in by_channel], axis=0)
        both = lax.dot_general(
            stacked_split(value),
            selector(slab),
            (((1,), (1,)), ((), ())),
            preferred_element_type=jnp.float32,
        )
        half = both.shape[0] // 2
        parts[slab] = both[:half] + both[half:]
        return carry

    lax.fori_loop(0, nslab, sum_by_atom, 0)

    def couple(slab, carry):
        following = lax.rem(slab + 1, nslab)
        total = parts[slab, :, lanes:] + parts[following, :, :lanes]
        for c in range(channel):
            mixed = jnp.zeros((rows, lanes), jnp.float32)
            for e in range(channel):
                factor = coupling_ref[slab, pl.ds(c * channel + e, 1), :]
                mixed = mixed + factor * total[e * rows : (e + 1) * rows]
            parts[slab, c * rows : (c + 1) * rows, lanes:] = mixed
        return carry

    lax.fori_loop(0, nslab, couple, 0)

    def spread(slab, carry):
        below = lax.rem(slab + nslab - 1, nslab)
        value = jnp.concatenate([parts[below, :, lanes:], parts[slab, :, lanes:]], axis=1)
        both = jnp.dot(stacked_split(value), selector(slab), preferred_element_type=jnp.float32)
        half = both.shape[0] // 2
        value = both[:half] + both[half:]
        for k in range(groups // chunk):
            tiles = [
                value[c * rows : (c + 1) * rows, k * width : (k + 1) * width]
                for c in range(channel)
            ]
            for i, tile in enumerate(swap_blocks(tiles, lane_block, width)):
                proj[slab * groups + k * chunk + i] = tile
        return carry

    lax.fori_loop(0, nslab, spread, 0)

    nsum = sums.shape[0]
    for j in range(nsum):
        sums[j] = jnp.zeros(sums.shape[1:], jnp.float32)
    for c in beta_copies:
        c.wait()

    low_half = lax.broadcasted_iota(jnp.int32, (GROUP, 128), 1) < BOXPTS
    lane_slot = lax.broadcasted_iota(jnp.int32, (rows, width), 1) % GROUP

    def slab_step(slab, carry):
        def step(g, inner):
            slot_base = slab * slots + g * GROUP
            values = beta[pl.ds(pl.multiple_of(slot_base, GROUP), GROUP), :]
            tile = split_slots(values, low_half)
            weights = jnp.concatenate([tile, high_only(tile)], axis=0)
            c = proj[slab * groups + g]
            high = c.astype(jnp.bfloat16).astype(jnp.float32)
            low = c - high
            left = jnp.concatenate(
                [
                    jnp.concatenate(
                        [
                            jnp.where(lane_slot == s, high, 0.0).astype(jnp.bfloat16),
                            jnp.where(lane_slot == s, low, 0.0).astype(jnp.bfloat16),
                        ],
                        axis=1,
                    )
                    for s in range(GROUP)
                ],
                axis=0,
            )
            product = jnp.dot(left, weights, preferred_element_type=jnp.float32)
            for s in range(GROUP):
                box = slab * boxes + box_ref[slot_base + s]
                sums[s % nsum, box] = sums[s % nsum, box] + product[s * rows : (s + 1) * rows]
            return inner

        lax.fori_loop(0, live_groups(live_ref[slab], 0, slots), step, 0)
        return carry

    lax.fori_loop(0, nslab, slab_step, 0)
    pair_half = lax.broadcasted_iota(jnp.int32, (rows, 128), 1) < BOXPTS

    span = beta.shape[1]

    def leaving(k):
        return pltpu.make_async_copy(
            beta.at[pl.ds(pl.multiple_of(k * rows, GROUP), rows), :],
            out_ref.at[:, pl.ds(pl.multiple_of(k * span, 128), span)],
            out_sem.at[k],
        )

    def finish(k, carry):
        for pair in range(span // 128):
            folded = []
            for i in range(2):
                box = k * (span // BOXPTS) + 2 * pair + i
                value = sums[0, box]
                for j in range(1, nsum):
                    value = value + sums[j, box]
                folded.append(value + pltpu.roll(value, BOXPTS, 1))
            beta[pl.ds(pl.multiple_of(k * rows, GROUP), rows), pair * 128 : (pair + 1) * 128] = (
                jnp.where(pair_half, folded[0], folded[1])
            )
        leaving(k).start()
        return carry

    def leave(k, carry):
        leaving(k).wait()
        return carry

    lax.fori_loop(0, out_ref.shape[1] // span, finish, 0)
    lax.fori_loop(0, out_ref.shape[1] // span, leave, 0)


def apply(pieces, projections, place, live, box, column, coupling, nslab, slots, rows, ngrid):
    width = projections[0].shape[2]
    lanes = coupling.shape[2]
    one_sum = ngrid // BOXPTS * rows * 128 * 4
    nsum = 2 if one_sum <= 8 * MIB else 1
    npiece = len(pieces)
    scratch = [
        pltpu.VMEM((nslab * slots, pieces[0].shape[1]), jnp.float32),
        pltpu.VMEM((nslab * slots // GROUP, rows, width), jnp.float32),
        pltpu.VMEM((nslab, width // GROUP * rows, 2 * lanes), jnp.float32),
        pltpu.VMEM((nsum, ngrid // BOXPTS, rows, 128), jnp.float32),
        pltpu.SemaphoreType.DMA((npiece,)),
        pltpu.SemaphoreType.DMA((npiece,)),
        pltpu.SemaphoreType.DMA((ngrid // pieces[0].shape[1],)),
    ]
    need = 4 * sum(math.prod(s.shape) for s in scratch[:4])
    return pl.pallas_call(
        functools.partial(apply_kernel, nslab, slots, npiece),
        out_shape=jax.ShapeDtypeStruct((rows, ngrid), jnp.float32),
        in_specs=[SMEM, SMEM, SMEM, VMEM, VMEM] + [ANY] * (2 * npiece),
        out_specs=ANY,
        scratch_shapes=scratch,
        compiler_params=params(min(need + 4 * MIB, 63 * MIB)),
        name="apply",
    )(place, live, box, column, coupling, *pieces, *projections)


def piece_table(nband, nslab, slots):
    order, place = cycle_tables(nslab)
    half = slots // 2
    quarter = half // 2
    reach = nslab // 2
    table = []
    for band in range(nband):
        core = band % 2
        for slab in range(nslab):
            at = lambda distance: order[(place[slab] + distance) % nslab]
            rows = [(slab, 0)]
            for step in range(1, reach):
                for c in (core, 1 - core):
                    rows += [(at(-step), c * half), (at(step), c * half)]
            for c in (core, 1 - core):
                rows += [(at(reach), c * half), (at(reach), c * half + quarter)]
            table.append(rows)
    return np.array(table, np.int32)


def gather_pieces(projectors, nband, nslab):
    slots = projectors.shape[0]
    order, place = cycle_tables(nslab)
    half = slots // 2
    quarter = half // 2
    reach = nslab // 2
    onward = [
        (b * nslab + order[i], b * nslab + order[(i + 1) % nslab])
        for b in range(nband)
        for i in range(nslab)
    ]
    backward = [(d, s) for s, d in onward]
    sibling = [(b * nslab + s, (b ^ 1) * nslab + s) for b in range(nband) for s in range(nslab)]
    core = lax.rem(lax.axis_index("band"), 2)
    mine = lax.dynamic_slice_in_dim(projectors, core * half, half, 0)
    steps = [[projectors]]
    up = down = mine
    for step in range(1, reach):
        up = lax.ppermute(up, AXES, onward)
        down = lax.ppermute(down, AXES, backward)
        steps.append([up, down])
        steps.append([lax.ppermute(up, AXES, sibling), lax.ppermute(down, AXES, sibling)])
    up = lax.ppermute(up[:quarter], AXES, onward)
    down = lax.ppermute(down[quarter:], AXES, backward)
    steps.append([up, down])
    steps.append([lax.ppermute(up, AXES, sibling), lax.ppermute(down, AXES, sibling)])
    return steps


def body(bands, projectors, slot_atom, slot_box, channels, coupling):
    nblock, band_local, ngrid = bands.shape
    nband, nslab = lax.axis_size("band"), lax.axis_size("slab")
    natoms = channels.shape[0]
    atom_dev = natoms // nslab
    channel = coupling.shape[0]
    slots = slot_atom.shape[0]
    lanes = round_up(atom_dev, 128)

    steps = gather_pieces(projectors, nband, nslab)
    table = jnp.asarray(piece_table(nband, nslab, slots))
    me = lax.axis_index("band") * nslab + lax.axis_index("slab")
    place = lax.dynamic_index_in_dim(table, me, 0, keepdims=False).reshape(-1)

    both = lax.all_gather(jnp.stack([slot_atom, slot_box]), "slab")
    atoms, box = both[:, 0], both[:, 1].reshape(-1)
    live = jnp.sum((atoms >= 0).astype(jnp.int32), axis=1)
    slab_ids = jnp.arange(nslab, dtype=jnp.int32)
    relative = (atoms - ((slab_ids - 1) % nslab * atom_dev)[:, None]) % natoms
    column = jnp.where(relative < atom_dev, relative, relative + (lanes - atom_dev))
    column = jnp.where(atoms >= 0, column, -1)[:, None, :]

    mask = (jnp.arange(channel, dtype=jnp.int32)[:, None] < channels[None, :]).astype(jnp.float32)
    masked = coupling * mask[:, None, :] * mask[None, :, :]
    masked = masked.reshape(channel * channel, nslab, atom_dev).transpose(1, 0, 2)
    masked = jnp.pad(masked, ((0, 0), (0, 0), (0, lanes - atom_dev)))

    rows = nblock * band_local
    padded = round_up(rows, GROUP)
    x = bands.reshape(rows, ngrid)
    if padded != rows:
        x = jnp.pad(x, ((0, padded - rows), (0, 0)))
    split = split_bands(x)
    pieces, projections = [], []
    for step in steps:
        projections += project(step, len(pieces), place, live, box, split, slots)
        pieces += step
    out = apply(
        pieces, projections, place, live, box, column, masked, nslab, slots, padded, ngrid
    )
    return out[:rows].reshape(nblock, band_local, ngrid)


def solution(mesh):
    in_specs = (P(None, ("band", "slab"), None), P("slab", None), P("slab"), P("slab"), P(), P())
    out_specs = P(None, ("band", "slab"), None)
    return jax.shard_map(body, mesh=mesh, in_specs=in_specs, out_specs=out_specs, check_vma=False)
```

```python
import collections
import functools
import math

import jax
import jax.numpy as jnp
import numpy as np
from jax import lax
from jax.experimental import pallas as pl
from jax.experimental.pallas import tpu as pltpu
from jax.sharding import PartitionSpec as P

BOXPTS = 64
GROUP = 16
INFO = 8
UNROLL = 4
AXES = ("band", "slab")
MIB = 1 << 20


def round_up(value, step):
    return (value + step - 1) // step * step


def cycle_tables(nslab):
    order = list(range(0, nslab, 2)) + list(range(nslab - 1 - nslab % 2, 0, -2))
    place = {s: i for i, s in enumerate(order)}
    return order, place


def params(limit):
    return pltpu.CompilerParams(vmem_limit_bytes=limit)


VMEM = pl.BlockSpec(memory_space=pltpu.VMEM)
SMEM = pl.BlockSpec(memory_space=pltpu.SMEM)
ANY = pl.BlockSpec(memory_space=pl.ANY)


def split_bands_kernel(x_ref, out_ref):
    rows = x_ref.shape[0]
    low_half = lax.broadcasted_iota(jnp.int32, (rows, 128), 1) < BOXPTS
    zero = jnp.zeros((rows, 128), jnp.float32)

    def step(pair, carry):
        x = x_ref[:, pl.ds(pl.multiple_of(pair * 128, 128), 128)]
        high = x.astype(jnp.bfloat16).astype(jnp.float32)
        low = x - high
        high_turned = pltpu.roll(high, BOXPTS, 1)
        low_turned = pltpu.roll(low, BOXPTS, 1)
        out_ref[2 * pair, :, 0:128] = jnp.where(low_half, high, high_turned).astype(jnp.bfloat16)
        out_ref[2 * pair, :, 128:256] = jnp.where(low_half, low, zero).astype(jnp.bfloat16)
        out_ref[2 * pair + 1, :, 0:128] = jnp.where(low_half, high_turned, high).astype(jnp.bfloat16)
        out_ref[2 * pair + 1, :, 128:256] = jnp.where(low_half, low_turned, zero).astype(jnp.bfloat16)
        return carry

    lax.fori_loop(0, x_ref.shape[1] // 128, step, 0, unroll=4)


def split_bands(x):
    rows, ngrid = x.shape
    shape = (ngrid // BOXPTS, rows, 256)
    return pl.pallas_call(
        split_bands_kernel,
        out_shape=jax.ShapeDtypeStruct(shape, jnp.bfloat16),
        in_specs=[VMEM],
        out_specs=VMEM,
        compiler_params=params(40 * MIB),
        cost_estimate=pl.CostEstimate(flops=8 * x.size, bytes_accessed=12 * x.size, transcendentals=0),
        name="split_bands",
    )(x)


def slot_weights(values, low_half, axis):
    full, top = [], []
    for t in range(values.shape[1] // 128):
        x = values[:, t * 128 : (t + 1) * 128]
        high = x.astype(jnp.bfloat16).astype(jnp.float32)
        low = x - high
        turned = pltpu.roll(high, BOXPTS, 1)
        full.append(jnp.where(low_half, high, pltpu.roll(low, BOXPTS, 1)).astype(jnp.bfloat16))
        full.append(jnp.where(low_half, turned, low).astype(jnp.bfloat16))
        top.append(jnp.where(low_half, high, 0.0).astype(jnp.bfloat16))
        top.append(jnp.where(low_half, turned, 0.0).astype(jnp.bfloat16))
    return jnp.concatenate(
        [jnp.concatenate(full, axis=0), jnp.concatenate(top, axis=0)], axis=axis
    )


def live_groups(live, start, length):
    return lax.div(jnp.clip(live - start, 0, length) + (GROUP - 1), GROUP)


def describe(slot_atom, slot_box, slab, nslab, natoms, width, lanes):
    atom_dev = natoms // nslab
    relative = (slot_atom - (slab + nslab - 1) % nslab * atom_dev) % natoms
    column = jnp.where(relative < atom_dev, relative, relative + (lanes - atom_dev))
    column = jnp.where(slot_atom >= 0, column, -1)
    live = jnp.broadcast_to(jnp.sum((slot_atom >= 0).astype(jnp.int32)), slot_atom.shape)
    rows = jnp.stack([slot_box, live, column]).astype(jnp.float32)
    return jnp.pad(rows, ((0, INFO - rows.shape[0]), (0, width - rows.shape[1])))


def project_kernel(pieces, infos, place_ref, x_ref, *refs):
    arrays = refs[: -len(pieces) - 3]
    outs = refs[-len(pieces) - 3 : -3]
    whole, table, sem = refs[-3:]
    copies = []
    for k, index in enumerate(infos):
        whole[k] = arrays[index][0:INFO, :].astype(jnp.int32)
        copies.append(pltpu.make_async_copy(whole.at[k], table.at[k], sem.at[k]))
        copies[-1].start()
    rows = x_ref.shape[1]
    width = outs[0].shape[2]
    low_half = lax.broadcasted_iota(jnp.int32, (GROUP, 128), 1) < BOXPTS
    lane_slot = lax.broadcasted_iota(jnp.int32, (rows, width), 1) % GROUP
    for out in outs:
        out[...] = jnp.zeros(out.shape, jnp.float32)
    for c in copies:
        c.wait()
    for p, out in zip(pieces, outs):
        array = arrays[p.array]
        start = place_ref[3 * p.index + 1]
        box_base = place_ref[3 * p.index + 2]
        info = infos.index(p.info)
        count = live_groups(table[info, 1, 0], start, p.rows)

        def step(block, carry):
            groups = [block * UNROLL + u for u in range(UNROLL)]
            weights, patches = [], []
            for g in groups:
                first = pl.multiple_of(p.offset + g * GROUP, 8)
                weights.append(slot_weights(array[pl.ds(first, GROUP), :], low_half, 1))
                boxes = [table[info, 0, start + g * GROUP + s] for s in range(GROUP)]
                patches.append(jnp.concatenate([x_ref[box_base + b] for b in boxes], axis=0))
            totals = []
            for w, p_ in zip(weights, patches):
                product = lax.dot_general(
                    p_, w, (((1,), (1,)), ((), ())), preferred_element_type=jnp.float32
                )
                total = product[0:rows]
                for s in range(1, GROUP):
                    total = jnp.where(lane_slot == s, product[s * rows : (s + 1) * rows], total)
                totals.append(total)
            for g, total in zip(groups, totals):
                out[g] = total
            return carry

        lax.fori_loop(0, lax.div(count + (UNROLL - 1), UNROLL), step, 0)


def project(arrays, pieces, place, x):
    channel = arrays[0].shape[1] // BOXPTS
    used = sorted({p.array for p in pieces} | {p.info for p in pieces})
    local = [
        p._replace(array=used.index(p.array), info=used.index(p.info)) for p in pieces
    ]
    infos = sorted({p.info for p in local})
    shapes = [
        jax.ShapeDtypeStruct((p.rows // GROUP, x.shape[1], channel * GROUP), jnp.float32)
        for p in pieces
    ]
    size = sum(p.rows for p in pieces) * arrays[0].shape[1]
    table = (len(infos), INFO, arrays[0].shape[1])
    return pl.pallas_call(
        functools.partial(project_kernel, local, infos),
        out_shape=shapes,
        in_specs=[SMEM, VMEM] + [VMEM] * len(used),
        out_specs=[VMEM] * len(pieces),
        scratch_shapes=[
            pltpu.VMEM(table, jnp.int32),
            pltpu.SMEM(table, jnp.int32),
            pltpu.SemaphoreType.DMA((len(infos),)),
        ],
        compiler_params=params(40 * MIB),
        cost_estimate=pl.CostEstimate(
            flops=2 * 16 * 16 * size, bytes_accessed=4 * size + 2 * x.size, transcendentals=0
        ),
        name="project",
    )(place, x, *[arrays[i] for i in used])


def swap_blocks(tiles, lane_block, width):
    tiles = list(tiles)
    bit = 1
    while bit < len(tiles):
        upper = (lane_block & bit) != 0
        for i in range(len(tiles)):
            if not i & bit:
                a, b = tiles[i], tiles[i | bit]
                tiles[i] = jnp.where(upper, pltpu.roll(b, GROUP * bit, 1), a)
                tiles[i | bit] = jnp.where(upper, b, pltpu.roll(a, width - GROUP * bit, 1))
        bit *= 2
    return tiles


def stacked_split(value):
    high = value.astype(jnp.bfloat16)
    low = (value - high.astype(jnp.float32)).astype(jnp.bfloat16)
    return jnp.concatenate([high, low], axis=0)


def apply_kernel(nslab, slots, pieces, infos, place_ref, coupling_ref, *refs):
    npiece = len(pieces)
    proj, parts, beta, sums, done, masks, info, whole, table = refs[-13:-4]
    beta_sem, proj_sem, info_sem, out_sem = refs[-4:]
    out_ref = refs[-14]
    projections = refs[-14 - npiece : -14]
    arrays = refs[: -14 - npiece]
    groups = slots // GROUP
    rows, width = proj.shape[1], proj.shape[2]
    channel = width // GROUP
    lanes = parts.shape[2] // 2
    boxes = out_ref.shape[1] // BOXPTS // nslab
    chunk = width // GROUP
    info_copies, copies, beta_copies = [], [], []
    for i, (array, index) in enumerate(infos):
        slab = place_ref[3 * index]
        info_copies.append(
            pltpu.make_async_copy(arrays[array].at[0:INFO, :], info.at[slab], info_sem.at[i])
        )
    for i, p in enumerate(pieces):
        slab, start = place_ref[3 * p.index], place_ref[3 * p.index + 1]
        first = slab * groups + lax.div(start, GROUP)
        copies.append(
            pltpu.make_async_copy(
                projections[i], proj.at[pl.ds(first, p.rows // GROUP)], proj_sem.at[i]
            )
        )
        first = pl.multiple_of(slab * slots + start, GROUP)
        beta_copies.append(
            pltpu.make_async_copy(
                arrays[p.array].at[p.offset : p.offset + p.rows, :],
                beta.at[pl.ds(first, p.rows), :],
                beta_sem.at[i],
            )
        )
    for c in info_copies + copies + beta_copies:
        c.start()
    lane_slot = lax.broadcasted_iota(jnp.int32, (rows, width), 1) % GROUP
    for s in range(GROUP):
        masks[s] = jnp.where(lane_slot == s, 1.0, 0.0).astype(jnp.bfloat16)
    for c in info_copies:
        c.wait()
    whole[...] = info[...].astype(jnp.int32)
    to_scalars = pltpu.make_async_copy(whole, table, info_sem.at[0])
    to_scalars.start()
    for j in range(sums.shape[0]):
        sums[j] = jnp.zeros(sums.shape[1:], jnp.float32)
    parts[...] = jnp.zeros(parts.shape, jnp.float32)
    to_scalars.wait()
    for c in copies:
        c.wait()

    lane_block = lax.broadcasted_iota(jnp.int32, (rows, width), 1) // GROUP
    atom_row = lax.broadcasted_iota(jnp.int32, (2 * lanes, width), 0).astype(jnp.float32)

    def selector(slab, k):
        first = pl.multiple_of(k * width, 128)
        column = jnp.broadcast_to(info[slab, 2:3, pl.ds(first, width)], (2 * lanes, width))
        return jnp.where(column == atom_row, 1.0, 0.0).astype(jnp.bfloat16)

    def chunks(slab):
        return lax.div(table[slab, 1, 0] + (width - 1), width)

    def sum_by_atom(slab, carry):
        def step(k, inner):
            first = slab * groups + k * chunk
            tiles = [proj[first + i] for i in range(chunk)]
            value = jnp.concatenate(swap_blocks(tiles, lane_block, width), axis=0)
            both = lax.dot_general(
                stacked_split(value),
                selector(slab, k),
                (((1,), (1,)), ((), ())),
                preferred_element_type=jnp.float32,
            )
            half = both.shape[0] // 2
            parts[slab] = parts[slab] + (both[:half] + both[half:])
            return inner

        lax.fori_loop(0, chunks(slab), step, 0)
        return carry

    lax.fori_loop(0, nslab, sum_by_atom, 0)

    def couple(slab, carry):
        following = lax.rem(slab + 1, nslab)
        total = parts[slab, :, lanes:] + parts[following, :, :lanes]
        for c in range(channel):
            mixed = jnp.zeros((rows, lanes), jnp.float32)
            for e in range(channel):
                factor = coupling_ref[slab, pl.ds(c * channel + e, 1), :]
                mixed = mixed + factor * total[e * rows : (e + 1) * rows]
            parts[slab, c * rows : (c + 1) * rows, lanes:] = mixed
        return carry

    lax.fori_loop(0, nslab, couple, 0)

    def spread(slab, carry):
        below = lax.rem(slab + nslab - 1, nslab)
        value = jnp.concatenate([parts[below, :, lanes:], parts[slab, :, lanes:]], axis=1)
        value = stacked_split(value)

        def step(k, inner):
            both = jnp.dot(value, selector(slab, k), preferred_element_type=jnp.float32)
            half = both.shape[0] // 2
            both = both[:half] + both[half:]
            tiles = [both[c * rows : (c + 1) * rows] for c in range(channel)]
            for i, tile in enumerate(swap_blocks(tiles, lane_block, width)):
                proj[slab * groups + k * chunk + i] = tile
            return inner

        lax.fori_loop(0, chunks(slab), step, 0)
        return carry

    lax.fori_loop(0, nslab, spread, 0)

    nsum = sums.shape[0]
    for c in beta_copies:
        c.wait()

    low_half = lax.broadcasted_iota(jnp.int32, (GROUP, 128), 1) < BOXPTS
    pair_half = lax.broadcasted_iota(jnp.int32, (rows, 128), 1) < BOXPTS
    span = boxes * BOXPTS

    def leaving(slab):
        slot = lax.rem(slab, 2)
        return pltpu.make_async_copy(
            done.at[slot],
            out_ref.at[:, pl.ds(pl.multiple_of(slab * span, 128), span)],
            out_sem.at[slot],
        )

    def slab_step(slab, carry):
        def step(block, inner):
            products = []
            for u in range(UNROLL):
                g = block * UNROLL + u
                slot_base = pl.multiple_of(slab * slots + g * GROUP, GROUP)
                weights = slot_weights(beta[pl.ds(slot_base, GROUP), :], low_half, 0)
                c = proj[slab * groups + g]
                high = c.astype(jnp.bfloat16)
                low = (c - high.astype(jnp.float32)).astype(jnp.bfloat16)
                left = jnp.concatenate(
                    [
                        jnp.concatenate([high * masks[s], low * masks[s]], axis=1)
                        for s in range(GROUP)
                    ],
                    axis=0,
                )
                products.append((slot_base, jnp.dot(left, weights, preferred_element_type=jnp.float32)))
            for u, (slot_base, product) in enumerate(products):
                for s in range(GROUP):
                    box = slab * boxes + table[slab, 0, block * (UNROLL * GROUP) + u * GROUP + s]
                    j = (u * GROUP + s) % nsum
                    sums[j, box] = sums[j, box] + product[s * rows : (s + 1) * rows]
            return inner

        count = live_groups(table[slab, 1, 0], 0, slots)
        lax.fori_loop(0, lax.div(count + (UNROLL - 1), UNROLL), step, 0)

        @pl.when(slab >= 2)
        def _():
            leaving(slab - 2).wait()

        def finish(pair, inner):
            folded = []
            for i in range(2):
                box = slab * boxes + 2 * pair + i
                value = sums[0, box]
                for j in range(1, nsum):
                    value = value + sums[j, box]
                folded.append(value + pltpu.roll(value, BOXPTS, 1))
            done[lax.rem(slab, 2), :, pl.ds(pl.multiple_of(pair * 128, 128), 128)] = jnp.where(
                pair_half, folded[0], folded[1]
            )
            return inner

        lax.fori_loop(0, span // 128, finish, 0, unroll=8)
        leaving(slab).start()
        return carry

    lax.fori_loop(0, nslab, slab_step, 0)
    for slab in range(max(nslab - 2, 0), nslab):
        leaving(slab).wait()


def apply(arrays, pieces, infos, projections, place, coupling, nslab, slots, rows, ngrid):
    width = projections[0].shape[2]
    lanes = coupling.shape[2]
    depth = arrays[0].shape[1]
    one_sum = ngrid // BOXPTS * rows * 128 * 4
    nsum = 2 if one_sum <= 8 * MIB else 1
    buffers = [
        pltpu.VMEM((nslab * slots // GROUP, rows, width), jnp.float32),
        pltpu.VMEM((nslab, width // GROUP * rows, 2 * lanes), jnp.float32),
        pltpu.VMEM((nslab * slots, depth), jnp.float32),
        pltpu.VMEM((nsum, ngrid // BOXPTS, rows, 128), jnp.float32),
        pltpu.VMEM((2, rows, ngrid // nslab), jnp.float32),
        pltpu.VMEM((GROUP, rows, width), jnp.bfloat16),
        pltpu.VMEM((nslab, INFO, depth), jnp.float32),
        pltpu.VMEM((nslab, INFO, depth), jnp.int32),
    ]
    need = sum(math.prod(b.shape) * b.dtype.itemsize for b in buffers)
    scratch = buffers + [
        pltpu.SMEM((nslab, INFO, depth), jnp.int32),
        pltpu.SemaphoreType.DMA((len(pieces),)),
        pltpu.SemaphoreType.DMA((len(pieces),)),
        pltpu.SemaphoreType.DMA((len(infos),)),
        pltpu.SemaphoreType.DMA((2,)),
    ]
    return pl.pallas_call(
        functools.partial(apply_kernel, nslab, slots, pieces, infos),
        out_shape=jax.ShapeDtypeStruct((rows, ngrid), jnp.float32),
        in_specs=[SMEM, VMEM] + [ANY] * (len(arrays) + len(pieces)),
        out_specs=ANY,
        scratch_shapes=scratch,
        compiler_params=params(min(need + 4 * MIB, 63 * MIB)),
        name="apply",
    )(place, coupling, *arrays, *projections)


Piece = collections.namedtuple("Piece", ["array", "offset", "rows", "info", "index"])


def gather_pieces(projectors, described, nband, nslab):
    slots = projectors.shape[0]
    order, at = cycle_tables(nslab)
    half = slots // 2
    quarter = half // 2
    reach = nslab // 2
    onward = [
        (b * nslab + order[i], b * nslab + order[(i + 1) % nslab])
        for b in range(nband)
        for i in range(nslab)
    ]
    backward = [(d, s) for s, d in onward]
    sibling = [(b * nslab + s, (b ^ 1) * nslab + s) for b in range(nband) for s in range(nslab)]
    core = lax.rem(lax.axis_index("band"), 2)
    mine = lax.dynamic_slice_in_dim(projectors, core * half, half, 0)
    mine = jnp.concatenate([described, mine], axis=0)
    arrays, pieces, calls, infos = [described, projectors], [Piece(1, 0, slots, 0, 0)], [[0]], [(0, 0)]
    places = [lambda core, slab: (slab, 0)]

    def add(array, distance, start, other, info=None):
        arrays.append(array)
        own = len(arrays) - 1
        offset = INFO if info is None else 0
        info = own if info is None else info
        pieces.append(Piece(own, offset, array.shape[0] - offset, info, len(places)))
        places.append(
            lambda core, slab: (
                order[(at[slab] + distance) % nslab],
                (1 - core if other else core) * half + start,
            )
        )
        return len(pieces) - 1

    waiting = []
    up = down = mine
    for step in range(1, reach):
        up = lax.ppermute(up, AXES, onward)
        down = lax.ppermute(down, AXES, backward)
        now = [add(up, -step, 0, False), add(down, step, 0, False)]
        infos += [(pieces[i].array, pieces[i].index) for i in now]
        calls.append(now + waiting)
        waiting = [
            add(lax.ppermute(up, AXES, sibling), -step, 0, True),
            add(lax.ppermute(down, AXES, sibling), step, 0, True),
        ]
    up = lax.ppermute(up[: INFO + quarter], AXES, onward)
    down = lax.ppermute(down[INFO + quarter :], AXES, backward)
    first = add(up, reach, 0, False)
    infos.append((pieces[first].array, pieces[first].index))
    calls.append([first, add(down, reach, quarter, False, pieces[first].array)] + waiting)
    first = add(lax.ppermute(up, AXES, sibling), reach, 0, True)
    second = add(
        lax.ppermute(down, AXES, sibling), reach, quarter, True, pieces[first].array
    )
    calls.append([first, second])
    return arrays, pieces, calls, infos, places


def body(bands, projectors, slot_atom, slot_box, channels, coupling):
    nblock, band_local, ngrid = bands.shape
    nband, nslab = lax.axis_size("band"), lax.axis_size("slab")
    natoms = channels.shape[0]
    atom_dev = natoms // nslab
    channel = coupling.shape[0]
    slots = slot_atom.shape[0]
    lanes = round_up(atom_dev, 128)

    slab = lax.axis_index("slab")
    described = describe(slot_atom, slot_box, slab, nslab, natoms, projectors.shape[1], lanes)
    arrays, pieces, calls, infos, places = gather_pieces(projectors, described, nband, nslab)
    table = np.array(
        [[p(b % 2, s) for p in places] for b in range(nband) for s in range(nslab)], np.int32
    )
    boxes = ngrid // BOXPTS // nslab
    table = np.concatenate([table, table[:, :, :1] * boxes], axis=2)
    me = lax.axis_index("band") * nslab + slab
    place = lax.dynamic_index_in_dim(jnp.asarray(table), me, 0, keepdims=False).reshape(-1)

    mask = (jnp.arange(channel, dtype=jnp.int32)[:, None] < channels[None, :]).astype(jnp.float32)
    masked = coupling * mask[:, None, :] * mask[None, :, :]
    masked = masked.reshape(channel * channel, nslab, atom_dev).transpose(1, 0, 2)
    masked = jnp.pad(masked, ((0, 0), (0, 0), (0, lanes - atom_dev)))

    rows = nblock * band_local
    padded = round_up(rows, GROUP)
    x = bands.reshape(rows, ngrid)
    if padded != rows:
        x = jnp.pad(x, ((0, padded - rows), (0, 0)))
    split = split_bands(x)
    projections = [None] * len(pieces)
    for call in calls:
        for i, value in zip(call, project(arrays, [pieces[i] for i in call], place, split)):
            projections[i] = value
    out = apply(arrays, pieces, infos, projections, place, masked, nslab, slots, padded, ngrid)
    return out[:rows].reshape(nblock, band_local, ngrid)


def solution(mesh):
    in_specs = (P(None, ("band", "slab"), None), P("slab", None), P("slab"), P("slab"), P(), P())
    out_specs = P(None, ("band", "slab"), None)
    return jax.shard_map(body, mesh=mesh, in_specs=in_specs, out_specs=out_specs, check_vma=False)
```

```python
import collections
import functools
import math

import jax
import jax.numpy as jnp
import numpy as np
from jax import lax
from jax.experimental import pallas as pl
from jax.experimental.pallas import tpu as pltpu
from jax.sharding import PartitionSpec as P

BOXPTS = 64
GROUP = 16
INFO = 8
UNROLL = 4
AXES = ("band", "slab")
MIB = 1 << 20


def round_up(value, step):
    return (value + step - 1) // step * step


def cycle_tables(nslab):
    order = list(range(0, nslab, 2)) + list(range(nslab - 1 - nslab % 2, 0, -2))
    place = {s: i for i, s in enumerate(order)}
    return order, place


def params(limit):
    return pltpu.CompilerParams(vmem_limit_bytes=limit)


VMEM = pl.BlockSpec(memory_space=pltpu.VMEM)
SMEM = pl.BlockSpec(memory_space=pltpu.SMEM)
ANY = pl.BlockSpec(memory_space=pl.ANY)


def split_bands_kernel(x_ref, out_ref):
    rows = x_ref.shape[0]
    low_half = lax.broadcasted_iota(jnp.int32, (rows, 128), 1) < BOXPTS
    zero = jnp.zeros((rows, 128), jnp.float32)

    def step(pair, carry):
        x = x_ref[:, pl.ds(pl.multiple_of(pair * 128, 128), 128)]
        high = x.astype(jnp.bfloat16).astype(jnp.float32)
        low = x - high
        high_turned = pltpu.roll(high, BOXPTS, 1)
        low_turned = pltpu.roll(low, BOXPTS, 1)
        out_ref[2 * pair, :, 0:128] = jnp.where(low_half, high, high_turned).astype(jnp.bfloat16)
        out_ref[2 * pair, :, 128:256] = jnp.where(low_half, low, zero).astype(jnp.bfloat16)
        out_ref[2 * pair + 1, :, 0:128] = jnp.where(low_half, high_turned, high).astype(jnp.bfloat16)
        out_ref[2 * pair + 1, :, 128:256] = jnp.where(low_half, low_turned, zero).astype(jnp.bfloat16)
        return carry

    lax.fori_loop(0, x_ref.shape[1] // 128, step, 0, unroll=4)


def split_bands(x):
    rows, ngrid = x.shape
    shape = (ngrid // BOXPTS, rows, 256)
    return pl.pallas_call(
        split_bands_kernel,
        out_shape=jax.ShapeDtypeStruct(shape, jnp.bfloat16),
        in_specs=[VMEM],
        out_specs=VMEM,
        compiler_params=params(40 * MIB),
        cost_estimate=pl.CostEstimate(flops=8 * x.size, bytes_accessed=12 * x.size, transcendentals=0),
        name="split_bands",
    )(x)


def slot_weights(values, low_half, axis):
    full, top = [], []
    for t in range(values.shape[1] // 128):
        x = values[:, t * 128 : (t + 1) * 128]
        high = x.astype(jnp.bfloat16).astype(jnp.float32)
        low = x - high
        turned = pltpu.roll(high, BOXPTS, 1)
        full.append(jnp.where(low_half, high, pltpu.roll(low, BOXPTS, 1)).astype(jnp.bfloat16))
        full.append(jnp.where(low_half, turned, low).astype(jnp.bfloat16))
        top.append(jnp.where(low_half, high, 0.0).astype(jnp.bfloat16))
        top.append(jnp.where(low_half, turned, 0.0).astype(jnp.bfloat16))
    return jnp.concatenate(
        [jnp.concatenate(full, axis=0), jnp.concatenate(top, axis=0)], axis=axis
    )


def live_groups(live, start, length):
    return lax.div(jnp.clip(live - start, 0, length) + (GROUP - 1), GROUP)


def describe(slot_atom, slot_box, slab, nslab, natoms, width, lanes):
    atom_dev = natoms // nslab
    relative = (slot_atom - (slab + nslab - 1) % nslab * atom_dev) % natoms
    column = jnp.where(relative < atom_dev, relative, relative + (lanes - atom_dev))
    column = jnp.where(slot_atom >= 0, column, -1)
    live = jnp.broadcast_to(jnp.sum((slot_atom >= 0).astype(jnp.int32)), slot_atom.shape)
    rows = jnp.stack([slot_box, live, column]).astype(jnp.float32)
    return jnp.pad(rows, ((0, INFO - rows.shape[0]), (0, width - rows.shape[1])))


def project_kernel(pieces, infos, place_ref, x_ref, *refs):
    arrays = refs[: -len(pieces) - 3]
    outs = refs[-len(pieces) - 3 : -3]
    whole, table, sem = refs[-3:]
    copies = []
    for k, index in enumerate(infos):
        whole[k] = arrays[index][0:INFO, :].astype(jnp.int32)
        copies.append(pltpu.make_async_copy(whole.at[k], table.at[k], sem.at[k]))
        copies[-1].start()
    rows = x_ref.shape[1]
    width = outs[0].shape[2]
    low_half = lax.broadcasted_iota(jnp.int32, (GROUP, 128), 1) < BOXPTS
    lane_slot = lax.broadcasted_iota(jnp.int32, (rows, width), 1) % GROUP
    for out in outs:
        out[...] = jnp.zeros(out.shape, jnp.float32)
    for c in copies:
        c.wait()
    for p, out in zip(pieces, outs):
        array = arrays[p.array]
        start = place_ref[3 * p.index + 1]
        box_base = place_ref[3 * p.index + 2]
        info = infos.index(p.info)
        count = live_groups(table[info, 1, 0], start, p.rows)

        def step(block, carry):
            groups = [block * UNROLL + u for u in range(UNROLL)]
            weights, patches = [], []
            for g in groups:
                first = pl.multiple_of(p.offset + g * GROUP, 8)
                weights.append(slot_weights(array[pl.ds(first, GROUP), :], low_half, 1))
                boxes = [table[info, 0, start + g * GROUP + s] for s in range(GROUP)]
                patches.append(jnp.concatenate([x_ref[box_base + b] for b in boxes], axis=0))
            totals = []
            for w, p_ in zip(weights, patches):
                product = lax.dot_general(
                    p_, w, (((1,), (1,)), ((), ())), preferred_element_type=jnp.float32
                )
                total = product[0:rows]
                for s in range(1, GROUP):
                    total = jnp.where(lane_slot == s, product[s * rows : (s + 1) * rows], total)
                totals.append(total)
            for g, total in zip(groups, totals):
                out[g] = total
            return carry

        lax.fori_loop(0, lax.div(count + (UNROLL - 1), UNROLL), step, 0)


def project(arrays, pieces, place, x):
    channel = arrays[0].shape[1] // BOXPTS
    used = sorted({p.array for p in pieces} | {p.info for p in pieces})
    local = [
        p._replace(array=used.index(p.array), info=used.index(p.info)) for p in pieces
    ]
    infos = sorted({p.info for p in local})
    shapes = [
        jax.ShapeDtypeStruct((p.rows // GROUP, x.shape[1], channel * GROUP), jnp.float32)
        for p in pieces
    ]
    size = sum(p.rows for p in pieces) * arrays[0].shape[1]
    table = (len(infos), INFO, arrays[0].shape[1])
    return pl.pallas_call(
        functools.partial(project_kernel, local, infos),
        out_shape=shapes,
        in_specs=[SMEM, VMEM] + [VMEM] * len(used),
        out_specs=[VMEM] * len(pieces),
        scratch_shapes=[
            pltpu.VMEM(table, jnp.int32),
            pltpu.SMEM(table, jnp.int32),
            pltpu.SemaphoreType.DMA((len(infos),)),
        ],
        compiler_params=params(40 * MIB),
        cost_estimate=pl.CostEstimate(
            flops=2 * 16 * 16 * size, bytes_accessed=4 * size + 2 * x.size, transcendentals=0
        ),
        name="project",
    )(place, x, *[arrays[i] for i in used])


def swap_blocks(tiles, lane_block, width):
    tiles = list(tiles)
    bit = 1
    while bit < len(tiles):
        upper = (lane_block & bit) != 0
        for i in range(len(tiles)):
            if not i & bit:
                a, b = tiles[i], tiles[i | bit]
                tiles[i] = jnp.where(upper, pltpu.roll(b, GROUP * bit, 1), a)
                tiles[i | bit] = jnp.where(upper, b, pltpu.roll(a, width - GROUP * bit, 1))
        bit *= 2
    return tiles


def stacked_split(value):
    high = value.astype(jnp.bfloat16)
    low = (value - high.astype(jnp.float32)).astype(jnp.bfloat16)
    return jnp.concatenate([high, low], axis=0)


def apply_kernel(nslab, slots, pieces, infos, place_ref, coupling_ref, *refs):
    npiece = len(pieces)
    proj, parts, beta, sums, done, masks, info, whole, table = refs[-13:-4]
    beta_sem, proj_sem, info_sem, out_sem = refs[-4:]
    out_ref = refs[-14]
    projections = refs[-14 - npiece : -14]
    arrays = refs[: -14 - npiece]
    groups = slots // GROUP
    rows, width = proj.shape[1], proj.shape[2]
    channel = width // GROUP
    lanes = parts.shape[2] // 2
    boxes = out_ref.shape[1] // BOXPTS // nslab
    chunk = width // GROUP
    info_copies, copies, beta_copies = [], [], []
    for i, (array, index) in enumerate(infos):
        slab = place_ref[3 * index]
        info_copies.append(
            pltpu.make_async_copy(arrays[array].at[0:INFO, :], info.at[slab], info_sem.at[i])
        )
    for i, p in enumerate(pieces):
        slab, start = place_ref[3 * p.index], place_ref[3 * p.index + 1]
        first = slab * groups + lax.div(start, GROUP)
        copies.append(
            pltpu.make_async_copy(
                projections[i], proj.at[pl.ds(first, p.rows // GROUP)], proj_sem.at[i]
            )
        )
        first = pl.multiple_of(slab * slots + start, GROUP)
        beta_copies.append(
            pltpu.make_async_copy(
                arrays[p.array].at[p.offset : p.offset + p.rows, :],
                beta.at[pl.ds(first, p.rows), :],
                beta_sem.at[i],
            )
        )
    for c in info_copies + copies + beta_copies:
        c.start()
    lane_slot = lax.broadcasted_iota(jnp.int32, (rows, width), 1) % GROUP
    for s in range(GROUP):
        masks[s] = jnp.where(lane_slot == s, 1.0, 0.0).astype(jnp.bfloat16)
    for c in info_copies:
        c.wait()
    whole[...] = info[...].astype(jnp.int32)
    to_scalars = pltpu.make_async_copy(whole, table, info_sem.at[0])
    to_scalars.start()
    for j in range(sums.shape[0]):
        sums[j] = jnp.zeros(sums.shape[1:], jnp.float32)
    parts[...] = jnp.zeros(parts.shape, jnp.float32)
    to_scalars.wait()
    for c in copies:
        c.wait()

    lane_block = lax.broadcasted_iota(jnp.int32, (rows, width), 1) // GROUP
    atom_row = lax.broadcasted_iota(jnp.int32, (2 * lanes, width), 0).astype(jnp.float32)

    def selector(slab, k):
        first = pl.multiple_of(k * width, 128)
        column = jnp.broadcast_to(info[slab, 2:3, pl.ds(first, width)], (2 * lanes, width))
        return jnp.where(column == atom_row, 1.0, 0.0).astype(jnp.bfloat16)

    def chunks(slab):
        return lax.div(table[slab, 1, 0] + (width - 1), width)

    def sum_by_atom(slab, carry):
        def step(k, inner):
            first = slab * groups + k * chunk
            tiles = [proj[first + i] for i in range(chunk)]
            value = jnp.concatenate(swap_blocks(tiles, lane_block, width), axis=0)
            both = lax.dot_general(
                stacked_split(value),
                selector(slab, k),
                (((1,), (1,)), ((), ())),
                preferred_element_type=jnp.float32,
            )
            half = both.shape[0] // 2
            parts[slab] = parts[slab] + (both[:half] + both[half:])
            return inner

        lax.fori_loop(0, chunks(slab), step, 0)
        return carry

    lax.fori_loop(0, nslab, sum_by_atom, 0)

    def couple(slab, carry):
        following = lax.rem(slab + 1, nslab)
        total = parts[slab, :, lanes:] + parts[following, :, :lanes]
        for c in range(channel):
            mixed = jnp.zeros((rows, lanes), jnp.float32)
            for e in range(channel):
                factor = coupling_ref[slab, pl.ds(c * channel + e, 1), :]
                mixed = mixed + factor * total[e * rows : (e + 1) * rows]
            parts[slab, c * rows : (c + 1) * rows, lanes:] = mixed
        return carry

    lax.fori_loop(0, nslab, couple, 0)

    def spread(slab, carry):
        below = lax.rem(slab + nslab - 1, nslab)
        value = jnp.concatenate([parts[below, :, lanes:], parts[slab, :, lanes:]], axis=1)
        value = stacked_split(value)

        def step(k, inner):
            both = jnp.dot(value, selector(slab, k), preferred_element_type=jnp.float32)
            half = both.shape[0] // 2
            both = both[:half] + both[half:]
            tiles = [both[c * rows : (c + 1) * rows] for c in range(channel)]
            for i, tile in enumerate(swap_blocks(tiles, lane_block, width)):
                proj[slab * groups + k * chunk + i] = tile
            return inner

        lax.fori_loop(0, chunks(slab), step, 0)
        return carry

    lax.fori_loop(0, nslab, spread, 0)

    nsum = sums.shape[0]
    for c in beta_copies:
        c.wait()

    low_half = lax.broadcasted_iota(jnp.int32, (GROUP, 128), 1) < BOXPTS
    pair_half = lax.broadcasted_iota(jnp.int32, (rows, 128), 1) < BOXPTS
    span = boxes * BOXPTS

    def leaving(slab):
        slot = lax.rem(slab, 2)
        return pltpu.make_async_copy(
            done.at[slot],
            out_ref.at[:, pl.ds(pl.multiple_of(slab * span, 128), span)],
            out_sem.at[slot],
        )

    def slab_step(slab, carry):
        def step(block, inner):
            products = []
            for u in range(UNROLL):
                g = block * UNROLL + u
                slot_base = pl.multiple_of(slab * slots + g * GROUP, GROUP)
                weights = slot_weights(beta[pl.ds(slot_base, GROUP), :], low_half, 0)
                c = proj[slab * groups + g]
                high = c.astype(jnp.bfloat16)
                low = (c - high.astype(jnp.float32)).astype(jnp.bfloat16)
                left = jnp.concatenate(
                    [
                        jnp.concatenate([high * masks[s], low * masks[s]], axis=1)
                        for s in range(GROUP)
                    ],
                    axis=0,
                )
                products.append((slot_base, jnp.dot(left, weights, preferred_element_type=jnp.float32)))
            for u, (slot_base, product) in enumerate(products):
                for s in range(GROUP):
                    box = slab * boxes + table[slab, 0, block * (UNROLL * GROUP) + u * GROUP + s]
                    j = (u * GROUP + s) % nsum
                    sums[j, box] = sums[j, box] + product[s * rows : (s + 1) * rows]
            return inner

        count = live_groups(table[slab, 1, 0], 0, slots)
        lax.fori_loop(0, lax.div(count + (UNROLL - 1), UNROLL), step, 0)

        @pl.when(slab >= 2)
        def _():
            leaving(slab - 2).wait()

        def finish(pair, inner):
            folded = []
            for i in range(2):
                box = slab * boxes + 2 * pair + i
                value = sums[0, box]
                for j in range(1, nsum):
                    value = value + sums[j, box]
                folded.append(value + pltpu.roll(value, BOXPTS, 1))
            done[lax.rem(slab, 2), :, pl.ds(pl.multiple_of(pair * 128, 128), 128)] = jnp.where(
                pair_half, folded[0], folded[1]
            )
            return inner

        lax.fori_loop(0, span // 128, finish, 0, unroll=8)
        leaving(slab).start()
        return carry

    lax.fori_loop(0, nslab, slab_step, 0)
    for slab in range(max(nslab - 2, 0), nslab):
        leaving(slab).wait()


def apply(arrays, pieces, infos, projections, place, coupling, nslab, slots, rows, ngrid):
    width = projections[0].shape[2]
    lanes = coupling.shape[2]
    depth = arrays[0].shape[1]
    one_sum = ngrid // BOXPTS * rows * 128 * 4
    nsum = 2 if one_sum <= 8 * MIB else 1
    buffers = [
        pltpu.VMEM((nslab * slots // GROUP, rows, width), jnp.float32),
        pltpu.VMEM((nslab, width // GROUP * rows, 2 * lanes), jnp.float32),
        pltpu.VMEM((nslab * slots, depth), jnp.float32),
        pltpu.VMEM((nsum, ngrid // BOXPTS, rows, 128), jnp.float32),
        pltpu.VMEM((2, rows, ngrid // nslab), jnp.float32),
        pltpu.VMEM((GROUP, rows, width), jnp.bfloat16),
        pltpu.VMEM((nslab, INFO, depth), jnp.float32),
        pltpu.VMEM((nslab, INFO, depth), jnp.int32),
    ]
    need = sum(math.prod(b.shape) * b.dtype.itemsize for b in buffers)
    scratch = buffers + [
        pltpu.SMEM((nslab, INFO, depth), jnp.int32),
        pltpu.SemaphoreType.DMA((len(pieces),)),
        pltpu.SemaphoreType.DMA((len(pieces),)),
        pltpu.SemaphoreType.DMA((len(infos),)),
        pltpu.SemaphoreType.DMA((2,)),
    ]
    return pl.pallas_call(
        functools.partial(apply_kernel, nslab, slots, pieces, infos),
        out_shape=jax.ShapeDtypeStruct((rows, ngrid), jnp.float32),
        in_specs=[SMEM, VMEM] + [ANY] * (len(arrays) + len(pieces)),
        out_specs=ANY,
        scratch_shapes=scratch,
        compiler_params=params(min(need + 4 * MIB, 63 * MIB)),
        name="apply",
    )(place, coupling, *arrays, *projections)


Piece = collections.namedtuple("Piece", ["array", "offset", "rows", "info", "index"])


def gather_and_project(projectors, described, split, extra, nband, nslab):
    slots = projectors.shape[0]
    order, at = cycle_tables(nslab)
    half = slots // 2
    quarter = half // 2
    reach = nslab // 2
    onward = [
        (b * nslab + order[i], b * nslab + order[(i + 1) % nslab])
        for b in range(nband)
        for i in range(nslab)
    ]
    backward = [(d, s) for s, d in onward]
    sibling = [(b * nslab + s, (b ^ 1) * nslab + s) for b in range(nband) for s in range(nslab)]
    core = lax.rem(lax.axis_index("band"), 2)
    mine = lax.dynamic_slice_in_dim(projectors, core * half, half, 0)
    mine = jnp.concatenate([described, mine], axis=0)

    where = [(0, 0, None)]
    for step in range(1, reach):
        where += [(1 - step, 0, True), (step - 1, 0, True)] if step > 1 else []
        where += [(-step, 0, False), (step, 0, False)]
    where += [(1 - reach, 0, True), (reach - 1, 0, True)]
    where += [(reach, 0, False), (reach, quarter, False), (reach, 0, True), (reach, quarter, True)]
    boxes = split.shape[0] // nslab

    def entry(core, slab, distance, start, other):
        there = order[(at[slab] + distance) % nslab]
        if other is not None:
            start += half * ((1 - core) if other else core)
        return there, start, there * boxes

    table = [[entry(b % 2, s, *w) for w in where] for b in range(nband) for s in range(nslab)]
    me = lax.axis_index("band") * nslab + lax.axis_index("slab")
    place = lax.dynamic_index_in_dim(
        jnp.asarray(np.array(table, np.int32)), me, 0, keepdims=False
    ).reshape(-1)

    arrays, pieces, infos, projections = [described, projectors], [], [(0, 0)], []

    def add(array, info=None):
        arrays.append(array)
        own = len(arrays) - 1
        offset = INFO if info is None else 0
        pieces.append(
            Piece(own, offset, array.shape[0] - offset, own if info is None else info, len(pieces))
        )
        return own

    pieces.append(Piece(1, 0, slots, 0, 0))
    up = lax.ppermute(mine, AXES, onward)
    down = lax.ppermute(mine, AXES, backward)
    done = 0

    def project_new():
        nonlocal done
        projections.extend(project(arrays, pieces[done:], place, split))
        done = len(pieces)

    project_new()
    up, down, projections, place, extra = lax.optimization_barrier(
        (up, down, projections, place, extra)
    )
    projections = list(projections)
    near = []
    for step in range(1, reach + 1):
        last = step == reach
        for array in near:
            add(array)
        for array in (up,) if last else (up, down):
            infos.append((add(array), len(pieces) - 1))
        if last:
            add(down, len(arrays) - 1)
        near = [lax.ppermute(up, AXES, sibling), lax.ppermute(down, AXES, sibling)]
        if step + 1 < reach:
            up = lax.ppermute(up, AXES, onward)
            down = lax.ppermute(down, AXES, backward)
        elif not last:
            up = lax.ppermute(up[: INFO + quarter], AXES, onward)
            down = lax.ppermute(down[INFO + quarter :], AXES, backward)
        project_new()
        up, down, near, projections = lax.optimization_barrier((up, down, near, projections))
        near, projections = list(near), list(projections)
    add(near[0])
    add(near[1], len(arrays) - 1)
    project_new()
    return arrays, pieces, infos, projections, place, extra


def body(bands, projectors, slot_atom, slot_box, channels, coupling):
    nblock, band_local, ngrid = bands.shape
    nband, nslab = lax.axis_size("band"), lax.axis_size("slab")
    natoms = channels.shape[0]
    atom_dev = natoms // nslab
    channel = coupling.shape[0]
    slots = slot_atom.shape[0]
    lanes = round_up(atom_dev, 128)

    slab = lax.axis_index("slab")
    described = describe(slot_atom, slot_box, slab, nslab, natoms, projectors.shape[1], lanes)
    mask = (jnp.arange(channel, dtype=jnp.int32)[:, None] < channels[None, :]).astype(jnp.float32)
    masked = coupling * mask[:, None, :] * mask[None, :, :]
    masked = masked.reshape(channel * channel, nslab, atom_dev).transpose(1, 0, 2)
    masked = jnp.pad(masked, ((0, 0), (0, 0), (0, lanes - atom_dev)))

    rows = nblock * band_local
    padded = round_up(rows, GROUP)
    x = bands.reshape(rows, ngrid)
    if padded != rows:
        x = jnp.pad(x, ((0, padded - rows), (0, 0)))
    split = split_bands(x)
    arrays, pieces, infos, projections, place, masked = gather_and_project(
        projectors, described, split, masked, nband, nslab
    )
    out = apply(arrays, pieces, infos, projections, place, masked, nslab, slots, padded, ngrid)
    return out[:rows].reshape(nblock, band_local, ngrid)


def solution(mesh):
    in_specs = (P(None, ("band", "slab"), None), P("slab", None), P("slab"), P("slab"), P(), P())
    out_specs = P(None, ("band", "slab"), None)
    return jax.shard_map(body, mesh=mesh, in_specs=in_specs, out_specs=out_specs, check_vma=False)
```

```python
import collections
import functools
import math

import jax
import jax.numpy as jnp
import numpy as np
from jax import lax
from jax.experimental import pallas as pl
from jax.experimental.pallas import tpu as pltpu
from jax.sharding import PartitionSpec as P

BOXPTS = 64
GROUP = 16
INFO = 8
UNROLL = 4
AXES = ("band", "slab")
MIB = 1 << 20


def round_up(value, step):
    return (value + step - 1) // step * step


def cycle_tables(nslab):
    order = list(range(0, nslab, 2)) + list(range(nslab - 1 - nslab % 2, 0, -2))
    place = {s: i for i, s in enumerate(order)}
    return order, place


def params(limit):
    return pltpu.CompilerParams(vmem_limit_bytes=limit)


VMEM = pl.BlockSpec(memory_space=pltpu.VMEM)
SMEM = pl.BlockSpec(memory_space=pltpu.SMEM)
ANY = pl.BlockSpec(memory_space=pl.ANY)


def split_bands_kernel(x_ref, out_ref):
    rows = x_ref.shape[0]
    low_half = lax.broadcasted_iota(jnp.int32, (rows, 128), 1) < BOXPTS
    zero = jnp.zeros((rows, 128), jnp.float32)

    def step(pair, carry):
        x = x_ref[:, pl.ds(pl.multiple_of(pair * 128, 128), 128)]
        high = x.astype(jnp.bfloat16).astype(jnp.float32)
        low = x - high
        high_turned = pltpu.roll(high, BOXPTS, 1)
        low_turned = pltpu.roll(low, BOXPTS, 1)
        out_ref[2 * pair, :, 0:128] = jnp.where(low_half, high, high_turned).astype(jnp.bfloat16)
        out_ref[2 * pair, :, 128:256] = jnp.where(low_half, low, zero).astype(jnp.bfloat16)
        out_ref[2 * pair + 1, :, 0:128] = jnp.where(low_half, high_turned, high).astype(jnp.bfloat16)
        out_ref[2 * pair + 1, :, 128:256] = jnp.where(low_half, low_turned, zero).astype(jnp.bfloat16)
        return carry

    lax.fori_loop(0, x_ref.shape[1] // 128, step, 0, unroll=4)


def split_bands(x):
    rows, ngrid = x.shape
    shape = (ngrid // BOXPTS, rows, 256)
    return pl.pallas_call(
        split_bands_kernel,
        out_shape=jax.ShapeDtypeStruct(shape, jnp.bfloat16),
        in_specs=[VMEM],
        out_specs=VMEM,
        compiler_params=params(40 * MIB),
        cost_estimate=pl.CostEstimate(flops=8 * x.size, bytes_accessed=12 * x.size, transcendentals=0),
        name="split_bands",
    )(x)


def slot_weights(values, low_half, axis):
    full, top = [], []
    for t in range(values.shape[1] // 128):
        x = values[:, t * 128 : (t + 1) * 128]
        high = x.astype(jnp.bfloat16).astype(jnp.float32)
        low = x - high
        turned = pltpu.roll(high, BOXPTS, 1)
        full.append(jnp.where(low_half, high, pltpu.roll(low, BOXPTS, 1)).astype(jnp.bfloat16))
        full.append(jnp.where(low_half, turned, low).astype(jnp.bfloat16))
        top.append(jnp.where(low_half, high, 0.0).astype(jnp.bfloat16))
        top.append(jnp.where(low_half, turned, 0.0).astype(jnp.bfloat16))
    return jnp.concatenate(
        [jnp.concatenate(full, axis=0), jnp.concatenate(top, axis=0)], axis=axis
    )


def live_groups(live, start, length):
    return lax.div(jnp.clip(live - start, 0, length) + (GROUP - 1), GROUP)


def begin_kernel(natoms, lanes, atom_ref, box_ref, projector_ref, info_ref, mine_ref, info_sem, half_sem):
    nslab = lax.axis_size("slab")
    half = mine_ref.shape[0] - INFO
    core = lax.rem(lax.axis_index("band"), 2)
    copy = pltpu.make_async_copy(
        projector_ref.at[pl.ds(pl.multiple_of(core * half, GROUP), half), :],
        mine_ref.at[pl.ds(INFO, half), :],
        half_sem,
    )
    copy.start()
    atom_dev = natoms // nslab
    below = lax.rem(lax.axis_index("slab") + nslab - 1, nslab) * atom_dev
    atom = atom_ref[...]
    slots = atom.shape[1]
    relative = atom - below
    relative = jnp.where(relative < 0, relative + natoms, relative)
    column = jnp.where(relative < atom_dev, relative, relative + (lanes - atom_dev))
    live = jnp.sum(jnp.where(atom >= 0, 1.0, 0.0), axis=1, keepdims=True)
    info_ref[...] = jnp.zeros(info_ref.shape, jnp.float32)
    info_ref[0:1, 0:slots] = box_ref[...].astype(jnp.float32)
    info_ref[1:2, 0:slots] = jnp.broadcast_to(live, (1, slots))
    info_ref[2:3, 0:slots] = jnp.where(atom >= 0, column, -1).astype(jnp.float32)
    head = pltpu.make_async_copy(info_ref, mine_ref.at[pl.ds(0, INFO), :], info_sem)
    head.start()
    head.wait()
    copy.wait()


def begin(slot_atom, slot_box, projectors, natoms, lanes):
    slots, depth = projectors.shape
    return pl.pallas_call(
        functools.partial(begin_kernel, natoms, lanes),
        out_shape=[
            jax.ShapeDtypeStruct((INFO, depth), jnp.float32),
            jax.ShapeDtypeStruct((INFO + slots // 2, depth), jnp.float32),
        ],
        in_specs=[VMEM, VMEM, ANY],
        out_specs=[VMEM, ANY],
        scratch_shapes=[pltpu.SemaphoreType.DMA(()), pltpu.SemaphoreType.DMA(())],
        compiler_params=params(8 * MIB),
        name="begin",
    )(slot_atom.reshape(1, slots), slot_box.reshape(1, slots), projectors)


def project_kernel(pieces, infos, place_ref, x_ref, *refs):
    arrays = refs[: -len(pieces) - 4]
    outs = refs[-len(pieces) - 4 : -4]
    whole, proj, table, sem = refs[-4:]
    copies = []
    for k, index in enumerate(infos):
        whole[k] = arrays[index][0:INFO, :].astype(jnp.int32)
        copies.append(pltpu.make_async_copy(whole.at[k], table.at[k], sem.at[k]))
        copies[-1].start()
    rows = x_ref.shape[1]
    width = proj.shape[2]
    chunk = width // GROUP
    lane_block = lax.broadcasted_iota(jnp.int32, (rows, width), 1) // GROUP
    low_half = lax.broadcasted_iota(jnp.int32, (GROUP, 128), 1) < BOXPTS
    lane_slot = lax.broadcasted_iota(jnp.int32, (rows, width), 1) % GROUP
    for c in copies:
        c.wait()
    for p, out in zip(pieces, outs):
        array = arrays[p.array]
        start = place_ref[3 * p.index + 1]
        box_base = place_ref[3 * p.index + 2]
        info = infos.index(p.info)
        count = live_groups(table[info, 1, 0], start, p.rows)

        def step(block, carry):
            groups = [block * UNROLL + u for u in range(UNROLL)]
            weights, patches = [], []
            for g in groups:
                first = pl.multiple_of(p.offset + g * GROUP, 8)
                weights.append(slot_weights(array[pl.ds(first, GROUP), :], low_half, 1))
                boxes = [table[info, 0, start + g * GROUP + s] for s in range(GROUP)]
                patches.append(jnp.concatenate([x_ref[box_base + b] for b in boxes], axis=0))
            totals = []
            for w, p_ in zip(weights, patches):
                product = lax.dot_general(
                    p_, w, (((1,), (1,)), ((), ())), preferred_element_type=jnp.float32
                )
                total = product[0:rows]
                for s in range(1, GROUP):
                    total = jnp.where(lane_slot == s, product[s * rows : (s + 1) * rows], total)
                totals.append(total)
            for g, total in zip(groups, totals):
                proj[g] = total
            return carry

        proj[...] = jnp.zeros(proj.shape, jnp.float32)
        lax.fori_loop(0, lax.div(count + (UNROLL - 1), UNROLL), step, 0)

        @pl.when(count == 0)
        def _():
            out[...] = jnp.zeros(out.shape, jnp.float32)

        @pl.when(count > 0)
        def _():
            columns = arrays[p.info][2:3, :]
            columns = pltpu.roll(columns, lax.rem(columns.shape[1] - start, columns.shape[1]), 1)
            nchunk = (p.rows // GROUP + chunk - 1) // chunk
            value = jnp.concatenate(
                [
                    jnp.concatenate(
                        swap_blocks([proj[k * chunk + i] for i in range(chunk)], lane_block, width),
                        axis=0,
                    )
                    for k in range(nchunk)
                ],
                axis=1,
            )
            both = lax.dot_general(
                stacked_split(value),
                selector(columns[:, : nchunk * width], out.shape[1]),
                (((1,), (1,)), ((), ())),
                preferred_element_type=jnp.float32,
            )
            half = both.shape[0] // 2
            out[...] = both[:half] + both[half:]


def project(arrays, pieces, place, x, lanes):
    channel = arrays[0].shape[1] // BOXPTS
    used = sorted({p.array for p in pieces} | {p.info for p in pieces})
    local = [
        p._replace(array=used.index(p.array), info=used.index(p.info)) for p in pieces
    ]
    infos = sorted({p.info for p in local})
    shapes = [
        jax.ShapeDtypeStruct((channel * x.shape[1], 2 * lanes), jnp.float32) for p in pieces
    ]
    size = sum(p.rows for p in pieces) * arrays[0].shape[1]
    table = (len(infos), INFO, arrays[0].shape[1])
    groups = round_up(max(p.rows for p in pieces), channel * GROUP) // GROUP
    return pl.pallas_call(
        functools.partial(project_kernel, local, infos),
        out_shape=shapes,
        in_specs=[SMEM, VMEM] + [VMEM] * len(used),
        out_specs=[VMEM] * len(pieces),
        scratch_shapes=[
            pltpu.VMEM(table, jnp.int32),
            pltpu.VMEM((groups, x.shape[1], channel * GROUP), jnp.float32),
            pltpu.SMEM(table, jnp.int32),
            pltpu.SemaphoreType.DMA((len(infos),)),
        ],
        compiler_params=params(40 * MIB),
        cost_estimate=pl.CostEstimate(
            flops=2 * 16 * 16 * size, bytes_accessed=4 * size + 2 * x.size, transcendentals=0
        ),
        name="project",
    )(place, x, *[arrays[i] for i in used])


def swap_blocks(tiles, lane_block, width):
    tiles = list(tiles)
    bit = 1
    while bit < len(tiles):
        upper = (lane_block & bit) != 0
        for i in range(len(tiles)):
            if not i & bit:
                a, b = tiles[i], tiles[i | bit]
                tiles[i] = jnp.where(upper, pltpu.roll(b, GROUP * bit, 1), a)
                tiles[i | bit] = jnp.where(upper, b, pltpu.roll(a, width - GROUP * bit, 1))
        bit *= 2
    return tiles


def selector(columns, count):
    shape = (count, columns.shape[1])
    row = lax.broadcasted_iota(jnp.int32, shape, 0).astype(jnp.float32)
    return jnp.where(jnp.broadcast_to(columns, shape) == row, 1.0, 0.0).astype(jnp.bfloat16)


def stacked_split(value):
    high = value.astype(jnp.bfloat16)
    low = (value - high.astype(jnp.float32)).astype(jnp.bfloat16)
    return jnp.concatenate([high, low], axis=0)


def apply_kernel(nslab, slots, pieces, infos, place_ref, coupling_ref, *refs):
    npiece = len(pieces)
    proj, loaded, parts, beta, sums, done, masks, info, whole, table = refs[-14:-4]
    beta_sem, proj_sem, info_sem, out_sem = refs[-4:]
    out_ref = refs[-15]
    projections = refs[-15 - npiece : -15]
    arrays = refs[: -15 - npiece]
    groups = slots // GROUP
    rows, width = proj.shape[1], proj.shape[2]
    channel = width // GROUP
    lanes = parts.shape[2] // 2
    boxes = out_ref.shape[1] // BOXPTS // nslab
    chunk = width // GROUP
    info_copies, copies, beta_copies = [], [], []
    for i, (array, index) in enumerate(infos):
        slab = place_ref[3 * index]
        info_copies.append(
            pltpu.make_async_copy(arrays[array].at[0:INFO, :], info.at[slab], info_sem.at[i])
        )
    for i, p in enumerate(pieces):
        slab, start = place_ref[3 * p.index], place_ref[3 * p.index + 1]
        j = i % loaded.shape[0]
        copies.append(
            pltpu.make_async_copy(projections[i], loaded.at[j], proj_sem.at[i])
        )
        first = pl.multiple_of(slab * slots + start, GROUP)
        beta_copies.append(
            pltpu.make_async_copy(
                arrays[p.array].at[p.offset : p.offset + p.rows, :],
                beta.at[pl.ds(first, p.rows), :],
                beta_sem.at[i],
            )
        )
    for c in info_copies + copies[: loaded.shape[0]] + beta_copies:
        c.start()
    lane_slot = lax.broadcasted_iota(jnp.int32, (rows, width), 1) % GROUP
    for s in range(GROUP):
        masks[s] = jnp.where(lane_slot == s, 1.0, 0.0).astype(jnp.bfloat16)
    for j in range(sums.shape[0]):
        sums[j] = jnp.zeros(sums.shape[1:], jnp.float32)
    parts[...] = jnp.zeros(parts.shape, jnp.float32)
    for c in info_copies:
        c.wait()
    whole[...] = info[...].astype(jnp.int32)
    to_scalars = pltpu.make_async_copy(whole, table, info_sem.at[0])
    to_scalars.start()
    for first in range(0, npiece, loaded.shape[0]):
        wave = range(first, min(first + loaded.shape[0], npiece))
        for i in wave:
            if first > 0:
                copies[i].start()
        for i in wave:
            copies[i].wait()
        for i in wave:
            slab = place_ref[3 * pieces[i].index]
            parts[slab] = parts[slab] + loaded[i % loaded.shape[0]]

    lane_block = lax.broadcasted_iota(jnp.int32, (rows, width), 1) // GROUP
    def couple(slab, carry):
        following = lax.rem(slab + 1, nslab)
        total = parts[slab, :, lanes:] + parts[following, :, :lanes]
        for c in range(channel):
            mixed = jnp.zeros((rows, lanes), jnp.float32)
            for e in range(channel):
                factor = coupling_ref[slab, pl.ds(c * channel + e, 1), :]
                mixed = mixed + factor * total[e * rows : (e + 1) * rows]
            parts[slab, c * rows : (c + 1) * rows, lanes:] = mixed
        return carry

    lax.fori_loop(0, nslab, couple, 0)

    wide = min(2 * width, slots)

    def spread(slab, carry):
        below = lax.rem(slab + nslab - 1, nslab)
        value = jnp.concatenate([parts[below, :, lanes:], parts[slab, :, lanes:]], axis=1)
        value = stacked_split(value)

        def step(k, inner):
            columns = info[slab, 2:3, pl.ds(pl.multiple_of(k * wide, 128), wide)]
            both = jnp.dot(value, selector(columns, 2 * lanes), preferred_element_type=jnp.float32)
            half = both.shape[0] // 2
            both = both[:half] + both[half:]
            for q in range(wide // width):
                tiles = [
                    both[c * rows : (c + 1) * rows, q * width : (q + 1) * width]
                    for c in range(channel)
                ]
                for i, tile in enumerate(swap_blocks(tiles, lane_block, width)):
                    proj[slab * groups + k * (wide // GROUP) + q * chunk + i] = tile
            return inner

        lax.fori_loop(0, lax.div(table[slab, 1, 0] + (wide - 1), wide), step, 0)
        return carry

    to_scalars.wait()
    lax.fori_loop(0, nslab, spread, 0)

    nsum = sums.shape[0]
    for c in beta_copies:
        c.wait()

    low_half = lax.broadcasted_iota(jnp.int32, (GROUP, 128), 1) < BOXPTS
    pair_half = lax.broadcasted_iota(jnp.int32, (rows, 128), 1) < BOXPTS
    span = boxes * BOXPTS

    def leaving(slab):
        slot = lax.rem(slab, 2)
        return pltpu.make_async_copy(
            done.at[slot],
            out_ref.at[:, pl.ds(pl.multiple_of(slab * span, 128), span)],
            out_sem.at[slot],
        )

    def slab_step(slab, carry):
        def step(block, inner):
            products = []
            for u in range(UNROLL):
                g = block * UNROLL + u
                slot_base = pl.multiple_of(slab * slots + g * GROUP, GROUP)
                weights = slot_weights(beta[pl.ds(slot_base, GROUP), :], low_half, 0)
                c = proj[slab * groups + g]
                high = c.astype(jnp.bfloat16)
                low = (c - high.astype(jnp.float32)).astype(jnp.bfloat16)
                left = jnp.concatenate(
                    [
                        jnp.concatenate([high * masks[s], low * masks[s]], axis=1)
                        for s in range(GROUP)
                    ],
                    axis=0,
                )
                products.append((slot_base, jnp.dot(left, weights, preferred_element_type=jnp.float32)))
            for u, (slot_base, product) in enumerate(products):
                for s in range(GROUP):
                    box = slab * boxes + table[slab, 0, block * (UNROLL * GROUP) + u * GROUP + s]
                    j = (u * GROUP + s) % nsum
                    sums[j, box] = sums[j, box] + product[s * rows : (s + 1) * rows]
            return inner

        count = live_groups(table[slab, 1, 0], 0, slots)
        lax.fori_loop(0, lax.div(count + (UNROLL - 1), UNROLL), step, 0)

        @pl.when(slab >= 2)
        def _():
            leaving(slab - 2).wait()

        def finish(pair, inner):
            folded = []
            for i in range(2):
                box = slab * boxes + 2 * pair + i
                value = sums[0, box]
                for j in range(1, nsum):
                    value = value + sums[j, box]
                folded.append(value + pltpu.roll(value, BOXPTS, 1))
            done[lax.rem(slab, 2), :, pl.ds(pl.multiple_of(pair * 128, 128), 128)] = jnp.where(
                pair_half, folded[0], folded[1]
            )
            return inner

        lax.fori_loop(0, span // 128, finish, 0, unroll=8)
        leaving(slab).start()
        return carry

    lax.fori_loop(0, nslab, slab_step, 0)
    for slab in range(max(nslab - 2, 0), nslab):
        leaving(slab).wait()


def apply(arrays, pieces, infos, projections, place, coupling, nslab, slots, rows, ngrid):
    width = projections[0].shape[0] // rows * GROUP
    lanes = coupling.shape[2]
    depth = arrays[0].shape[1]
    one_sum = ngrid // BOXPTS * rows * 128 * 4
    nsum = 2 if one_sum <= 8 * MIB else 1
    buffers = [
        pltpu.VMEM((nslab * slots // GROUP, rows, width), jnp.float32),
        pltpu.VMEM((len(pieces) if len(pieces) <= 24 else 1,) + projections[0].shape, jnp.float32),
        pltpu.VMEM((nslab,) + projections[0].shape, jnp.float32),
        pltpu.VMEM((nslab * slots, depth), jnp.float32),
        pltpu.VMEM((nsum, ngrid // BOXPTS, rows, 128), jnp.float32),
        pltpu.VMEM((2, rows, ngrid // nslab), jnp.float32),
        pltpu.VMEM((GROUP, rows, width), jnp.bfloat16),
        pltpu.VMEM((nslab, INFO, depth), jnp.float32),
        pltpu.VMEM((nslab, INFO, depth), jnp.int32),
    ]
    need = sum(math.prod(b.shape) * b.dtype.itemsize for b in buffers)
    scratch = buffers + [
        pltpu.SMEM((nslab, INFO, depth), jnp.int32),
        pltpu.SemaphoreType.DMA((len(pieces),)),
        pltpu.SemaphoreType.DMA((len(pieces),)),
        pltpu.SemaphoreType.DMA((len(infos),)),
        pltpu.SemaphoreType.DMA((2,)),
    ]
    return pl.pallas_call(
        functools.partial(apply_kernel, nslab, slots, pieces, infos),
        out_shape=jax.ShapeDtypeStruct((rows, ngrid), jnp.float32),
        in_specs=[SMEM, VMEM] + [ANY] * (len(arrays) + len(pieces)),
        out_specs=ANY,
        scratch_shapes=scratch,
        compiler_params=params(min(need + 4 * MIB, 63 * MIB)),
        name="apply",
    )(place, coupling, *arrays, *projections)


Piece = collections.namedtuple("Piece", ["array", "offset", "rows", "info", "index"])


def gather_and_project(projectors, described, mine, split, extra, lanes, nband, nslab):
    slots = projectors.shape[0]
    order, at = cycle_tables(nslab)
    half = slots // 2
    quarter = half // 2
    reach = nslab // 2
    onward = [
        (b * nslab + order[i], b * nslab + order[(i + 1) % nslab])
        for b in range(nband)
        for i in range(nslab)
    ]
    backward = [(d, s) for s, d in onward]
    sibling = [(b * nslab + s, (b ^ 1) * nslab + s) for b in range(nband) for s in range(nslab)]

    where = [(0, 0, None)]
    for step in range(1, reach):
        where += [(1 - step, 0, True), (step - 1, 0, True)] if step > 1 else []
        where += [(-step, 0, False), (step, 0, False)]
    where += [(1 - reach, 0, True), (reach - 1, 0, True)]
    where += [(reach, 0, False), (reach, quarter, False), (reach, 0, True), (reach, quarter, True)]
    boxes = split.shape[0] // nslab

    def entry(core, slab, distance, start, other):
        there = order[(at[slab] + distance) % nslab]
        if other is not None:
            start += half * ((1 - core) if other else core)
        return there, start, there * boxes

    table = [[entry(b % 2, s, *w) for w in where] for b in range(nband) for s in range(nslab)]
    me = lax.axis_index("band") * nslab + lax.axis_index("slab")
    place = lax.dynamic_index_in_dim(
        jnp.asarray(np.array(table, np.int32)), me, 0, keepdims=False
    ).reshape(-1)

    arrays, pieces, infos, projections = [described, projectors], [], [(0, 0)], []

    def add(array, info=None):
        arrays.append(array)
        own = len(arrays) - 1
        offset = INFO if info is None else 0
        pieces.append(
            Piece(own, offset, array.shape[0] - offset, own if info is None else info, len(pieces))
        )
        return own

    pieces.append(Piece(1, 0, slots, 0, 0))
    up = lax.ppermute(mine, AXES, onward)
    down = lax.ppermute(mine, AXES, backward)
    done = 0

    def project_new():
        nonlocal done
        projections.extend(project(arrays, pieces[done:], place, split, lanes))
        done = len(pieces)

    project_new()
    up, down, projections, place, extra = lax.optimization_barrier(
        (up, down, projections, place, extra)
    )
    projections = list(projections)
    near = []
    for step in range(1, reach + 1):
        last = step == reach
        for array in near:
            add(array)
        for array in (up,) if last else (up, down):
            infos.append((add(array), len(pieces) - 1))
        if last:
            add(down, len(arrays) - 1)
        near = [lax.ppermute(up, AXES, sibling), lax.ppermute(down, AXES, sibling)]
        if step + 1 < reach:
            up = lax.ppermute(up, AXES, onward)
            down = lax.ppermute(down, AXES, backward)
        elif not last:
            up = lax.ppermute(up[: INFO + quarter], AXES, onward)
            down = lax.ppermute(down[INFO + quarter :], AXES, backward)
        project_new()
        up, down, near, projections = lax.optimization_barrier((up, down, near, projections))
        near, projections = list(near), list(projections)
    add(near[0])
    add(near[1], len(arrays) - 1)
    project_new()
    return arrays, pieces, infos, projections, place, extra


def body(bands, projectors, slot_atom, slot_box, channels, coupling):
    nblock, band_local, ngrid = bands.shape
    nband, nslab = lax.axis_size("band"), lax.axis_size("slab")
    natoms = channels.shape[0]
    atom_dev = natoms // nslab
    channel = coupling.shape[0]
    slots = slot_atom.shape[0]
    lanes = round_up(atom_dev, 128)

    described, mine = begin(slot_atom, slot_box, projectors, natoms, lanes)
    mask = (jnp.arange(channel, dtype=jnp.int32)[:, None] < channels[None, :]).astype(jnp.float32)
    masked = coupling * mask[:, None, :] * mask[None, :, :]
    masked = masked.reshape(channel * channel, nslab, atom_dev).transpose(1, 0, 2)
    masked = jnp.pad(masked, ((0, 0), (0, 0), (0, lanes - atom_dev)))

    rows = nblock * band_local
    padded = round_up(rows, GROUP)
    x = bands.reshape(rows, ngrid)
    if padded != rows:
        x = jnp.pad(x, ((0, padded - rows), (0, 0)))
    split = split_bands(x)
    arrays, pieces, infos, projections, place, masked = gather_and_project(
        projectors, described, mine, split, masked, lanes, nband, nslab
    )
    out = apply(arrays, pieces, infos, projections, place, masked, nslab, slots, padded, ngrid)
    return out[:rows].reshape(nblock, band_local, ngrid)


def solution(mesh):
    in_specs = (P(None, ("band", "slab"), None), P("slab", None), P("slab"), P("slab"), P(), P())
    out_specs = P(None, ("band", "slab"), None)
    return jax.shard_map(body, mesh=mesh, in_specs=in_specs, out_specs=out_specs, check_vma=False)
```

```python
import collections
import functools
import math

import jax
import jax.numpy as jnp
import numpy as np
from jax import lax
from jax.experimental import pallas as pl
from jax.experimental.pallas import tpu as pltpu
from jax.sharding import PartitionSpec as P

BOXPTS = 64
GROUP = 16
INFO = 8
UNROLL = 4
AXES = ("band", "slab")
MIB = 1 << 20


def round_up(value, step):
    return (value + step - 1) // step * step


def cycle_tables(nslab):
    order = list(range(0, nslab, 2)) + list(range(nslab - 1 - nslab % 2, 0, -2))
    place = {s: i for i, s in enumerate(order)}
    return order, place


def params(limit):
    return pltpu.CompilerParams(vmem_limit_bytes=limit)


VMEM = pl.BlockSpec(memory_space=pltpu.VMEM)
SMEM = pl.BlockSpec(memory_space=pltpu.SMEM)
ANY = pl.BlockSpec(memory_space=pl.ANY)


def split_bands_kernel(x_ref, out_ref):
    rows = x_ref.shape[0]
    low_half = lax.broadcasted_iota(jnp.int32, (rows, 128), 1) < BOXPTS
    zero = jnp.zeros((rows, 128), jnp.float32)

    def step(pair, carry):
        x = x_ref[:, pl.ds(pl.multiple_of(pair * 128, 128), 128)]
        high = x.astype(jnp.bfloat16).astype(jnp.float32)
        low = x - high
        high_turned = pltpu.roll(high, BOXPTS, 1)
        low_turned = pltpu.roll(low, BOXPTS, 1)
        out_ref[2 * pair, :, 0:128] = jnp.where(low_half, high, high_turned).astype(jnp.bfloat16)
        out_ref[2 * pair, :, 128:256] = jnp.where(low_half, low, zero).astype(jnp.bfloat16)
        out_ref[2 * pair + 1, :, 0:128] = jnp.where(low_half, high_turned, high).astype(jnp.bfloat16)
        out_ref[2 * pair + 1, :, 128:256] = jnp.where(low_half, low_turned, zero).astype(jnp.bfloat16)
        return carry

    lax.fori_loop(0, x_ref.shape[1] // 128, step, 0, unroll=4)


def split_bands(x):
    rows, ngrid = x.shape
    shape = (ngrid // BOXPTS, rows, 256)
    return pl.pallas_call(
        split_bands_kernel,
        out_shape=jax.ShapeDtypeStruct(shape, jnp.bfloat16),
        in_specs=[VMEM],
        out_specs=VMEM,
        compiler_params=params(40 * MIB),
        cost_estimate=pl.CostEstimate(flops=8 * x.size, bytes_accessed=12 * x.size, transcendentals=0),
        name="split_bands",
    )(x)


def slot_weights(values, low_half, axis):
    full, top = [], []
    for t in range(values.shape[1] // 128):
        x = values[:, t * 128 : (t + 1) * 128]
        high = x.astype(jnp.bfloat16).astype(jnp.float32)
        low = x - high
        turned = pltpu.roll(high, BOXPTS, 1)
        full.append(jnp.where(low_half, high, pltpu.roll(low, BOXPTS, 1)).astype(jnp.bfloat16))
        full.append(jnp.where(low_half, turned, low).astype(jnp.bfloat16))
        top.append(jnp.where(low_half, high, 0.0).astype(jnp.bfloat16))
        top.append(jnp.where(low_half, turned, 0.0).astype(jnp.bfloat16))
    return jnp.concatenate(
        [jnp.concatenate(full, axis=0), jnp.concatenate(top, axis=0)], axis=axis
    )


def live_groups(live, start, length):
    return lax.div(jnp.clip(live - start, 0, length) + (GROUP - 1), GROUP)


def begin_kernel(natoms, lanes, atom_ref, box_ref, projector_ref, info_ref, mine_ref, info_sem, half_sem):
    nslab = lax.axis_size("slab")
    half = mine_ref.shape[0] - INFO
    core = lax.rem(lax.axis_index("band"), 2)
    copy = pltpu.make_async_copy(
        projector_ref.at[pl.ds(pl.multiple_of(core * half, GROUP), half), :],
        mine_ref.at[pl.ds(INFO, half), :],
        half_sem,
    )
    copy.start()
    atom_dev = natoms // nslab
    below = lax.rem(lax.axis_index("slab") + nslab - 1, nslab) * atom_dev
    atom = atom_ref[...]
    slots = atom.shape[1]
    relative = atom - below
    relative = jnp.where(relative < 0, relative + natoms, relative)
    column = jnp.where(relative < atom_dev, relative, relative + (lanes - atom_dev))
    live = jnp.sum(jnp.where(atom >= 0, 1.0, 0.0), axis=1, keepdims=True)
    info_ref[...] = jnp.zeros(info_ref.shape, jnp.float32)
    info_ref[0:1, 0:slots] = box_ref[...].astype(jnp.float32)
    info_ref[1:2, 0:slots] = jnp.broadcast_to(live, (1, slots))
    info_ref[2:3, 0:slots] = jnp.where(atom >= 0, column, -1).astype(jnp.float32)
    head = pltpu.make_async_copy(info_ref, mine_ref.at[pl.ds(0, INFO), :], info_sem)
    head.start()
    head.wait()
    copy.wait()


def begin(slot_atom, slot_box, projectors, natoms, lanes):
    slots, depth = projectors.shape
    return pl.pallas_call(
        functools.partial(begin_kernel, natoms, lanes),
        out_shape=[
            jax.ShapeDtypeStruct((INFO, depth), jnp.float32),
            jax.ShapeDtypeStruct((INFO + slots // 2, depth), jnp.float32),
        ],
        in_specs=[VMEM, VMEM, ANY],
        out_specs=[VMEM, ANY],
        scratch_shapes=[pltpu.SemaphoreType.DMA(()), pltpu.SemaphoreType.DMA(())],
        compiler_params=params(8 * MIB),
        name="begin",
    )(
        slot_atom.reshape(1, slots),
        slot_box.reshape(1, slots),
        pltpu.with_memory_space_constraint(projectors, pltpu.HBM),
    )


def scalar_row(info, first):
    return jnp.concatenate([info[0:1, :] + first, info[1:2, 0:128]], axis=1).astype(jnp.int32)


def project_kernel(pieces, infos, place_ref, x_ref, *refs):
    arrays = refs[: -len(pieces) - 4]
    outs = refs[-len(pieces) - 4 : -4]
    whole, proj, table, sem = refs[-4:]
    for k, index in enumerate(infos):
        whole[k : k + 1, :] = scalar_row(arrays[index][0:INFO, :], 0)
    copy = pltpu.make_async_copy(whole, table, sem)
    copy.start()
    rows = x_ref.shape[1]
    slots = arrays[infos[0]].shape[1]
    width = proj.shape[3]
    chunk = width // GROUP
    lane_block = lax.broadcasted_iota(jnp.int32, (rows, width), 1) // GROUP
    low_half = lax.broadcasted_iota(jnp.int32, (GROUP, 128), 1) < BOXPTS
    lane_slot = lax.broadcasted_iota(jnp.int32, (rows, width), 1) % GROUP
    proj[...] = jnp.zeros(proj.shape, jnp.float32)
    copy.wait()
    for which, p in enumerate(pieces):
        array = arrays[p.array]
        start = place_ref[3 * p.index + 1]
        box_base = place_ref[3 * p.index + 2]
        info = infos.index(p.info)
        count = live_groups(table[info, slots], start, p.rows)

        def step(block, carry):
            groups = [block * UNROLL + u for u in range(UNROLL)]
            weights, patches = [], []
            for g in groups:
                first = pl.multiple_of(p.offset + g * GROUP, 8)
                weights.append(slot_weights(array[pl.ds(first, GROUP), :], low_half, 1))
                boxes = [table[info, start + g * GROUP + s] for s in range(GROUP)]
                patches.append(jnp.concatenate([x_ref[box_base + b] for b in boxes], axis=0))
            totals = []
            for w, p_ in zip(weights, patches):
                product = lax.dot_general(
                    p_, w, (((1,), (1,)), ((), ())), preferred_element_type=jnp.float32
                )
                total = product[0:rows]
                for s in range(1, GROUP):
                    total = jnp.where(lane_slot == s, product[s * rows : (s + 1) * rows], total)
                totals.append(total)
            for g, total in zip(groups, totals):
                proj[which, g] = total
            return carry

        lax.fori_loop(0, lax.div(count + (UNROLL - 1), UNROLL), step, 0)

    for which, (p, out) in enumerate(zip(pieces, outs)):
        start = place_ref[3 * p.index + 1]
        columns = arrays[p.info][2:3, :]
        columns = pltpu.roll(columns, lax.rem(columns.shape[1] - start, columns.shape[1]), 1)
        nchunk = (p.rows // GROUP + chunk - 1) // chunk
        value = jnp.concatenate(
            [
                jnp.concatenate(
                    swap_blocks(
                        [proj[which, k * chunk + i] for i in range(chunk)], lane_block, width
                    ),
                    axis=0,
                )
                for k in range(nchunk)
            ],
            axis=1,
        )
        both = lax.dot_general(
            stacked_split(value),
            selector(columns[:, : nchunk * width], out.shape[1]),
            (((1,), (1,)), ((), ())),
            preferred_element_type=jnp.float32,
        )
        half = both.shape[0] // 2
        out[...] = both[:half] + both[half:]


def project(arrays, pieces, place, x, lanes):
    channel = arrays[0].shape[1] // BOXPTS
    used = sorted({p.array for p in pieces} | {p.info for p in pieces})
    local = [
        p._replace(array=used.index(p.array), info=used.index(p.info)) for p in pieces
    ]
    infos = sorted({p.info for p in local})
    shapes = [
        jax.ShapeDtypeStruct((channel * x.shape[1], 2 * lanes), jnp.float32) for p in pieces
    ]
    size = sum(p.rows for p in pieces) * arrays[0].shape[1]
    table = (round_up(len(infos), 8), arrays[0].shape[1] + 128)
    groups = round_up(max(p.rows for p in pieces), channel * GROUP) // GROUP
    return pl.pallas_call(
        functools.partial(project_kernel, local, infos),
        out_shape=shapes,
        in_specs=[SMEM, VMEM] + [VMEM] * len(used),
        out_specs=[VMEM] * len(pieces),
        scratch_shapes=[
            pltpu.VMEM(table, jnp.int32),
            pltpu.VMEM((len(pieces), groups, x.shape[1], channel * GROUP), jnp.float32),
            pltpu.SMEM(table, jnp.int32),
            pltpu.SemaphoreType.DMA(()),
        ],
        compiler_params=params(40 * MIB),
        cost_estimate=pl.CostEstimate(
            flops=2 * 16 * 16 * size, bytes_accessed=4 * size + 2 * x.size, transcendentals=0
        ),
        name="project",
    )(place, x, *[arrays[i] for i in used])


def swap_blocks(tiles, lane_block, width):
    tiles = list(tiles)
    bit = 1
    while bit < len(tiles):
        upper = (lane_block & bit) != 0
        for i in range(len(tiles)):
            if not i & bit:
                a, b = tiles[i], tiles[i | bit]
                tiles[i] = jnp.where(upper, pltpu.roll(b, GROUP * bit, 1), a)
                tiles[i | bit] = jnp.where(upper, b, pltpu.roll(a, width - GROUP * bit, 1))
        bit *= 2
    return tiles


def selector(columns, count):
    shape = (count, columns.shape[1])
    row = lax.broadcasted_iota(jnp.int32, shape, 0).astype(jnp.float32)
    return jnp.where(jnp.broadcast_to(columns, shape) == row, 1.0, 0.0).astype(jnp.bfloat16)


def stacked_split(value):
    high = value.astype(jnp.bfloat16)
    low = (value - high.astype(jnp.float32)).astype(jnp.bfloat16)
    return jnp.concatenate([high, low], axis=0)


def apply_kernel(nslab, slots, nsum, pieces, infos, place_ref, coupling_ref, *refs):
    npiece = len(pieces)
    proj, loaded, parts, beta, done, masks, info, whole, table = refs[-13:-4]
    sums = refs[-13 - nsum : -13]
    beta_sem, proj_sem, info_sem, out_sem = refs[-4:]
    base = len(refs) - 14 - nsum
    out_ref = refs[base]
    projections = refs[base - npiece : base]
    arrays = refs[: base - npiece]
    groups = slots // GROUP
    rows, width = proj.shape[1], proj.shape[2]
    channel = width // GROUP
    lanes = parts.shape[2] // 2
    boxes = out_ref.shape[1] // BOXPTS // nslab
    chunk = width // GROUP
    info_copies, copies, beta_copies = [], [], []
    for i, (array, index) in enumerate(infos):
        slab = place_ref[3 * index]
        info_copies.append(
            pltpu.make_async_copy(arrays[array].at[0:INFO, :], info.at[slab], info_sem.at[i])
        )
    for i, p in enumerate(pieces):
        slab, start = place_ref[3 * p.index], place_ref[3 * p.index + 1]
        j = i % loaded.shape[0]
        copies.append(
            pltpu.make_async_copy(projections[i], loaded.at[j], proj_sem.at[i])
        )
        first = pl.multiple_of(slab * slots + start, GROUP)
        beta_copies.append(
            pltpu.make_async_copy(
                arrays[p.array].at[p.offset : p.offset + p.rows, :],
                beta.at[pl.ds(first, p.rows), :],
                beta_sem.at[i],
            )
        )
    for c in info_copies + copies[: loaded.shape[0]] + beta_copies:
        c.start()
    lane_slot = lax.broadcasted_iota(jnp.int32, (rows, width), 1) % GROUP
    for s in range(GROUP):
        masks[s] = jnp.where(lane_slot == s, 1.0, 0.0).astype(jnp.bfloat16)
    for total in sums:
        total[...] = jnp.zeros(total.shape, jnp.float32)
    parts[...] = jnp.zeros(parts.shape, jnp.float32)
    for c in info_copies:
        c.wait()
    for slab in range(nslab):
        whole[slab : slab + 1, :] = scalar_row(info[slab], float(slab * boxes))
    to_scalars = pltpu.make_async_copy(whole, table, info_sem.at[0])
    to_scalars.start()
    for first in range(0, npiece, loaded.shape[0]):
        wave = range(first, min(first + loaded.shape[0], npiece))
        for i in wave:
            if first > 0:
                copies[i].start()
        for i in wave:
            copies[i].wait()
        for i in wave:
            slab = place_ref[3 * pieces[i].index]
            parts[slab] = parts[slab] + loaded[i % loaded.shape[0]]

    lane_block = lax.broadcasted_iota(jnp.int32, (rows, width), 1) // GROUP
    def couple(slab, carry):
        following = lax.rem(slab + 1, nslab)
        total = parts[slab, :, lanes:] + parts[following, :, :lanes]
        for c in range(channel):
            mixed = jnp.zeros((rows, lanes), jnp.float32)
            for e in range(channel):
                factor = coupling_ref[slab, pl.ds(c * channel + e, 1), :]
                mixed = mixed + factor * total[e * rows : (e + 1) * rows]
            parts[slab, c * rows : (c + 1) * rows, lanes:] = mixed
        return carry

    lax.fori_loop(0, nslab, couple, 0)

    def spread(slab, carry):
        below = lax.rem(slab + nslab - 1, nslab)
        value = jnp.concatenate([parts[below, :, lanes:], parts[slab, :, lanes:]], axis=1)
        value = stacked_split(value)

        both = jnp.dot(
            value, selector(info[slab, 2:3, 0:slots], 2 * lanes), preferred_element_type=jnp.float32
        )
        half = both.shape[0] // 2
        both = both[:half] + both[half:]
        for k in range(groups // chunk):
            tiles = [
                both[c * rows : (c + 1) * rows, k * width : (k + 1) * width]
                for c in range(channel)
            ]
            for i, tile in enumerate(swap_blocks(tiles, lane_block, width)):
                proj[slab * groups + k * chunk + i] = tile
        return carry

    lax.fori_loop(0, nslab, spread, 0, unroll=4 if nsum > 1 else 1)
    to_scalars.wait()

    for c in beta_copies:
        c.wait()

    low_half = lax.broadcasted_iota(jnp.int32, (GROUP, 128), 1) < BOXPTS
    pair_half = lax.broadcasted_iota(jnp.int32, (rows, 128), 1) < BOXPTS
    span = boxes * BOXPTS

    def leaving(slab):
        slot = lax.rem(slab, 2)
        return pltpu.make_async_copy(
            done.at[slot],
            out_ref.at[:, pl.ds(pl.multiple_of(slab * span, 128), span)],
            out_sem.at[slot],
        )

    def slab_step(slab, carry):
        def step(block, inner):
            products = []
            for u in range(UNROLL):
                g = block * UNROLL + u
                slot_base = pl.multiple_of(slab * slots + g * GROUP, GROUP)
                weights = slot_weights(beta[pl.ds(slot_base, GROUP), :], low_half, 0)
                c = proj[slab * groups + g]
                high = c.astype(jnp.bfloat16)
                low = (c - high.astype(jnp.float32)).astype(jnp.bfloat16)
                left = jnp.concatenate(
                    [
                        jnp.concatenate([high * masks[s], low * masks[s]], axis=1)
                        for s in range(GROUP)
                    ],
                    axis=0,
                )
                products.append((slot_base, jnp.dot(left, weights, preferred_element_type=jnp.float32)))
            for u, (slot_base, product) in enumerate(products):
                for s in range(GROUP):
                    box = table[slab, block * (UNROLL * GROUP) + u * GROUP + s]
                    j = (u * GROUP + s) % nsum
                    sums[j][box] = sums[j][box] + product[s * rows : (s + 1) * rows]
            return inner

        count = live_groups(table[slab, info.shape[2]], 0, slots)
        lax.fori_loop(0, lax.div(count + (UNROLL - 1), UNROLL), step, 0)

        @pl.when(slab >= 2)
        def _():
            leaving(slab - 2).wait()

        def finish(pair, inner):
            folded = []
            for i in range(2):
                box = slab * boxes + 2 * pair + i
                value = sums[0][box]
                for j in range(1, nsum):
                    value = value + sums[j][box]
                folded.append(value + pltpu.roll(value, BOXPTS, 1))
            done[lax.rem(slab, 2), :, pl.ds(pl.multiple_of(pair * 128, 128), 128)] = jnp.where(
                pair_half, folded[0], folded[1]
            )
            return inner

        lax.fori_loop(0, span // 128, finish, 0, unroll=8)
        leaving(slab).start()
        return carry

    lax.fori_loop(0, nslab, slab_step, 0)
    for slab in range(max(nslab - 2, 0), nslab):
        leaving(slab).wait()


def apply(arrays, pieces, infos, projections, place, coupling, nslab, slots, rows, ngrid):
    width = projections[0].shape[0] // rows * GROUP
    lanes = coupling.shape[2]
    depth = arrays[0].shape[1]
    one_sum = ngrid // BOXPTS * rows * 128 * 4
    nsum = 2 if one_sum <= 8 * MIB else 1
    buffers = [pltpu.VMEM((ngrid // BOXPTS, rows, 128), jnp.float32) for _ in range(nsum)]
    buffers += [
        pltpu.VMEM((nslab * slots // GROUP, rows, width), jnp.float32),
        pltpu.VMEM((len(pieces) if len(pieces) <= 24 else 1,) + projections[0].shape, jnp.float32),
        pltpu.VMEM((nslab,) + projections[0].shape, jnp.float32),
        pltpu.VMEM((nslab * slots, depth), jnp.float32),
        pltpu.VMEM((2, rows, ngrid // nslab), jnp.float32),
        pltpu.VMEM((GROUP, rows, width), jnp.bfloat16),
        pltpu.VMEM((nslab, INFO, depth), jnp.float32),
        pltpu.VMEM((nslab, depth + 128), jnp.int32),
    ]
    need = sum(math.prod(b.shape) * b.dtype.itemsize for b in buffers)
    scratch = buffers + [
        pltpu.SMEM((nslab, depth + 128), jnp.int32),
        pltpu.SemaphoreType.DMA((len(pieces),)),
        pltpu.SemaphoreType.DMA((len(pieces),)),
        pltpu.SemaphoreType.DMA((len(infos),)),
        pltpu.SemaphoreType.DMA((2,)),
    ]
    return pl.pallas_call(
        functools.partial(apply_kernel, nslab, slots, nsum, pieces, infos),
        out_shape=jax.ShapeDtypeStruct((rows, ngrid), jnp.float32),
        in_specs=[SMEM, VMEM] + [ANY] * (len(arrays) + len(pieces)),
        out_specs=ANY,
        scratch_shapes=scratch,
        compiler_params=params(min(need + 4 * MIB, 63 * MIB)),
        name="apply",
    )(place, coupling, *arrays, *projections)


Piece = collections.namedtuple("Piece", ["array", "offset", "rows", "info", "index"])


def gather_and_project(projectors, described, mine, split, extra, lanes, nband, nslab):
    slots = projectors.shape[0]
    order, at = cycle_tables(nslab)
    half = slots // 2
    quarter = half // 2
    reach = nslab // 2
    onward = [
        (b * nslab + order[i], b * nslab + order[(i + 1) % nslab])
        for b in range(nband)
        for i in range(nslab)
    ]
    backward = [(d, s) for s, d in onward]
    sibling = [(b * nslab + s, (b ^ 1) * nslab + s) for b in range(nband) for s in range(nslab)]

    where = [(0, 0, None)]
    for step in range(1, reach):
        where += [(1 - step, 0, True), (step - 1, 0, True)] if step > 1 else []
        where += [(-step, 0, False), (step, 0, False)]
    where += [(1 - reach, 0, True), (reach - 1, 0, True)]
    where += [(reach, 0, False), (reach, quarter, False), (reach, 0, True), (reach, quarter, True)]
    boxes = split.shape[0] // nslab

    def entry(core, slab, distance, start, other):
        there = order[(at[slab] + distance) % nslab]
        if other is not None:
            start += half * ((1 - core) if other else core)
        return there, start, there * boxes

    table = [[entry(b % 2, s, *w) for w in where] for b in range(nband) for s in range(nslab)]
    me = lax.axis_index("band") * nslab + lax.axis_index("slab")
    place = lax.dynamic_index_in_dim(
        jnp.asarray(np.array(table, np.int32)), me, 0, keepdims=False
    ).reshape(-1)

    arrays, pieces, infos, projections = [described, projectors], [], [(0, 0)], []

    def add(array, info=None):
        arrays.append(array)
        own = len(arrays) - 1
        offset = INFO if info is None else 0
        pieces.append(
            Piece(own, offset, array.shape[0] - offset, own if info is None else info, len(pieces))
        )
        return own

    pieces.append(Piece(1, 0, slots, 0, 0))
    up = lax.ppermute(mine, AXES, onward)
    down = lax.ppermute(mine, AXES, backward)
    done = 0

    def project_new():
        nonlocal done
        projections.extend(project(arrays, pieces[done:], place, split, lanes))
        done = len(pieces)

    project_new()
    up, down, projections, place = lax.optimization_barrier((up, down, projections, place))
    projections = list(projections)
    near = []
    for step in range(1, reach + 1):
        last = step == reach
        for array in near:
            add(array)
        for array in (up,) if last else (up, down):
            infos.append((add(array), len(pieces) - 1))
        if last:
            add(down, len(arrays) - 1)
        near = [lax.ppermute(up, AXES, sibling), lax.ppermute(down, AXES, sibling)]
        if step + 1 < reach:
            up = lax.ppermute(up, AXES, onward)
            down = lax.ppermute(down, AXES, backward)
        elif not last:
            up = lax.ppermute(up[: INFO + quarter], AXES, onward)
            down = lax.ppermute(down[INFO + quarter :], AXES, backward)
        project_new()
        up, down, near, projections, extra = lax.optimization_barrier(
            (up, down, near, projections, extra)
        )
        near, projections = list(near), list(projections)
    add(near[0])
    add(near[1], len(arrays) - 1)
    project_new()
    return arrays, pieces, infos, projections, place, extra


def body(bands, projectors, slot_atom, slot_box, channels, coupling):
    nblock, band_local, ngrid = bands.shape
    nband, nslab = lax.axis_size("band"), lax.axis_size("slab")
    natoms = channels.shape[0]
    atom_dev = natoms // nslab
    channel = coupling.shape[0]
    slots = slot_atom.shape[0]
    lanes = round_up(atom_dev, 128)

    described, mine = begin(slot_atom, slot_box, projectors, natoms, lanes)
    mask = (jnp.arange(channel, dtype=jnp.int32)[:, None] < channels[None, :]).astype(jnp.float32)
    masked = coupling * mask[:, None, :] * mask[None, :, :]
    masked = masked.reshape(channel * channel, nslab, atom_dev).transpose(1, 0, 2)
    masked = jnp.pad(masked, ((0, 0), (0, 0), (0, lanes - atom_dev)))

    rows = nblock * band_local
    padded = round_up(rows, GROUP)
    x = bands.reshape(rows, ngrid)
    if padded != rows:
        x = jnp.pad(x, ((0, padded - rows), (0, 0)))
    split = split_bands(x)
    arrays, pieces, infos, projections, place, masked = gather_and_project(
        projectors, described, mine, split, masked, lanes, nband, nslab
    )
    out = apply(arrays, pieces, infos, projections, place, masked, nslab, slots, padded, ngrid)
    return out[:rows].reshape(nblock, band_local, ngrid)


def solution(mesh):
    in_specs = (P(None, ("band", "slab"), None), P("slab", None), P("slab"), P("slab"), P(), P())
    out_specs = P(None, ("band", "slab"), None)
    return jax.shard_map(body, mesh=mesh, in_specs=in_specs, out_specs=out_specs, check_vma=False)
```

```python
import collections
import functools
import math

import jax
import jax.numpy as jnp
import numpy as np
from jax import lax
from jax.experimental import pallas as pl
from jax.experimental.pallas import tpu as pltpu
from jax.sharding import PartitionSpec as P

BOXPTS = 64
GROUP = 16
INFO = 8
UNROLL = 8
AXES = ("band", "slab")
MIB = 1 << 20


def round_up(value, step):
    return (value + step - 1) // step * step


def cycle_tables(nslab):
    order = list(range(0, nslab, 2)) + list(range(nslab - 1 - nslab % 2, 0, -2))
    place = {s: i for i, s in enumerate(order)}
    return order, place


def params(limit):
    return pltpu.CompilerParams(vmem_limit_bytes=limit)


VMEM = pl.BlockSpec(memory_space=pltpu.VMEM)
SMEM = pl.BlockSpec(memory_space=pltpu.SMEM)
ANY = pl.BlockSpec(memory_space=pl.ANY)


def split_bands_kernel(atom_dev, x_ref, coupling_ref, channels_ref, out_ref, masked_ref, whole):
    @pl.when(pl.program_id(0) == 0)
    def _():
        channel = channels_ref.shape[0]
        natoms = channels_ref.shape[1]
        number = lax.broadcasted_iota(jnp.int32, (channel, natoms), 0)
        mask = jnp.where(number < channels_ref[...], 1.0, 0.0)
        for c in range(channel):
            own = slice(c * channel, (c + 1) * channel)
            whole[own, :] = coupling_ref[own, :] * mask * mask[c : c + 1, :]
        lanes = masked_ref.shape[2]
        for slab in range(masked_ref.shape[0]):
            base = slab * atom_dev // 128 * 128
            part = whole[:, base : min(base + lanes + 128, natoms)]
            if part.shape[1] < lanes:
                part = jnp.concatenate([part, part[:, : lanes - part.shape[1]]], axis=1)
            if slab * atom_dev != base:
                part = pltpu.roll(part, part.shape[1] - (slab * atom_dev - base), 1)
            masked_ref[slab] = part[:, :lanes]

    rows = x_ref.shape[0]
    low_half = lax.broadcasted_iota(jnp.int32, (rows, 128), 1) < BOXPTS
    zero = jnp.zeros((rows, 128), jnp.float32)

    def step(pair, carry):
        x = x_ref[:, pl.ds(pl.multiple_of(pair * 128, 128), 128)]
        high = x.astype(jnp.bfloat16).astype(jnp.float32)
        low = x - high
        high_turned = pltpu.roll(high, BOXPTS, 1)
        low_turned = pltpu.roll(low, BOXPTS, 1)
        out_ref[2 * pair, :, 0:128] = jnp.where(low_half, high, high_turned).astype(jnp.bfloat16)
        out_ref[2 * pair, :, 128:256] = jnp.where(low_half, low, zero).astype(jnp.bfloat16)
        out_ref[2 * pair + 1, :, 0:128] = jnp.where(low_half, high_turned, high).astype(jnp.bfloat16)
        out_ref[2 * pair + 1, :, 128:256] = jnp.where(low_half, low_turned, zero).astype(jnp.bfloat16)
        return carry

    lax.fori_loop(0, x_ref.shape[1] // 128, step, 0, unroll=4)


def split_bands(x, coupling, channels, nslab, lanes):
    rows, ngrid = x.shape
    channel, natoms = coupling.shape[1:]
    span = ngrid // nslab
    boxes = span // BOXPTS
    return pl.pallas_call(
        functools.partial(split_bands_kernel, natoms // nslab),
        grid=(nslab,),
        out_shape=[
            jax.ShapeDtypeStruct((ngrid // BOXPTS, rows, 256), jnp.bfloat16),
            jax.ShapeDtypeStruct((nslab, channel * channel, lanes), jnp.float32),
        ],
        in_specs=[
            pl.BlockSpec((rows, span), lambda i: (0, i)),
            pl.BlockSpec((channel * channel, natoms), lambda i: (0, 0)),
            pl.BlockSpec((channel, natoms), lambda i: (0, 0)),
        ],
        out_specs=[
            pl.BlockSpec((boxes, rows, 256), lambda i: (i, 0, 0)),
            pl.BlockSpec((nslab, channel * channel, lanes), lambda i: (0, 0, 0)),
        ],
        scratch_shapes=[pltpu.VMEM((channel * channel, natoms), jnp.float32)],
        compiler_params=params(16 * MIB),
        cost_estimate=pl.CostEstimate(
            flops=8 * x.size, bytes_accessed=12 * x.size, transcendentals=0
        ),
        name="split_bands",
    )(
        pltpu.with_memory_space_constraint(x, pltpu.HBM),
        coupling.reshape(channel * channel, natoms),
        jnp.broadcast_to(channels[None, :], (channel, natoms)),
    )


def slot_weights(values, low_half, axis):
    full, top = [], []
    for t in range(values.shape[1] // 128):
        x = values[:, t * 128 : (t + 1) * 128]
        high = x.astype(jnp.bfloat16).astype(jnp.float32)
        low = x - high
        turned = pltpu.roll(high, BOXPTS, 1)
        full.append(jnp.where(low_half, high, pltpu.roll(low, BOXPTS, 1)).astype(jnp.bfloat16))
        full.append(jnp.where(low_half, turned, low).astype(jnp.bfloat16))
        top.append(jnp.where(low_half, high, 0.0).astype(jnp.bfloat16))
        top.append(jnp.where(low_half, turned, 0.0).astype(jnp.bfloat16))
    return jnp.concatenate(
        [jnp.concatenate(full, axis=0), jnp.concatenate(top, axis=0)], axis=axis
    )


def live_groups(live, start, length):
    return lax.div(jnp.clip(live - start, 0, length) + (GROUP - 1), GROUP)


def begin_kernel(natoms, lanes, atom_ref, box_ref, projector_ref, info_ref, mine_ref, info_sem, half_sem):
    nslab = lax.axis_size("slab")
    half = mine_ref.shape[0] - INFO
    core = lax.rem(lax.axis_index("band"), 2)
    copy = pltpu.make_async_copy(
        projector_ref.at[pl.ds(pl.multiple_of(core * half, GROUP), half), :],
        mine_ref.at[pl.ds(INFO, half), :],
        half_sem,
    )
    copy.start()
    atom_dev = natoms // nslab
    below = lax.rem(lax.axis_index("slab") + nslab - 1, nslab) * atom_dev
    atom = atom_ref[...]
    slots = atom.shape[1]
    relative = atom - below
    relative = jnp.where(relative < 0, relative + natoms, relative)
    column = jnp.where(relative < atom_dev, relative, relative + (lanes - atom_dev))
    live = jnp.sum(jnp.where(atom >= 0, 1.0, 0.0), axis=1, keepdims=True)
    info_ref[...] = jnp.zeros(info_ref.shape, jnp.float32)
    info_ref[0:1, 0:slots] = box_ref[...].astype(jnp.float32)
    info_ref[1:2, 0:slots] = jnp.broadcast_to(live, (1, slots))
    info_ref[2:3, 0:slots] = jnp.where(atom >= 0, column, -1).astype(jnp.float32)
    head = pltpu.make_async_copy(info_ref, mine_ref.at[pl.ds(0, INFO), :], info_sem)
    head.start()
    head.wait()
    copy.wait()


def begin(slot_atom, slot_box, projectors, natoms, lanes):
    slots, depth = projectors.shape
    return pl.pallas_call(
        functools.partial(begin_kernel, natoms, lanes),
        out_shape=[
            jax.ShapeDtypeStruct((INFO, depth), jnp.float32),
            jax.ShapeDtypeStruct((INFO + slots // 2, depth), jnp.float32),
        ],
        in_specs=[VMEM, VMEM, ANY],
        out_specs=[VMEM, ANY],
        scratch_shapes=[pltpu.SemaphoreType.DMA(()), pltpu.SemaphoreType.DMA(())],
        compiler_params=params(8 * MIB),
        name="begin",
    )(
        slot_atom.reshape(1, slots),
        slot_box.reshape(1, slots),
        pltpu.with_memory_space_constraint(projectors, pltpu.HBM),
    )


def scalar_row(info, first):
    return jnp.concatenate([info[0:1, :] + first, info[1:2, 0:128]], axis=1).astype(jnp.int32)


def project_kernel(pieces, infos, place_ref, x_ref, *refs):
    arrays = refs[: -len(pieces) - 4]
    outs = refs[-len(pieces) - 4 : -4]
    whole, proj, table, sem = refs[-4:]
    for k, index in enumerate(infos):
        whole[k : k + 1, :] = scalar_row(arrays[index][0:INFO, :], 0)
    copy = pltpu.make_async_copy(whole, table, sem)
    copy.start()
    rows = x_ref.shape[1]
    slots = arrays[infos[0]].shape[1]
    width = proj.shape[3]
    chunk = width // GROUP
    lane_block = lax.broadcasted_iota(jnp.int32, (rows, width), 1) // GROUP
    low_half = lax.broadcasted_iota(jnp.int32, (GROUP, 128), 1) < BOXPTS
    lane_slot = lax.broadcasted_iota(jnp.int32, (rows, width), 1) % GROUP
    proj[...] = jnp.zeros(proj.shape, jnp.float32)
    copy.wait()
    for which, p in enumerate(pieces):
        array = arrays[p.array]
        start = place_ref[3 * p.index + 1]
        box_base = place_ref[3 * p.index + 2]
        info = infos.index(p.info)
        count = live_groups(table[info, slots], start, p.rows)

        def step(block, carry):
            groups = [block * UNROLL + u for u in range(UNROLL)]
            weights, patches = [], []
            for g in groups:
                first = pl.multiple_of(p.offset + g * GROUP, 8)
                weights.append(slot_weights(array[pl.ds(first, GROUP), :], low_half, 1))
                boxes = [table[info, start + g * GROUP + s] for s in range(GROUP)]
                patches.append(jnp.concatenate([x_ref[box_base + b] for b in boxes], axis=0))
            totals = []
            for w, p_ in zip(weights, patches):
                product = lax.dot_general(
                    p_, w, (((1,), (1,)), ((), ())), preferred_element_type=jnp.float32
                )
                total = product[0:rows]
                for s in range(1, GROUP):
                    total = jnp.where(lane_slot == s, product[s * rows : (s + 1) * rows], total)
                totals.append(total)
            for g, total in zip(groups, totals):
                proj[which, g] = total
            return carry

        lax.fori_loop(0, lax.div(count + (UNROLL - 1), UNROLL), step, 0)

    for which, (p, out) in enumerate(zip(pieces, outs)):
        start = place_ref[3 * p.index + 1]
        columns = arrays[p.info][2:3, :]
        columns = pltpu.roll(columns, lax.rem(columns.shape[1] - start, columns.shape[1]), 1)
        nchunk = (p.rows // GROUP + chunk - 1) // chunk
        value = jnp.concatenate(
            [
                jnp.concatenate(
                    swap_blocks(
                        [proj[which, k * chunk + i] for i in range(chunk)], lane_block, width
                    ),
                    axis=0,
                )
                for k in range(nchunk)
            ],
            axis=1,
        )
        both = lax.dot_general(
            stacked_split(value),
            selector(columns[:, : nchunk * width], out.shape[1]),
            (((1,), (1,)), ((), ())),
            preferred_element_type=jnp.float32,
        )
        half = both.shape[0] // 2
        out[...] = both[:half] + both[half:]


def project(arrays, pieces, place, x, lanes):
    channel = arrays[0].shape[1] // BOXPTS
    used = sorted({p.array for p in pieces} | {p.info for p in pieces})
    local = [
        p._replace(array=used.index(p.array), info=used.index(p.info)) for p in pieces
    ]
    infos = sorted({p.info for p in local})
    shapes = [
        jax.ShapeDtypeStruct((channel * x.shape[1], 2 * lanes), jnp.float32) for p in pieces
    ]
    size = sum(p.rows for p in pieces) * arrays[0].shape[1]
    table = (round_up(len(infos), 8), arrays[0].shape[1] + 128)
    groups = round_up(max(p.rows for p in pieces), channel * GROUP) // GROUP
    return pl.pallas_call(
        functools.partial(project_kernel, local, infos),
        out_shape=shapes,
        in_specs=[SMEM, VMEM] + [VMEM] * len(used),
        out_specs=[VMEM] * len(pieces),
        scratch_shapes=[
            pltpu.VMEM(table, jnp.int32),
            pltpu.VMEM((len(pieces), groups, x.shape[1], channel * GROUP), jnp.float32),
            pltpu.SMEM(table, jnp.int32),
            pltpu.SemaphoreType.DMA(()),
        ],
        compiler_params=params(40 * MIB),
        cost_estimate=pl.CostEstimate(
            flops=2 * 16 * 16 * size, bytes_accessed=4 * size + 2 * x.size, transcendentals=0
        ),
        name="project",
    )(place, x, *[arrays[i] for i in used])


def swap_blocks(tiles, lane_block, width):
    tiles = list(tiles)
    bit = 1
    while bit < len(tiles):
        upper = (lane_block & bit) != 0
        for i in range(len(tiles)):
            if not i & bit:
                a, b = tiles[i], tiles[i | bit]
                tiles[i] = jnp.where(upper, pltpu.roll(b, GROUP * bit, 1), a)
                tiles[i | bit] = jnp.where(upper, b, pltpu.roll(a, width - GROUP * bit, 1))
        bit *= 2
    return tiles


def selector(columns, count):
    shape = (count, columns.shape[1])
    row = lax.broadcasted_iota(jnp.int32, shape, 0).astype(jnp.float32)
    return jnp.where(jnp.broadcast_to(columns, shape) == row, 1.0, 0.0).astype(jnp.bfloat16)


def stacked_split(value):
    high = value.astype(jnp.bfloat16)
    low = (value - high.astype(jnp.float32)).astype(jnp.bfloat16)
    return jnp.concatenate([high, low], axis=0)


def apply_kernel(nslab, slots, nsum, pieces, infos, place_ref, coupling_ref, *refs):
    npiece = len(pieces)
    proj, loaded, parts, beta, done, masks, info, whole, table = refs[-13:-4]
    sums = refs[-13 - nsum : -13]
    beta_sem, proj_sem, info_sem, out_sem = refs[-4:]
    base = len(refs) - 14 - nsum
    out_ref = refs[base]
    projections = refs[base - npiece : base]
    arrays = refs[: base - npiece]
    groups = slots // GROUP
    rows, width = proj.shape[1], proj.shape[2]
    channel = width // GROUP
    lanes = parts.shape[2] // 2
    boxes = out_ref.shape[1] // BOXPTS // nslab
    chunk = width // GROUP
    info_copies, copies, beta_copies = [], [], []
    for i, (array, index) in enumerate(infos):
        slab = place_ref[3 * index]
        info_copies.append(
            pltpu.make_async_copy(arrays[array].at[0:INFO, :], info.at[slab], info_sem.at[i])
        )
    for i, p in enumerate(pieces):
        slab, start = place_ref[3 * p.index], place_ref[3 * p.index + 1]
        j = i % loaded.shape[0]
        copies.append(
            pltpu.make_async_copy(projections[i], loaded.at[j], proj_sem.at[i])
        )
        first = pl.multiple_of(slab * slots + start, GROUP)
        beta_copies.append(
            pltpu.make_async_copy(
                arrays[p.array].at[p.offset : p.offset + p.rows, :],
                beta.at[pl.ds(first, p.rows), :],
                beta_sem.at[i],
            )
        )
    for c in info_copies + copies[: loaded.shape[0]] + beta_copies:
        c.start()
    lane_slot = lax.broadcasted_iota(jnp.int32, (rows, width), 1) % GROUP
    for s in range(GROUP):
        masks[s] = jnp.where(lane_slot == s, 1.0, 0.0).astype(jnp.bfloat16)
    for total in sums:
        total[...] = jnp.zeros(total.shape, jnp.float32)
    parts[...] = jnp.zeros(parts.shape, jnp.float32)
    for c in info_copies:
        c.wait()
    for slab in range(nslab):
        whole[slab : slab + 1, :] = scalar_row(info[slab], float(slab * boxes))
    to_scalars = pltpu.make_async_copy(whole, table, info_sem.at[0])
    to_scalars.start()
    for first in range(0, npiece, loaded.shape[0]):
        wave = range(first, min(first + loaded.shape[0], npiece))
        for i in wave:
            if first > 0:
                copies[i].start()
        for i in wave:
            copies[i].wait()
        for i in wave:
            slab = place_ref[3 * pieces[i].index]
            parts[slab] = parts[slab] + loaded[i % loaded.shape[0]]

    lane_block = lax.broadcasted_iota(jnp.int32, (rows, width), 1) // GROUP
    def couple(slab, carry):
        following = lax.rem(slab + 1, nslab)
        total = parts[slab, :, lanes:] + parts[following, :, :lanes]
        for c in range(channel):
            mixed = jnp.zeros((rows, lanes), jnp.float32)
            for e in range(channel):
                factor = coupling_ref[slab, pl.ds(c * channel + e, 1), :]
                mixed = mixed + factor * total[e * rows : (e + 1) * rows]
            parts[slab, c * rows : (c + 1) * rows, lanes:] = mixed
        return carry

    lax.fori_loop(0, nslab, couple, 0)

    def spread(slab, carry):
        below = lax.rem(slab + nslab - 1, nslab)
        value = jnp.concatenate([parts[below, :, lanes:], parts[slab, :, lanes:]], axis=1)
        value = stacked_split(value)

        both = jnp.dot(
            value, selector(info[slab, 2:3, 0:slots], 2 * lanes), preferred_element_type=jnp.float32
        )
        half = both.shape[0] // 2
        both = both[:half] + both[half:]
        for k in range(groups // chunk):
            tiles = [
                both[c * rows : (c + 1) * rows, k * width : (k + 1) * width]
                for c in range(channel)
            ]
            for i, tile in enumerate(swap_blocks(tiles, lane_block, width)):
                proj[slab * groups + k * chunk + i] = tile
        return carry

    lax.fori_loop(0, nslab, spread, 0, unroll=4 if nsum > 1 else 1)
    to_scalars.wait()

    for c in beta_copies:
        c.wait()

    low_half = lax.broadcasted_iota(jnp.int32, (GROUP, 128), 1) < BOXPTS
    pair_half = lax.broadcasted_iota(jnp.int32, (rows, 128), 1) < BOXPTS
    span = boxes * BOXPTS

    def leaving(slab):
        slot = lax.rem(slab, 2)
        return pltpu.make_async_copy(
            done.at[slot],
            out_ref.at[:, pl.ds(pl.multiple_of(slab * span, 128), span)],
            out_sem.at[slot],
        )

    def slab_step(slab, carry):
        def step(block, inner):
            products = []
            for u in range(UNROLL):
                g = block * UNROLL + u
                slot_base = pl.multiple_of(slab * slots + g * GROUP, GROUP)
                weights = slot_weights(beta[pl.ds(slot_base, GROUP), :], low_half, 0)
                c = proj[slab * groups + g]
                high = c.astype(jnp.bfloat16)
                low = (c - high.astype(jnp.float32)).astype(jnp.bfloat16)
                left = jnp.concatenate(
                    [
                        jnp.concatenate([high * masks[s], low * masks[s]], axis=1)
                        for s in range(GROUP)
                    ],
                    axis=0,
                )
                products.append((slot_base, jnp.dot(left, weights, preferred_element_type=jnp.float32)))
            for u, (slot_base, product) in enumerate(products):
                for s in range(GROUP):
                    box = table[slab, block * (UNROLL * GROUP) + u * GROUP + s]
                    j = (u * GROUP + s) % nsum
                    sums[j][box] = sums[j][box] + product[s * rows : (s + 1) * rows]
            return inner

        count = live_groups(table[slab, info.shape[2]], 0, slots)
        lax.fori_loop(0, lax.div(count + (UNROLL - 1), UNROLL), step, 0)

        @pl.when(slab >= 2)
        def _():
            leaving(slab - 2).wait()

        def finish(pair, inner):
            folded = []
            for i in range(2):
                box = slab * boxes + 2 * pair + i
                value = sums[0][box]
                for j in range(1, nsum):
                    value = value + sums[j][box]
                folded.append(value + pltpu.roll(value, BOXPTS, 1))
            done[lax.rem(slab, 2), :, pl.ds(pl.multiple_of(pair * 128, 128), 128)] = jnp.where(
                pair_half, folded[0], folded[1]
            )
            return inner

        lax.fori_loop(0, span // 128, finish, 0, unroll=min(32, span // 128))
        leaving(slab).start()
        return carry

    lax.fori_loop(0, nslab, slab_step, 0)
    for slab in range(max(nslab - 2, 0), nslab):
        leaving(slab).wait()


def apply(arrays, pieces, infos, projections, place, coupling, nslab, slots, rows, ngrid):
    width = projections[0].shape[0] // rows * GROUP
    lanes = coupling.shape[2]
    depth = arrays[0].shape[1]
    one_sum = ngrid // BOXPTS * rows * 128 * 4
    nsum = 2 if one_sum <= 8 * MIB else 1
    buffers = [pltpu.VMEM((ngrid // BOXPTS, rows, 128), jnp.float32) for _ in range(nsum)]
    buffers += [
        pltpu.VMEM((nslab * slots // GROUP, rows, width), jnp.float32),
        pltpu.VMEM((len(pieces) if len(pieces) <= 24 else 1,) + projections[0].shape, jnp.float32),
        pltpu.VMEM((nslab,) + projections[0].shape, jnp.float32),
        pltpu.VMEM((nslab * slots, depth), jnp.float32),
        pltpu.VMEM((2, rows, ngrid // nslab), jnp.float32),
        pltpu.VMEM((GROUP, rows, width), jnp.bfloat16),
        pltpu.VMEM((nslab, INFO, depth), jnp.float32),
        pltpu.VMEM((nslab, depth + 128), jnp.int32),
    ]
    need = sum(math.prod(b.shape) * b.dtype.itemsize for b in buffers)
    scratch = buffers + [
        pltpu.SMEM((nslab, depth + 128), jnp.int32),
        pltpu.SemaphoreType.DMA((len(pieces),)),
        pltpu.SemaphoreType.DMA((len(pieces),)),
        pltpu.SemaphoreType.DMA((len(infos),)),
        pltpu.SemaphoreType.DMA((2,)),
    ]
    return pl.pallas_call(
        functools.partial(apply_kernel, nslab, slots, nsum, pieces, infos),
        out_shape=jax.ShapeDtypeStruct((rows, ngrid), jnp.float32),
        in_specs=[SMEM, VMEM] + [ANY] * (len(arrays) + len(pieces)),
        out_specs=ANY,
        scratch_shapes=scratch,
        compiler_params=params(min(need + 4 * MIB, 63 * MIB)),
        name="apply",
    )(place, coupling, *arrays, *projections)


Piece = collections.namedtuple("Piece", ["array", "offset", "rows", "info", "index"])


def gather_and_project(projectors, described, mine, split, lanes, nband, nslab):
    slots = projectors.shape[0]
    order, at = cycle_tables(nslab)
    half = slots // 2
    quarter = half // 2
    reach = nslab // 2
    onward = [
        (b * nslab + order[i], b * nslab + order[(i + 1) % nslab])
        for b in range(nband)
        for i in range(nslab)
    ]
    backward = [(d, s) for s, d in onward]
    sibling = [(b * nslab + s, (b ^ 1) * nslab + s) for b in range(nband) for s in range(nslab)]

    where = [(0, 0, None)]
    for step in range(1, reach):
        where += [(1 - step, 0, True), (step - 1, 0, True)] if step > 1 else []
        where += [(-step, 0, False), (step, 0, False)]
    where += [(1 - reach, 0, True), (reach - 1, 0, True)]
    where += [(reach, 0, False), (reach, quarter, False), (reach, 0, True), (reach, quarter, True)]
    boxes = split.shape[0] // nslab

    def entry(core, slab, distance, start, other):
        there = order[(at[slab] + distance) % nslab]
        if other is not None:
            start += half * ((1 - core) if other else core)
        return there, start, there * boxes

    table = [[entry(b % 2, s, *w) for w in where] for b in range(nband) for s in range(nslab)]
    me = lax.axis_index("band") * nslab + lax.axis_index("slab")
    place = lax.dynamic_index_in_dim(
        jnp.asarray(np.array(table, np.int32)), me, 0, keepdims=False
    ).reshape(-1)

    arrays, pieces, infos, projections = [described, projectors], [], [(0, 0)], []

    def add(array, info=None):
        arrays.append(array)
        own = len(arrays) - 1
        offset = INFO if info is None else 0
        pieces.append(
            Piece(own, offset, array.shape[0] - offset, own if info is None else info, len(pieces))
        )
        return own

    pieces.append(Piece(1, 0, slots, 0, 0))
    up = lax.ppermute(mine, AXES, onward)
    down = lax.ppermute(mine, AXES, backward)
    done = 0

    def project_new():
        nonlocal done
        projections.extend(project(arrays, pieces[done:], place, split, lanes))
        done = len(pieces)

    project_new()
    up, down, projections, place = lax.optimization_barrier((up, down, projections, place))
    projections = list(projections)
    near = []
    for step in range(1, reach + 1):
        last = step == reach
        for array in near:
            add(array)
        for array in (up,) if last else (up, down):
            infos.append((add(array), len(pieces) - 1))
        if last:
            add(down, len(arrays) - 1)
        near = [lax.ppermute(up, AXES, sibling), lax.ppermute(down, AXES, sibling)]
        if step + 1 < reach:
            up = lax.ppermute(up, AXES, onward)
            down = lax.ppermute(down, AXES, backward)
        elif not last:
            up = lax.ppermute(up[: INFO + quarter], AXES, onward)
            down = lax.ppermute(down[INFO + quarter :], AXES, backward)
        project_new()
        up, down, near, projections = lax.optimization_barrier((up, down, near, projections))
        near, projections = list(near), list(projections)
    add(near[0])
    add(near[1], len(arrays) - 1)
    project_new()
    return arrays, pieces, infos, projections, place


def body(bands, projectors, slot_atom, slot_box, channels, coupling):
    nblock, band_local, ngrid = bands.shape
    nband, nslab = lax.axis_size("band"), lax.axis_size("slab")
    natoms = channels.shape[0]
    atom_dev = natoms // nslab
    slots = slot_atom.shape[0]
    lanes = round_up(atom_dev, 128)

    described, mine = begin(slot_atom, slot_box, projectors, natoms, lanes)
    rows = nblock * band_local
    padded = round_up(rows, GROUP)
    x = bands.reshape(rows, ngrid)
    if padded != rows:
        x = jnp.pad(x, ((0, padded - rows), (0, 0)))
    split, masked = split_bands(x, coupling, channels, nslab, lanes)
    arrays, pieces, infos, projections, place = gather_and_project(
        projectors, described, mine, split, lanes, nband, nslab
    )
    out = apply(arrays, pieces, infos, projections, place, masked, nslab, slots, padded, ngrid)
    return out[:rows].reshape(nblock, band_local, ngrid)


def solution(mesh):
    in_specs = (P(None, ("band", "slab"), None), P("slab", None), P("slab"), P("slab"), P(), P())
    out_specs = P(None, ("band", "slab"), None)
    return jax.shard_map(body, mesh=mesh, in_specs=in_specs, out_specs=out_specs, check_vma=False)
```

```python
import collections
import functools
import math

import jax
import jax.numpy as jnp
import numpy as np
from jax import lax
from jax.experimental import pallas as pl
from jax.experimental.pallas import tpu as pltpu
from jax.sharding import PartitionSpec as P

BOXPTS = 64
GROUP = 16
INFO = 8
UNROLL = 8
AXES = ("band", "slab")
MIB = 1 << 20


def round_up(value, step):
    return (value + step - 1) // step * step


def cycle_tables(nslab):
    order = list(range(0, nslab, 2)) + list(range(nslab - 1 - nslab % 2, 0, -2))
    place = {s: i for i, s in enumerate(order)}
    return order, place


def params(limit):
    return pltpu.CompilerParams(vmem_limit_bytes=limit)


VMEM = pl.BlockSpec(memory_space=pltpu.VMEM)
SMEM = pl.BlockSpec(memory_space=pltpu.SMEM)
ANY = pl.BlockSpec(memory_space=pl.ANY)


def split_bands_kernel(atom_dev, x_ref, coupling_ref, channels_ref, out_ref, masked_ref, whole):
    @pl.when(pl.program_id(0) == 0)
    def _():
        channel = channels_ref.shape[0]
        natoms = channels_ref.shape[1]
        number = lax.broadcasted_iota(jnp.int32, (channel, natoms), 0)
        mask = jnp.where(number < channels_ref[...], 1.0, 0.0)
        for c in range(channel):
            own = slice(c * channel, (c + 1) * channel)
            whole[own, :] = coupling_ref[own, :] * mask * mask[c : c + 1, :]
        lanes = masked_ref.shape[2]
        for slab in range(masked_ref.shape[0]):
            base = slab * atom_dev // 128 * 128
            part = whole[:, base : min(base + lanes + 128, natoms)]
            if part.shape[1] < lanes:
                part = jnp.concatenate([part, part[:, : lanes - part.shape[1]]], axis=1)
            if slab * atom_dev != base:
                part = pltpu.roll(part, part.shape[1] - (slab * atom_dev - base), 1)
            masked_ref[slab] = part[:, :lanes]

    rows = x_ref.shape[0]
    low_half = lax.broadcasted_iota(jnp.int32, (rows, 128), 1) < BOXPTS
    zero = jnp.zeros((rows, 128), jnp.float32)

    def step(pair, carry):
        x = x_ref[:, pl.ds(pl.multiple_of(pair * 128, 128), 128)]
        high = x.astype(jnp.bfloat16).astype(jnp.float32)
        low = x - high
        high_turned = pltpu.roll(high, BOXPTS, 1)
        low_turned = pltpu.roll(low, BOXPTS, 1)
        out_ref[2 * pair, :, 0:128] = jnp.where(low_half, high, high_turned).astype(jnp.bfloat16)
        out_ref[2 * pair, :, 128:256] = jnp.where(low_half, low, zero).astype(jnp.bfloat16)
        out_ref[2 * pair + 1, :, 0:128] = jnp.where(low_half, high_turned, high).astype(jnp.bfloat16)
        out_ref[2 * pair + 1, :, 128:256] = jnp.where(low_half, low_turned, zero).astype(jnp.bfloat16)
        return carry

    lax.fori_loop(0, x_ref.shape[1] // 128, step, 0, unroll=4)


def split_bands(x, coupling, channels, nslab, lanes):
    rows, ngrid = x.shape
    channel, natoms = coupling.shape[1:]
    span = ngrid // nslab
    boxes = span // BOXPTS
    return pl.pallas_call(
        functools.partial(split_bands_kernel, natoms // nslab),
        grid=(nslab,),
        out_shape=[
            jax.ShapeDtypeStruct((ngrid // BOXPTS, rows, 256), jnp.bfloat16),
            jax.ShapeDtypeStruct((nslab, channel * channel, lanes), jnp.float32),
        ],
        in_specs=[
            pl.BlockSpec((rows, span), lambda i: (0, i)),
            pl.BlockSpec((channel * channel, natoms), lambda i: (0, 0)),
            pl.BlockSpec((channel, natoms), lambda i: (0, 0)),
        ],
        out_specs=[
            pl.BlockSpec((boxes, rows, 256), lambda i: (i, 0, 0)),
            pl.BlockSpec((nslab, channel * channel, lanes), lambda i: (0, 0, 0)),
        ],
        scratch_shapes=[pltpu.VMEM((channel * channel, natoms), jnp.float32)],
        compiler_params=params(16 * MIB),
        cost_estimate=pl.CostEstimate(
            flops=8 * x.size, bytes_accessed=12 * x.size, transcendentals=0
        ),
        name="split_bands",
    )(
        pltpu.with_memory_space_constraint(x, pltpu.HBM),
        coupling.reshape(channel * channel, natoms),
        jnp.broadcast_to(channels[None, :], (channel, natoms)),
    )


def slot_weights(values, low_half, axis):
    full, top = [], []
    for t in range(values.shape[1] // 128):
        x = values[:, t * 128 : (t + 1) * 128]
        high = x.astype(jnp.bfloat16).astype(jnp.float32)
        low = x - high
        turned = pltpu.roll(high, BOXPTS, 1)
        full.append(jnp.where(low_half, high, pltpu.roll(low, BOXPTS, 1)).astype(jnp.bfloat16))
        full.append(jnp.where(low_half, turned, low).astype(jnp.bfloat16))
        top.append(jnp.where(low_half, high, 0.0).astype(jnp.bfloat16))
        top.append(jnp.where(low_half, turned, 0.0).astype(jnp.bfloat16))
    return jnp.concatenate(
        [jnp.concatenate(full, axis=0), jnp.concatenate(top, axis=0)], axis=axis
    )


def live_groups(live, start, length):
    return lax.div(jnp.clip(live - start, 0, length) + (GROUP - 1), GROUP)


def begin_kernel(
    natoms, lanes, atom_ref, box_ref, projector_ref, info_ref, first_ref, second_ref, sem
):
    nslab = lax.axis_size("slab")
    count = second_ref.shape[0]
    start = lax.rem(lax.axis_index("band"), 2) * (2 * count)
    copies = []
    for k, out in enumerate((first_ref.at[pl.ds(INFO, count), :], second_ref)):
        rows = pl.ds(pl.multiple_of(start + k * count, GROUP), count)
        copies.append(pltpu.make_async_copy(projector_ref.at[rows, :], out, sem.at[k]))
        copies[-1].start()
    atom_dev = natoms // nslab
    below = lax.rem(lax.axis_index("slab") + nslab - 1, nslab) * atom_dev
    atom = atom_ref[...]
    slots = atom.shape[1]
    relative = atom - below
    relative = jnp.where(relative < 0, relative + natoms, relative)
    column = jnp.where(relative < atom_dev, relative, relative + (lanes - atom_dev))
    live = jnp.sum(jnp.where(atom >= 0, 1.0, 0.0), axis=1, keepdims=True)
    info_ref[...] = jnp.zeros(info_ref.shape, jnp.float32)
    info_ref[0:1, 0:slots] = box_ref[...].astype(jnp.float32)
    info_ref[1:2, 0:slots] = jnp.broadcast_to(live, (1, slots))
    info_ref[2:3, 0:slots] = jnp.where(atom >= 0, column, -1).astype(jnp.float32)
    head = pltpu.make_async_copy(info_ref, first_ref.at[pl.ds(0, INFO), :], sem.at[2])
    head.start()
    head.wait()
    for c in copies:
        c.wait()


def begin(slot_atom, slot_box, projectors, natoms, lanes):
    slots, depth = projectors.shape
    return pl.pallas_call(
        functools.partial(begin_kernel, natoms, lanes),
        out_shape=[
            jax.ShapeDtypeStruct((INFO, depth), jnp.float32),
            jax.ShapeDtypeStruct((INFO + slots // 4, depth), jnp.float32),
            jax.ShapeDtypeStruct((slots // 4, depth), jnp.float32),
        ],
        in_specs=[VMEM, VMEM, ANY],
        out_specs=[VMEM, ANY, ANY],
        scratch_shapes=[pltpu.SemaphoreType.DMA((3,))],
        compiler_params=params(8 * MIB),
        name="begin",
    )(
        slot_atom.reshape(1, slots),
        slot_box.reshape(1, slots),
        pltpu.with_memory_space_constraint(projectors, pltpu.HBM),
    )


def scalar_row(info, first):
    return jnp.concatenate([info[0:1, :] + first, info[1:2, 0:128]], axis=1).astype(jnp.int32)


def in_units(pieces):
    order = sorted({p.unit for p in pieces})
    return [[i for i, p in enumerate(pieces) if p.unit == u] for u in order]


def project_kernel(pieces, infos, place_ref, x_ref, *refs):
    units = in_units(pieces)
    arrays = refs[: -len(units) - 4]
    outs = refs[-len(units) - 4 : -4]
    whole, proj, table, sem = refs[-4:]
    for k, index in enumerate(infos):
        whole[k : k + 1, :] = scalar_row(arrays[index][0:INFO, :], 0)
    copy = pltpu.make_async_copy(whole, table, sem)
    copy.start()
    rows = x_ref.shape[1]
    slots = arrays[infos[0]].shape[1]
    width = proj.shape[3]
    chunk = width // GROUP
    lane_block = lax.broadcasted_iota(jnp.int32, (rows, width), 1) // GROUP
    low_half = lax.broadcasted_iota(jnp.int32, (GROUP, 128), 1) < BOXPTS
    lane_slot = lax.broadcasted_iota(jnp.int32, (rows, width), 1) % GROUP
    proj[...] = jnp.zeros(proj.shape, jnp.float32)
    copy.wait()
    for which, p in enumerate(pieces):
        array = arrays[p.array]
        start = place_ref[3 * p.index + 1]
        box_base = place_ref[3 * p.index + 2]
        info = infos.index(p.info)
        count = live_groups(table[info, slots], start, p.rows)

        def step(block, carry):
            groups = [block * UNROLL + u for u in range(UNROLL)]
            weights, patches = [], []
            for g in groups:
                first = pl.multiple_of(p.offset + g * GROUP, 8)
                weights.append(slot_weights(array[pl.ds(first, GROUP), :], low_half, 1))
                boxes = [table[info, start + g * GROUP + s] for s in range(GROUP)]
                patches.append(jnp.concatenate([x_ref[box_base + b] for b in boxes], axis=0))
            totals = []
            for w, p_ in zip(weights, patches):
                product = lax.dot_general(
                    p_, w, (((1,), (1,)), ((), ())), preferred_element_type=jnp.float32
                )
                total = product[0:rows]
                for s in range(1, GROUP):
                    total = jnp.where(lane_slot == s, product[s * rows : (s + 1) * rows], total)
                totals.append(total)
            for g, total in zip(groups, totals):
                proj[which, g] = total
            return carry

        lax.fori_loop(0, lax.div(count + (UNROLL - 1), UNROLL), step, 0)

    for unit, out in zip(units, outs):
        head = pieces[unit[0]]
        start = place_ref[3 * head.index + 1]
        columns = arrays[head.info][2:3, :]
        columns = pltpu.roll(columns, lax.rem(columns.shape[1] - start, columns.shape[1]), 1)
        tiles = [proj[i, g] for i in unit for g in range(pieces[i].rows // GROUP)]
        nchunk = len(tiles) // chunk
        value = jnp.concatenate(
            [
                jnp.concatenate(
                    swap_blocks(tiles[k * chunk : (k + 1) * chunk], lane_block, width), axis=0
                )
                for k in range(nchunk)
            ],
            axis=1,
        )
        both = lax.dot_general(
            stacked_split(value),
            selector(columns[:, : nchunk * width], out.shape[1]),
            (((1,), (1,)), ((), ())),
            preferred_element_type=jnp.float32,
        )
        half = both.shape[0] // 2
        out[...] = both[:half] + both[half:]


def project(arrays, pieces, place, x, lanes):
    channel = arrays[0].shape[1] // BOXPTS
    used = sorted({p.array for p in pieces} | {p.info for p in pieces})
    local = [
        p._replace(array=used.index(p.array), info=used.index(p.info)) for p in pieces
    ]
    infos = sorted({p.info for p in local})
    units = in_units(pieces)
    shapes = [
        jax.ShapeDtypeStruct((channel * x.shape[1], 2 * lanes), jnp.float32) for _ in units
    ]
    size = sum(p.rows for p in pieces) * arrays[0].shape[1]
    table = (round_up(len(infos), 8), arrays[0].shape[1] + 128)
    groups = round_up(max(p.rows for p in pieces), channel * GROUP) // GROUP
    return pl.pallas_call(
        functools.partial(project_kernel, local, infos),
        out_shape=shapes,
        in_specs=[SMEM, VMEM] + [VMEM] * len(used),
        out_specs=[VMEM] * len(units),
        scratch_shapes=[
            pltpu.VMEM(table, jnp.int32),
            pltpu.VMEM((len(pieces), groups, x.shape[1], channel * GROUP), jnp.float32),
            pltpu.SMEM(table, jnp.int32),
            pltpu.SemaphoreType.DMA(()),
        ],
        compiler_params=params(40 * MIB),
        cost_estimate=pl.CostEstimate(
            flops=2 * 16 * 16 * size, bytes_accessed=4 * size + 2 * x.size, transcendentals=0
        ),
        name="project",
    )(place, x, *[arrays[i] for i in used])


def swap_blocks(tiles, lane_block, width):
    tiles = list(tiles)
    bit = 1
    while bit < len(tiles):
        upper = (lane_block & bit) != 0
        for i in range(len(tiles)):
            if not i & bit:
                a, b = tiles[i], tiles[i | bit]
                tiles[i] = jnp.where(upper, pltpu.roll(b, GROUP * bit, 1), a)
                tiles[i | bit] = jnp.where(upper, b, pltpu.roll(a, width - GROUP * bit, 1))
        bit *= 2
    return tiles


def selector(columns, count):
    shape = (count, columns.shape[1])
    row = lax.broadcasted_iota(jnp.int32, shape, 0).astype(jnp.float32)
    return jnp.where(jnp.broadcast_to(columns, shape) == row, 1.0, 0.0).astype(jnp.bfloat16)


def stacked_split(value):
    high = value.astype(jnp.bfloat16)
    low = (value - high.astype(jnp.float32)).astype(jnp.bfloat16)
    return jnp.concatenate([high, low], axis=0)


def apply_kernel(nslab, slots, nsum, pieces, infos, place_ref, coupling_ref, *refs):
    proj, loaded, parts, beta, done, masks, info, whole, table = refs[-13:-4]
    sums = refs[-13 - nsum : -13]
    beta_sem, proj_sem, info_sem, out_sem = refs[-4:]
    base = len(refs) - 14 - nsum
    units = in_units(pieces)
    nunit = len(units)
    out_ref = refs[base]
    projections = refs[base - nunit : base]
    arrays = refs[: base - nunit]
    groups = slots // GROUP
    rows, width = proj.shape[1], proj.shape[2]
    channel = width // GROUP
    lanes = parts.shape[2] // 2
    boxes = out_ref.shape[1] // BOXPTS // nslab
    chunk = width // GROUP
    info_copies, beta_copies = [], []
    copies = [
        pltpu.make_async_copy(projections[i], loaded.at[i % loaded.shape[0]], proj_sem.at[i])
        for i in range(nunit)
    ]
    for i, (array, index) in enumerate(infos):
        slab = place_ref[3 * index]
        info_copies.append(
            pltpu.make_async_copy(arrays[array].at[0:INFO, :], info.at[slab], info_sem.at[i])
        )
    for i, p in enumerate(pieces):
        slab, start = place_ref[3 * p.index], place_ref[3 * p.index + 1]
        first = pl.multiple_of(slab * slots + start, GROUP)
        beta_copies.append(
            pltpu.make_async_copy(
                arrays[p.array].at[p.offset : p.offset + p.rows, :],
                beta.at[pl.ds(first, p.rows), :],
                beta_sem.at[i],
            )
        )
    for c in info_copies + copies[: loaded.shape[0]] + beta_copies:
        c.start()
    lane_slot = lax.broadcasted_iota(jnp.int32, (rows, width), 1) % GROUP
    for s in range(GROUP):
        masks[s] = jnp.where(lane_slot == s, 1.0, 0.0).astype(jnp.bfloat16)
    for total in sums:
        total[...] = jnp.zeros(total.shape, jnp.float32)
    parts[...] = jnp.zeros(parts.shape, jnp.float32)
    for c in info_copies:
        c.wait()
    for slab in range(nslab):
        whole[slab : slab + 1, :] = scalar_row(info[slab], float(slab * boxes))
    to_scalars = pltpu.make_async_copy(whole, table, info_sem.at[0])
    to_scalars.start()
    for first in range(0, nunit, loaded.shape[0]):
        wave = range(first, min(first + loaded.shape[0], nunit))
        for i in wave:
            if first > 0:
                copies[i].start()
        for i in wave:
            copies[i].wait()
        for i in wave:
            slab = place_ref[3 * pieces[units[i][0]].index]
            parts[slab] = parts[slab] + loaded[i % loaded.shape[0]]

    lane_block = lax.broadcasted_iota(jnp.int32, (rows, width), 1) // GROUP
    def couple(slab, carry):
        following = lax.rem(slab + 1, nslab)
        total = parts[slab, :, lanes:] + parts[following, :, :lanes]
        for c in range(channel):
            mixed = jnp.zeros((rows, lanes), jnp.float32)
            for e in range(channel):
                factor = coupling_ref[slab, pl.ds(c * channel + e, 1), :]
                mixed = mixed + factor * total[e * rows : (e + 1) * rows]
            parts[slab, c * rows : (c + 1) * rows, lanes:] = mixed
        return carry

    lax.fori_loop(0, nslab, couple, 0)

    def spread(slab, carry):
        below = lax.rem(slab + nslab - 1, nslab)
        value = jnp.concatenate([parts[below, :, lanes:], parts[slab, :, lanes:]], axis=1)
        value = stacked_split(value)

        both = jnp.dot(
            value, selector(info[slab, 2:3, 0:slots], 2 * lanes), preferred_element_type=jnp.float32
        )
        half = both.shape[0] // 2
        both = both[:half] + both[half:]
        for k in range(groups // chunk):
            tiles = [
                both[c * rows : (c + 1) * rows, k * width : (k + 1) * width]
                for c in range(channel)
            ]
            for i, tile in enumerate(swap_blocks(tiles, lane_block, width)):
                proj[slab * groups + k * chunk + i] = tile
        return carry

    lax.fori_loop(0, nslab, spread, 0, unroll=4 if nsum > 1 else 1)
    to_scalars.wait()

    for c in beta_copies:
        c.wait()

    low_half = lax.broadcasted_iota(jnp.int32, (GROUP, 128), 1) < BOXPTS
    pair_half = lax.broadcasted_iota(jnp.int32, (rows, 128), 1) < BOXPTS
    span = boxes * BOXPTS

    def leaving(slab):
        slot = lax.rem(slab, 2)
        return pltpu.make_async_copy(
            done.at[slot],
            out_ref.at[:, pl.ds(pl.multiple_of(slab * span, 128), span)],
            out_sem.at[slot],
        )

    def slab_step(slab, carry):
        def step(block, inner):
            products = []
            for u in range(UNROLL):
                g = block * UNROLL + u
                slot_base = pl.multiple_of(slab * slots + g * GROUP, GROUP)
                weights = slot_weights(beta[pl.ds(slot_base, GROUP), :], low_half, 0)
                c = proj[slab * groups + g]
                high = c.astype(jnp.bfloat16)
                low = (c - high.astype(jnp.float32)).astype(jnp.bfloat16)
                left = jnp.concatenate(
                    [
                        jnp.concatenate([high * masks[s], low * masks[s]], axis=1)
                        for s in range(GROUP)
                    ],
                    axis=0,
                )
                products.append((slot_base, jnp.dot(left, weights, preferred_element_type=jnp.float32)))
            for u, (slot_base, product) in enumerate(products):
                for s in range(GROUP):
                    box = table[slab, block * (UNROLL * GROUP) + u * GROUP + s]
                    j = (u * GROUP + s) % nsum
                    sums[j][box] = sums[j][box] + product[s * rows : (s + 1) * rows]
            return inner

        count = live_groups(table[slab, info.shape[2]], 0, slots)
        lax.fori_loop(0, lax.div(count + (UNROLL - 1), UNROLL), step, 0)

        @pl.when(slab >= 2)
        def _():
            leaving(slab - 2).wait()

        def finish(pair, inner):
            folded = []
            for i in range(2):
                box = slab * boxes + 2 * pair + i
                value = sums[0][box]
                for j in range(1, nsum):
                    value = value + sums[j][box]
                folded.append(value + pltpu.roll(value, BOXPTS, 1))
            done[lax.rem(slab, 2), :, pl.ds(pl.multiple_of(pair * 128, 128), 128)] = jnp.where(
                pair_half, folded[0], folded[1]
            )
            return inner

        lax.fori_loop(0, span // 128, finish, 0, unroll=min(32, span // 128))
        leaving(slab).start()
        return carry

    lax.fori_loop(0, nslab, slab_step, 0)
    for slab in range(max(nslab - 2, 0), nslab):
        leaving(slab).wait()


def apply(arrays, pieces, infos, projections, place, coupling, nslab, slots, rows, ngrid):
    width = projections[0].shape[0] // rows * GROUP
    lanes = coupling.shape[2]
    depth = arrays[0].shape[1]
    one_sum = ngrid // BOXPTS * rows * 128 * 4
    nsum = 2 if one_sum <= 8 * MIB else 1
    buffers = [pltpu.VMEM((ngrid // BOXPTS, rows, 128), jnp.float32) for _ in range(nsum)]
    buffers += [
        pltpu.VMEM((nslab * slots // GROUP, rows, width), jnp.float32),
        pltpu.VMEM(
            (len(projections) if len(projections) <= 24 else 1,) + projections[0].shape, jnp.float32
        ),
        pltpu.VMEM((nslab,) + projections[0].shape, jnp.float32),
        pltpu.VMEM((nslab * slots, depth), jnp.float32),
        pltpu.VMEM((2, rows, ngrid // nslab), jnp.float32),
        pltpu.VMEM((GROUP, rows, width), jnp.bfloat16),
        pltpu.VMEM((nslab, INFO, depth), jnp.float32),
        pltpu.VMEM((nslab, depth + 128), jnp.int32),
    ]
    need = sum(math.prod(b.shape) * b.dtype.itemsize for b in buffers)
    scratch = buffers + [
        pltpu.SMEM((nslab, depth + 128), jnp.int32),
        pltpu.SemaphoreType.DMA((len(pieces),)),
        pltpu.SemaphoreType.DMA((len(projections),)),
        pltpu.SemaphoreType.DMA((len(infos),)),
        pltpu.SemaphoreType.DMA((2,)),
    ]
    return pl.pallas_call(
        functools.partial(apply_kernel, nslab, slots, nsum, pieces, infos),
        out_shape=jax.ShapeDtypeStruct((rows, ngrid), jnp.float32),
        in_specs=[SMEM, VMEM] + [ANY] * (len(arrays) + len(projections)),
        out_specs=ANY,
        scratch_shapes=scratch,
        compiler_params=params(min(need + 4 * MIB, 63 * MIB)),
        name="apply",
    )(place, coupling, *arrays, *projections)


Piece = collections.namedtuple("Piece", ["array", "offset", "rows", "info", "index", "unit"])


def gather_and_project(projectors, described, first, second, split, lanes, nband, nslab):
    slots = projectors.shape[0]
    order, at = cycle_tables(nslab)
    half = slots // 2
    quarter = half // 2
    reach = nslab // 2
    onward = [
        (b * nslab + order[i], b * nslab + order[(i + 1) % nslab])
        for b in range(nband)
        for i in range(nslab)
    ]
    backward = [(d, s) for s, d in onward]
    sibling = [(b * nslab + s, (b ^ 1) * nslab + s) for b in range(nband) for s in range(nslab)]

    where = [(0, 0, None)]
    for step in range(1, reach + 1):
        for distance, other in ((1 - step, True), (step - 1, True), (-step, False), (step, False)):
            if distance != 0 and distance != reach:
                where += [(distance, 0, other), (distance, quarter, other)]
    where += [(reach, 0, True), (reach, quarter, True)]
    boxes = split.shape[0] // nslab

    def entry(core, slab, distance, start, other):
        there = order[(at[slab] + distance) % nslab]
        if other is not None:
            start += half * ((1 - core) if other else core)
        return there, start, there * boxes

    table = [[entry(b % 2, s, *w) for w in where] for b in range(nband) for s in range(nslab)]
    me = lax.axis_index("band") * nslab + lax.axis_index("slab")
    place = lax.dynamic_index_in_dim(
        jnp.asarray(np.array(table, np.int32)), me, 0, keepdims=False
    ).reshape(-1)

    arrays, pieces, infos, projections = [described, projectors], [], [(0, 0)], []

    pieces.append(Piece(1, 0, slots, 0, 0, 0))
    units = 1

    def add(one, two):
        nonlocal units
        arrays.extend([one, two])
        index, info = len(pieces), len(arrays) - 2
        pieces.append(Piece(info, INFO, one.shape[0] - INFO, info, index, units))
        pieces.append(Piece(info + 1, 0, two.shape[0], info, index + 1, units))
        units += 1
        return info, index

    done = 0

    def project_new():
        nonlocal done
        projections.extend(project(arrays, pieces[done:], place, split, lanes))
        done = len(pieces)

    near = []
    up, down = (first, second), (first, second)
    for step in range(reach + 1):
        for pair in near:
            add(*pair)
        if step == 0:
            near = []
        elif step < reach:
            infos.extend([add(*up), add(*down)])
            near = [up, down]
        else:
            infos.append(add(up[0], down[1]))
            near = [(up[0], down[1])]
        near = [tuple(lax.ppermute(x, AXES, sibling) for x in pair) for pair in near]
        if step + 1 < reach:
            ahead = [lax.ppermute(x, AXES, onward) for x in up]
            ahead += [lax.ppermute(x, AXES, backward) for x in down]
        elif step + 1 == reach:
            ahead = [lax.ppermute(up[0], AXES, onward), lax.ppermute(down[1], AXES, backward)]
        else:
            ahead = []
        project_new()
        if step + 1 < reach:
            ones, projections = lax.optimization_barrier((ahead[0::2], projections))
            twos, near, projections = lax.optimization_barrier((ahead[1::2], near, projections))
            up, down = (ones[0], twos[0]), (ones[1], twos[1])
        elif step + 1 == reach:
            ahead, near, projections = lax.optimization_barrier((ahead, near, projections))
            up, down = (ahead[0], None), (None, ahead[1])
        projections = list(projections)
    for pair in near:
        add(*pair)
    project_new()
    return arrays, pieces, infos, projections, place


def body(bands, projectors, slot_atom, slot_box, channels, coupling):
    nblock, band_local, ngrid = bands.shape
    nband, nslab = lax.axis_size("band"), lax.axis_size("slab")
    natoms = channels.shape[0]
    atom_dev = natoms // nslab
    slots = slot_atom.shape[0]
    lanes = round_up(atom_dev, 128)

    described, first, second = begin(slot_atom, slot_box, projectors, natoms, lanes)
    rows = nblock * band_local
    padded = round_up(rows, GROUP)
    x = bands.reshape(rows, ngrid)
    if padded != rows:
        x = jnp.pad(x, ((0, padded - rows), (0, 0)))
    split, masked = split_bands(x, coupling, channels, nslab, lanes)
    arrays, pieces, infos, projections, place = gather_and_project(
        projectors, described, first, second, split, lanes, nband, nslab
    )
    out = apply(arrays, pieces, infos, projections, place, masked, nslab, slots, padded, ngrid)
    return out[:rows].reshape(nblock, band_local, ngrid)


def solution(mesh):
    in_specs = (P(None, ("band", "slab"), None), P("slab", None), P("slab"), P("slab"), P(), P())
    out_specs = P(None, ("band", "slab"), None)
    return jax.shard_map(body, mesh=mesh, in_specs=in_specs, out_specs=out_specs, check_vma=False)
```

```python
import collections
import functools
import math

import jax
import jax.numpy as jnp
import numpy as np
from jax import lax
from jax.experimental import pallas as pl
from jax.experimental.pallas import tpu as pltpu
from jax.sharding import PartitionSpec as P

BOXPTS = 64
GROUP = 16
INFO = 8
UNROLL = 8
AXES = ("band", "slab")
MIB = 1 << 20


def round_up(value, step):
    return (value + step - 1) // step * step


def cycle_tables(nslab):
    order = list(range(0, nslab, 2)) + list(range(nslab - 1 - nslab % 2, 0, -2))
    place = {s: i for i, s in enumerate(order)}
    return order, place


def params(limit):
    return pltpu.CompilerParams(vmem_limit_bytes=limit)


VMEM = pl.BlockSpec(memory_space=pltpu.VMEM)
SMEM = pl.BlockSpec(memory_space=pltpu.SMEM)
ANY = pl.BlockSpec(memory_space=pl.ANY)


def split_bands_kernel(atom_dev, x_ref, coupling_ref, channels_ref, out_ref, masked_ref, whole):
    @pl.when(pl.program_id(0) == 0)
    def _():
        channel = channels_ref.shape[0]
        natoms = channels_ref.shape[1]
        number = lax.broadcasted_iota(jnp.int32, (channel, natoms), 0)
        mask = jnp.where(number < channels_ref[...], 1.0, 0.0)
        for c in range(channel):
            own = slice(c * channel, (c + 1) * channel)
            whole[own, :] = coupling_ref[own, :] * mask * mask[c : c + 1, :]
        lanes = masked_ref.shape[2]
        for slab in range(masked_ref.shape[0]):
            base = slab * atom_dev // 128 * 128
            part = whole[:, base : min(base + lanes + 128, natoms)]
            if part.shape[1] < lanes:
                part = jnp.concatenate([part, part[:, : lanes - part.shape[1]]], axis=1)
            if slab * atom_dev != base:
                part = pltpu.roll(part, part.shape[1] - (slab * atom_dev - base), 1)
            masked_ref[slab] = part[:, :lanes]

    rows = x_ref.shape[0]
    low_half = lax.broadcasted_iota(jnp.int32, (rows, 128), 1) < BOXPTS
    zero = jnp.zeros((rows, 128), jnp.float32)

    def step(pair, carry):
        x = x_ref[:, pl.ds(pl.multiple_of(pair * 128, 128), 128)]
        high = x.astype(jnp.bfloat16).astype(jnp.float32)
        low = x - high
        high_turned = pltpu.roll(high, BOXPTS, 1)
        low_turned = pltpu.roll(low, BOXPTS, 1)
        out_ref[2 * pair, :, 0:128] = jnp.where(low_half, high, high_turned).astype(jnp.bfloat16)
        out_ref[2 * pair, :, 128:256] = jnp.where(low_half, low, zero).astype(jnp.bfloat16)
        out_ref[2 * pair + 1, :, 0:128] = jnp.where(low_half, high_turned, high).astype(jnp.bfloat16)
        out_ref[2 * pair + 1, :, 128:256] = jnp.where(low_half, low_turned, zero).astype(jnp.bfloat16)
        return carry

    lax.fori_loop(0, x_ref.shape[1] // 128, step, 0, unroll=4)


def split_bands(x, coupling, channels, nslab, lanes):
    rows, ngrid = x.shape
    channel, natoms = coupling.shape[1:]
    span = ngrid // nslab
    boxes = span // BOXPTS
    return pl.pallas_call(
        functools.partial(split_bands_kernel, natoms // nslab),
        grid=(nslab,),
        out_shape=[
            jax.ShapeDtypeStruct((ngrid // BOXPTS, rows, 256), jnp.bfloat16),
            jax.ShapeDtypeStruct((nslab, channel * channel, lanes), jnp.float32),
        ],
        in_specs=[
            pl.BlockSpec((rows, span), lambda i: (0, i)),
            pl.BlockSpec((channel * channel, natoms), lambda i: (0, 0)),
            pl.BlockSpec((channel, natoms), lambda i: (0, 0)),
        ],
        out_specs=[
            pl.BlockSpec((boxes, rows, 256), lambda i: (i, 0, 0)),
            pl.BlockSpec((nslab, channel * channel, lanes), lambda i: (0, 0, 0)),
        ],
        scratch_shapes=[pltpu.VMEM((channel * channel, natoms), jnp.float32)],
        compiler_params=params(16 * MIB),
        cost_estimate=pl.CostEstimate(
            flops=8 * x.size, bytes_accessed=12 * x.size, transcendentals=0
        ),
        name="split_bands",
    )(
        pltpu.with_memory_space_constraint(x, pltpu.HBM),
        coupling.reshape(channel * channel, natoms),
        jnp.broadcast_to(channels[None, :], (channel, natoms)),
    )


def slot_weights(values, low_half, axis):
    full, top = [], []
    for t in range(values.shape[1] // 128):
        x = values[:, t * 128 : (t + 1) * 128]
        high = x.astype(jnp.bfloat16).astype(jnp.float32)
        low = x - high
        turned = pltpu.roll(high, BOXPTS, 1)
        full.append(jnp.where(low_half, high, pltpu.roll(low, BOXPTS, 1)).astype(jnp.bfloat16))
        full.append(jnp.where(low_half, turned, low).astype(jnp.bfloat16))
        top.append(jnp.where(low_half, high, 0.0).astype(jnp.bfloat16))
        top.append(jnp.where(low_half, turned, 0.0).astype(jnp.bfloat16))
    return jnp.concatenate(
        [jnp.concatenate(full, axis=0), jnp.concatenate(top, axis=0)], axis=axis
    )


def live_groups(live, start, length):
    return lax.div(jnp.clip(live - start, 0, length) + (GROUP - 1), GROUP)


def begin_kernel(
    natoms, lanes, atom_hbm, box_hbm, projector_ref, info_ref, mine_ref, atom_ref, box_ref, sem
):
    reads = [
        pltpu.make_async_copy(atom_hbm, atom_ref, sem.at[0]),
        pltpu.make_async_copy(box_hbm, box_ref, sem.at[1]),
    ]
    for c in reads:
        c.start()
    nslab = lax.axis_size("slab")
    half = mine_ref.shape[0] - INFO
    core = lax.rem(lax.axis_index("band"), 2)
    copy = pltpu.make_async_copy(
        projector_ref.at[pl.ds(pl.multiple_of(core * half, GROUP), half), :],
        mine_ref.at[pl.ds(INFO, half), :],
        sem.at[2],
    )
    copy.start()
    for c in reads:
        c.wait()
    atom_dev = natoms // nslab
    below = lax.rem(lax.axis_index("slab") + nslab - 1, nslab) * atom_dev
    atom = atom_ref[...]
    slots = atom.shape[1]
    relative = atom - below
    relative = jnp.where(relative < 0, relative + natoms, relative)
    column = jnp.where(relative < atom_dev, relative, relative + (lanes - atom_dev))
    live = jnp.sum(jnp.where(atom >= 0, 1.0, 0.0), axis=1, keepdims=True)
    info_ref[...] = jnp.zeros(info_ref.shape, jnp.float32)
    info_ref[0:1, 0:slots] = box_ref[...].astype(jnp.float32)
    info_ref[1:2, 0:slots] = jnp.broadcast_to(live, (1, slots))
    info_ref[2:3, 0:slots] = jnp.where(atom >= 0, column, -1).astype(jnp.float32)
    head = pltpu.make_async_copy(info_ref, mine_ref.at[pl.ds(0, INFO), :], sem.at[0])
    head.start()
    head.wait()
    copy.wait()


def begin(slot_atom, slot_box, projectors, natoms, lanes):
    slots, depth = projectors.shape
    return pl.pallas_call(
        functools.partial(begin_kernel, natoms, lanes),
        out_shape=[
            jax.ShapeDtypeStruct((INFO, depth), jnp.float32),
            jax.ShapeDtypeStruct((INFO + slots // 2, depth), jnp.float32),
        ],
        in_specs=[ANY, ANY, ANY],
        out_specs=[VMEM, ANY],
        scratch_shapes=[
            pltpu.VMEM((1, slots), jnp.int32),
            pltpu.VMEM((1, slots), jnp.int32),
            pltpu.SemaphoreType.DMA((3,)),
        ],
        compiler_params=params(8 * MIB),
        name="begin",
    )(
        pltpu.with_memory_space_constraint(slot_atom.reshape(1, slots), pltpu.HBM),
        pltpu.with_memory_space_constraint(slot_box.reshape(1, slots), pltpu.HBM),
        pltpu.with_memory_space_constraint(projectors, pltpu.HBM),
    )


def scalar_row(info, first):
    return jnp.concatenate([info[0:1, :] + first, info[1:2, 0:128]], axis=1).astype(jnp.int32)


def project_kernel(pieces, infos, place_ref, x_ref, *refs):
    arrays = refs[: -len(pieces) - 4]
    outs = refs[-len(pieces) - 4 : -4]
    whole, proj, table, sem = refs[-4:]
    for k, index in enumerate(infos):
        whole[k : k + 1, :] = scalar_row(arrays[index][0:INFO, :], 0)
    copy = pltpu.make_async_copy(whole, table, sem)
    copy.start()
    rows = x_ref.shape[1]
    slots = arrays[infos[0]].shape[1]
    width = proj.shape[3]
    chunk = width // GROUP
    lane_block = lax.broadcasted_iota(jnp.int32, (rows, width), 1) // GROUP
    low_half = lax.broadcasted_iota(jnp.int32, (GROUP, 128), 1) < BOXPTS
    lane_slot = lax.broadcasted_iota(jnp.int32, (rows, width), 1) % GROUP
    proj[...] = jnp.zeros(proj.shape, jnp.float32)
    copy.wait()
    for which, p in enumerate(pieces):
        array = arrays[p.array]
        start = place_ref[3 * p.index + 1]
        box_base = place_ref[3 * p.index + 2]
        info = infos.index(p.info)
        count = live_groups(table[info, slots], start, p.rows)

        def step(block, carry):
            groups = [block * UNROLL + u for u in range(UNROLL)]
            weights, patches = [], []
            for g in groups:
                first = pl.multiple_of(p.offset + g * GROUP, 8)
                weights.append(slot_weights(array[pl.ds(first, GROUP), :], low_half, 1))
                boxes = [table[info, start + g * GROUP + s] for s in range(GROUP)]
                patches.append(jnp.concatenate([x_ref[box_base + b] for b in boxes], axis=0))
            totals = []
            for w, p_ in zip(weights, patches):
                product = lax.dot_general(
                    p_, w, (((1,), (1,)), ((), ())), preferred_element_type=jnp.float32
                )
                total = product[0:rows]
                for s in range(1, GROUP):
                    total = jnp.where(lane_slot == s, product[s * rows : (s + 1) * rows], total)
                totals.append(total)
            for g, total in zip(groups, totals):
                proj[which, g] = total
            return carry

        lax.fori_loop(0, lax.div(count + (UNROLL - 1), UNROLL), step, 0)

    for which, (p, out) in enumerate(zip(pieces, outs)):
        start = place_ref[3 * p.index + 1]
        columns = arrays[p.info][2:3, :]
        columns = pltpu.roll(columns, lax.rem(columns.shape[1] - start, columns.shape[1]), 1)
        nchunk = (p.rows // GROUP + chunk - 1) // chunk
        value = jnp.concatenate(
            [
                jnp.concatenate(
                    swap_blocks(
                        [proj[which, k * chunk + i] for i in range(chunk)], lane_block, width
                    ),
                    axis=0,
                )
                for k in range(nchunk)
            ],
            axis=1,
        )
        both = lax.dot_general(
            stacked_split(value),
            selector(columns[:, : nchunk * width], out.shape[1]),
            (((1,), (1,)), ((), ())),
            preferred_element_type=jnp.float32,
        )
        half = both.shape[0] // 2
        out[...] = both[:half] + both[half:]


def project(arrays, pieces, place, x, lanes):
    channel = arrays[0].shape[1] // BOXPTS
    used = sorted({p.array for p in pieces} | {p.info for p in pieces})
    local = [
        p._replace(array=used.index(p.array), info=used.index(p.info)) for p in pieces
    ]
    infos = sorted({p.info for p in local})
    shapes = [
        jax.ShapeDtypeStruct((channel * x.shape[1], 2 * lanes), jnp.float32) for p in pieces
    ]
    size = sum(p.rows for p in pieces) * arrays[0].shape[1]
    table = (round_up(len(infos), 8), arrays[0].shape[1] + 128)
    groups = round_up(max(p.rows for p in pieces), channel * GROUP) // GROUP
    return pl.pallas_call(
        functools.partial(project_kernel, local, infos),
        out_shape=shapes,
        in_specs=[SMEM, VMEM] + [VMEM] * len(used),
        out_specs=[VMEM] * len(pieces),
        scratch_shapes=[
            pltpu.VMEM(table, jnp.int32),
            pltpu.VMEM((len(pieces), groups, x.shape[1], channel * GROUP), jnp.float32),
            pltpu.SMEM(table, jnp.int32),
            pltpu.SemaphoreType.DMA(()),
        ],
        compiler_params=params(40 * MIB),
        cost_estimate=pl.CostEstimate(
            flops=2 * 16 * 16 * size, bytes_accessed=4 * size + 2 * x.size, transcendentals=0
        ),
        name="project",
    )(place, x, *[arrays[i] for i in used])


def swap_blocks(tiles, lane_block, width):
    tiles = list(tiles)
    bit = 1
    while bit < len(tiles):
        upper = (lane_block & bit) != 0
        for i in range(len(tiles)):
            if not i & bit:
                a, b = tiles[i], tiles[i | bit]
                tiles[i] = jnp.where(upper, pltpu.roll(b, GROUP * bit, 1), a)
                tiles[i | bit] = jnp.where(upper, b, pltpu.roll(a, width - GROUP * bit, 1))
        bit *= 2
    return tiles


def selector(columns, count):
    shape = (count, columns.shape[1])
    row = lax.broadcasted_iota(jnp.int32, shape, 0).astype(jnp.float32)
    return jnp.where(jnp.broadcast_to(columns, shape) == row, 1.0, 0.0).astype(jnp.bfloat16)


def stacked_split(value):
    high = value.astype(jnp.bfloat16)
    low = (value - high.astype(jnp.float32)).astype(jnp.bfloat16)
    return jnp.concatenate([high, low], axis=0)


def apply_kernel(nslab, slots, nsum, pieces, infos, place_ref, coupling_ref, *refs):
    npiece = len(pieces)
    proj, loaded, parts, beta, done, masks, info, whole, table = refs[-13:-4]
    sums = refs[-13 - nsum : -13]
    beta_sem, proj_sem, info_sem, out_sem = refs[-4:]
    base = len(refs) - 14 - nsum
    out_ref = refs[base]
    projections = refs[base - npiece : base]
    arrays = refs[: base - npiece]
    groups = slots // GROUP
    rows, width = proj.shape[1], proj.shape[2]
    channel = width // GROUP
    lanes = parts.shape[2] // 2
    boxes = out_ref.shape[1] // BOXPTS // nslab
    chunk = width // GROUP
    info_copies, copies, beta_copies = [], [], []
    for i, (array, index) in enumerate(infos):
        slab = place_ref[3 * index]
        info_copies.append(
            pltpu.make_async_copy(arrays[array].at[0:INFO, :], info.at[slab], info_sem.at[i])
        )
    for i, p in enumerate(pieces):
        slab, start = place_ref[3 * p.index], place_ref[3 * p.index + 1]
        j = i % loaded.shape[0]
        copies.append(
            pltpu.make_async_copy(projections[i], loaded.at[j], proj_sem.at[i])
        )
        first = pl.multiple_of(slab * slots + start, GROUP)
        beta_copies.append(
            pltpu.make_async_copy(
                arrays[p.array].at[p.offset : p.offset + p.rows, :],
                beta.at[pl.ds(first, p.rows), :],
                beta_sem.at[i],
            )
        )
    for c in info_copies + copies[: loaded.shape[0]]:
        c.start()
    lane_slot = lax.broadcasted_iota(jnp.int32, (rows, width), 1) % GROUP
    for s in range(GROUP):
        masks[s] = jnp.where(lane_slot == s, 1.0, 0.0).astype(jnp.bfloat16)
    for total in sums:
        total[...] = jnp.zeros(total.shape, jnp.float32)
    parts[...] = jnp.zeros(parts.shape, jnp.float32)
    for c in info_copies:
        c.wait()
    for slab in range(nslab):
        whole[slab : slab + 1, :] = scalar_row(info[slab], float(slab * boxes))
    to_scalars = pltpu.make_async_copy(whole, table, info_sem.at[0])
    to_scalars.start()
    for first in range(0, npiece, loaded.shape[0]):
        wave = range(first, min(first + loaded.shape[0], npiece))
        for i in wave:
            if first > 0:
                copies[i].start()
        for i in wave:
            copies[i].wait()
        for i in wave:
            slab = place_ref[3 * pieces[i].index]
            parts[slab] = parts[slab] + loaded[i % loaded.shape[0]]

    lane_block = lax.broadcasted_iota(jnp.int32, (rows, width), 1) // GROUP
    for c in beta_copies:
        c.start()

    def couple(slab, carry):
        following = lax.rem(slab + 1, nslab)
        total = parts[slab, :, lanes:] + parts[following, :, :lanes]
        for c in range(channel):
            mixed = jnp.zeros((rows, lanes), jnp.float32)
            for e in range(channel):
                factor = coupling_ref[slab, pl.ds(c * channel + e, 1), :]
                mixed = mixed + factor * total[e * rows : (e + 1) * rows]
            parts[slab, c * rows : (c + 1) * rows, lanes:] = mixed
        return carry

    lax.fori_loop(0, nslab, couple, 0)

    def spread(slab, carry):
        below = lax.rem(slab + nslab - 1, nslab)
        value = jnp.concatenate([parts[below, :, lanes:], parts[slab, :, lanes:]], axis=1)
        value = stacked_split(value)

        both = jnp.dot(
            value, selector(info[slab, 2:3, 0:slots], 2 * lanes), preferred_element_type=jnp.float32
        )
        half = both.shape[0] // 2
        both = both[:half] + both[half:]
        for k in range(groups // chunk):
            tiles = [
                both[c * rows : (c + 1) * rows, k * width : (k + 1) * width]
                for c in range(channel)
            ]
            for i, tile in enumerate(swap_blocks(tiles, lane_block, width)):
                proj[slab * groups + k * chunk + i] = tile
        return carry

    lax.fori_loop(0, nslab, spread, 0, unroll=4 if nsum > 1 else 1)
    to_scalars.wait()

    for c in beta_copies:
        c.wait()

    low_half = lax.broadcasted_iota(jnp.int32, (GROUP, 128), 1) < BOXPTS
    pair_half = lax.broadcasted_iota(jnp.int32, (rows, 128), 1) < BOXPTS
    span = boxes * BOXPTS

    def leaving(slab):
        slot = lax.rem(slab, 2)
        return pltpu.make_async_copy(
            done.at[slot],
            out_ref.at[:, pl.ds(pl.multiple_of(slab * span, 128), span)],
            out_sem.at[slot],
        )

    def slab_step(slab, carry):
        def step(block, inner):
            products = []
            for u in range(UNROLL):
                g = block * UNROLL + u
                slot_base = pl.multiple_of(slab * slots + g * GROUP, GROUP)
                weights = slot_weights(beta[pl.ds(slot_base, GROUP), :], low_half, 0)
                c = proj[slab * groups + g]
                high = c.astype(jnp.bfloat16)
                low = (c - high.astype(jnp.float32)).astype(jnp.bfloat16)
                left = jnp.concatenate(
                    [
                        jnp.concatenate([high * masks[s], low * masks[s]], axis=1)
                        for s in range(GROUP)
                    ],
                    axis=0,
                )
                products.append((slot_base, jnp.dot(left, weights, preferred_element_type=jnp.float32)))
            for u, (slot_base, product) in enumerate(products):
                for s in range(GROUP):
                    box = table[slab, block * (UNROLL * GROUP) + u * GROUP + s]
                    j = (u * GROUP + s) % nsum
                    sums[j][box] = sums[j][box] + product[s * rows : (s + 1) * rows]
            return inner

        count = live_groups(table[slab, info.shape[2]], 0, slots)
        lax.fori_loop(0, lax.div(count + (UNROLL - 1), UNROLL), step, 0)

        @pl.when(slab >= 2)
        def _():
            leaving(slab - 2).wait()

        def finish(pair, inner):
            folded = []
            for i in range(2):
                box = slab * boxes + 2 * pair + i
                value = sums[0][box]
                for j in range(1, nsum):
                    value = value + sums[j][box]
                folded.append(value + pltpu.roll(value, BOXPTS, 1))
            done[lax.rem(slab, 2), :, pl.ds(pl.multiple_of(pair * 128, 128), 128)] = jnp.where(
                pair_half, folded[0], folded[1]
            )
            return inner

        lax.fori_loop(0, span // 128, finish, 0, unroll=min(32, span // 128))
        leaving(slab).start()
        return carry

    lax.fori_loop(0, nslab, slab_step, 0)
    for slab in range(max(nslab - 2, 0), nslab):
        leaving(slab).wait()


def apply(arrays, pieces, infos, projections, place, coupling, nslab, slots, rows, ngrid):
    width = projections[0].shape[0] // rows * GROUP
    lanes = coupling.shape[2]
    depth = arrays[0].shape[1]
    one_sum = ngrid // BOXPTS * rows * 128 * 4
    nsum = 2 if one_sum <= 8 * MIB else 1
    buffers = [pltpu.VMEM((ngrid // BOXPTS, rows, 128), jnp.float32) for _ in range(nsum)]
    buffers += [
        pltpu.VMEM((nslab * slots // GROUP, rows, width), jnp.float32),
        pltpu.VMEM((len(pieces) if len(pieces) <= 24 else 1,) + projections[0].shape, jnp.float32),
        pltpu.VMEM((nslab,) + projections[0].shape, jnp.float32),
        pltpu.VMEM((nslab * slots, depth), jnp.float32),
        pltpu.VMEM((2, rows, ngrid // nslab), jnp.float32),
        pltpu.VMEM((GROUP, rows, width), jnp.bfloat16),
        pltpu.VMEM((nslab, INFO, depth), jnp.float32),
        pltpu.VMEM((nslab, depth + 128), jnp.int32),
    ]
    need = sum(math.prod(b.shape) * b.dtype.itemsize for b in buffers)
    scratch = buffers + [
        pltpu.SMEM((nslab, depth + 128), jnp.int32),
        pltpu.SemaphoreType.DMA((len(pieces),)),
        pltpu.SemaphoreType.DMA((len(pieces),)),
        pltpu.SemaphoreType.DMA((len(infos),)),
        pltpu.SemaphoreType.DMA((2,)),
    ]
    return pl.pallas_call(
        functools.partial(apply_kernel, nslab, slots, nsum, pieces, infos),
        out_shape=jax.ShapeDtypeStruct((rows, ngrid), jnp.float32),
        in_specs=[SMEM, VMEM] + [ANY] * (len(arrays) + len(pieces)),
        out_specs=ANY,
        scratch_shapes=scratch,
        compiler_params=params(min(need + 4 * MIB, 63 * MIB)),
        name="apply",
    )(place, coupling, *arrays, *projections)


Piece = collections.namedtuple("Piece", ["array", "offset", "rows", "info", "index"])


def gather_and_project(projectors, described, mine, split, lanes, nband, nslab):
    slots = projectors.shape[0]
    order, at = cycle_tables(nslab)
    half = slots // 2
    quarter = half // 2
    reach = nslab // 2
    onward = [
        (b * nslab + order[i], b * nslab + order[(i + 1) % nslab])
        for b in range(nband)
        for i in range(nslab)
    ]
    backward = [(d, s) for s, d in onward]
    sibling = [(b * nslab + s, (b ^ 1) * nslab + s) for b in range(nband) for s in range(nslab)]

    where = [(0, 0, None)]
    for step in range(1, reach):
        where += [(-step, 0, False), (step, 0, False), (-step, 0, True), (step, 0, True)]
    where += [(reach, 0, False), (reach, quarter, False), (reach, 0, True), (reach, quarter, True)]
    boxes = split.shape[0] // nslab

    def entry(core, slab, distance, start, other):
        there = order[(at[slab] + distance) % nslab]
        if other is not None:
            start += half * ((1 - core) if other else core)
        return there, start, there * boxes

    table = [[entry(b % 2, s, *w) for w in where] for b in range(nband) for s in range(nslab)]
    me = lax.axis_index("band") * nslab + lax.axis_index("slab")
    place = lax.dynamic_index_in_dim(
        jnp.asarray(np.array(table, np.int32)), me, 0, keepdims=False
    ).reshape(-1)

    arrays, pieces, infos, projections = [described, projectors], [], [(0, 0)], []

    def add(array, info=None):
        arrays.append(array)
        own = len(arrays) - 1
        offset = INFO if info is None else 0
        pieces.append(
            Piece(own, offset, array.shape[0] - offset, own if info is None else info, len(pieces))
        )
        return own

    pieces.append(Piece(1, 0, slots, 0, 0))
    up = lax.ppermute(mine, AXES, onward)
    down = lax.ppermute(mine, AXES, backward)
    done = 0

    def project_new():
        nonlocal done
        projections.extend(project(arrays, pieces[done:], place, split, lanes))
        done = len(pieces)

    project_new()
    up, down, projections, place = lax.optimization_barrier((up, down, projections, place))
    projections = list(projections)
    for step in range(1, reach + 1):
        last = step == reach
        for array in (up,) if last else (up, down):
            infos.append((add(array), len(pieces) - 1))
        if last:
            add(down, len(arrays) - 1)
        near = [lax.ppermute(up, AXES, sibling), lax.ppermute(down, AXES, sibling)]
        if step + 1 < reach:
            up = lax.ppermute(up, AXES, onward)
            down = lax.ppermute(down, AXES, backward)
        elif not last:
            up = lax.ppermute(up[: INFO + quarter], AXES, onward)
            down = lax.ppermute(down[INFO + quarter :], AXES, backward)
        project_new()
        near, projections = lax.optimization_barrier((near, projections))
        near, projections = list(near), list(projections)
        add(near[0])
        add(near[1], len(arrays) - 1 if last else None)
        project_new()
        if not last:
            up, down, projections = lax.optimization_barrier((up, down, projections))
            projections = list(projections)
    return arrays, pieces, infos, projections, place


def body(bands, projectors, slot_atom, slot_box, channels, coupling):
    nblock, band_local, ngrid = bands.shape
    nband, nslab = lax.axis_size("band"), lax.axis_size("slab")
    natoms = channels.shape[0]
    atom_dev = natoms // nslab
    slots = slot_atom.shape[0]
    lanes = round_up(atom_dev, 128)

    described, mine = begin(slot_atom, slot_box, projectors, natoms, lanes)
    rows = nblock * band_local
    padded = round_up(rows, GROUP)
    x = bands.reshape(rows, ngrid)
    if padded != rows:
        x = jnp.pad(x, ((0, padded - rows), (0, 0)))
    split, masked = split_bands(x, coupling, channels, nslab, lanes)
    arrays, pieces, infos, projections, place = gather_and_project(
        projectors, described, mine, split, lanes, nband, nslab
    )
    out = apply(arrays, pieces, infos, projections, place, masked, nslab, slots, padded, ngrid)
    return out[:rows].reshape(nblock, band_local, ngrid)


def solution(mesh):
    in_specs = (P(None, ("band", "slab"), None), P("slab", None), P("slab"), P("slab"), P(), P())
    out_specs = P(None, ("band", "slab"), None)
    return jax.shard_map(body, mesh=mesh, in_specs=in_specs, out_specs=out_specs, check_vma=False)
```

```python
import collections
import functools
import math

import jax
import jax.numpy as jnp
import numpy as np
from jax import lax
from jax.experimental import pallas as pl
from jax.experimental.pallas import tpu as pltpu
from jax.sharding import PartitionSpec as P

BOXPTS = 64
GROUP = 16
INFO = 8
UNROLL = 8
AXES = ("band", "slab")
MIB = 1 << 20


def round_up(value, step):
    return (value + step - 1) // step * step


def cycle_tables(nslab):
    order = list(range(0, nslab, 2)) + list(range(nslab - 1 - nslab % 2, 0, -2))
    place = {s: i for i, s in enumerate(order)}
    return order, place


def params(limit):
    return pltpu.CompilerParams(vmem_limit_bytes=limit)


VMEM = pl.BlockSpec(memory_space=pltpu.VMEM)
SMEM = pl.BlockSpec(memory_space=pltpu.SMEM)
ANY = pl.BlockSpec(memory_space=pl.ANY)


def split_bands_kernel(atom_dev, x_ref, coupling_ref, channels_ref, out_ref, masked_ref, whole):
    @pl.when(pl.program_id(0) == 0)
    def _():
        channel = channels_ref.shape[0]
        natoms = channels_ref.shape[1]
        number = lax.broadcasted_iota(jnp.int32, (channel, natoms), 0)
        mask = jnp.where(number < channels_ref[...], 1.0, 0.0)
        for c in range(channel):
            own = slice(c * channel, (c + 1) * channel)
            whole[own, :] = coupling_ref[own, :] * mask * mask[c : c + 1, :]
        lanes = masked_ref.shape[2]
        for slab in range(masked_ref.shape[0]):
            base = slab * atom_dev // 128 * 128
            part = whole[:, base : min(base + lanes + 128, natoms)]
            if part.shape[1] < lanes:
                part = jnp.concatenate([part, part[:, : lanes - part.shape[1]]], axis=1)
            if slab * atom_dev != base:
                part = pltpu.roll(part, part.shape[1] - (slab * atom_dev - base), 1)
            masked_ref[slab] = part[:, :lanes]

    rows = x_ref.shape[0]
    low_half = lax.broadcasted_iota(jnp.int32, (rows, 128), 1) < BOXPTS
    zero = jnp.zeros((rows, 128), jnp.float32)

    def step(pair, carry):
        x = x_ref[:, pl.ds(pl.multiple_of(pair * 128, 128), 128)]
        high = x.astype(jnp.bfloat16).astype(jnp.float32)
        low = x - high
        high_turned = pltpu.roll(high, BOXPTS, 1)
        low_turned = pltpu.roll(low, BOXPTS, 1)
        out_ref[2 * pair, :, 0:128] = jnp.where(low_half, high, high_turned).astype(jnp.bfloat16)
        out_ref[2 * pair, :, 128:256] = jnp.where(low_half, low, zero).astype(jnp.bfloat16)
        out_ref[2 * pair + 1, :, 0:128] = jnp.where(low_half, high_turned, high).astype(jnp.bfloat16)
        out_ref[2 * pair + 1, :, 128:256] = jnp.where(low_half, low_turned, zero).astype(jnp.bfloat16)
        return carry

    lax.fori_loop(0, x_ref.shape[1] // 128, step, 0, unroll=4)


def split_bands(x, coupling, channels, nslab, lanes):
    rows, ngrid = x.shape
    channel, natoms = coupling.shape[1:]
    span = ngrid // nslab
    boxes = span // BOXPTS
    return pl.pallas_call(
        functools.partial(split_bands_kernel, natoms // nslab),
        grid=(nslab,),
        out_shape=[
            jax.ShapeDtypeStruct((ngrid // BOXPTS, rows, 256), jnp.bfloat16),
            jax.ShapeDtypeStruct((nslab, channel * channel, lanes), jnp.float32),
        ],
        in_specs=[
            pl.BlockSpec((rows, span), lambda i: (0, i)),
            pl.BlockSpec((channel * channel, natoms), lambda i: (0, 0)),
            pl.BlockSpec((channel, natoms), lambda i: (0, 0)),
        ],
        out_specs=[
            pl.BlockSpec((boxes, rows, 256), lambda i: (i, 0, 0)),
            pl.BlockSpec((nslab, channel * channel, lanes), lambda i: (0, 0, 0)),
        ],
        scratch_shapes=[pltpu.VMEM((channel * channel, natoms), jnp.float32)],
        compiler_params=params(16 * MIB),
        cost_estimate=pl.CostEstimate(
            flops=8 * x.size, bytes_accessed=12 * x.size, transcendentals=0
        ),
        name="split_bands",
    )(
        pltpu.with_memory_space_constraint(x, pltpu.HBM),
        coupling.reshape(channel * channel, natoms),
        jnp.broadcast_to(channels[None, :], (channel, natoms)),
    )


def slot_weights(values, low_half, axis):
    full, top = [], []
    for t in range(values.shape[1] // 128):
        x = values[:, t * 128 : (t + 1) * 128]
        high = x.astype(jnp.bfloat16).astype(jnp.float32)
        low = x - high
        turned = pltpu.roll(high, BOXPTS, 1)
        full.append(jnp.where(low_half, high, pltpu.roll(low, BOXPTS, 1)).astype(jnp.bfloat16))
        full.append(jnp.where(low_half, turned, low).astype(jnp.bfloat16))
        top.append(jnp.where(low_half, high, 0.0).astype(jnp.bfloat16))
        top.append(jnp.where(low_half, turned, 0.0).astype(jnp.bfloat16))
    return jnp.concatenate(
        [jnp.concatenate(full, axis=0), jnp.concatenate(top, axis=0)], axis=axis
    )


def live_groups(live, start, length):
    return lax.div(jnp.clip(live - start, 0, length) + (GROUP - 1), GROUP)


def begin_kernel(
    natoms, lanes, atom_hbm, box_hbm, projector_ref, info_ref, mine_ref, atom_ref, box_ref, sem
):
    reads = [
        pltpu.make_async_copy(atom_hbm, atom_ref, sem.at[0]),
        pltpu.make_async_copy(box_hbm, box_ref, sem.at[1]),
    ]
    for c in reads:
        c.start()
    nslab = lax.axis_size("slab")
    half = mine_ref.shape[0] - INFO
    core = lax.rem(lax.axis_index("band"), 2)
    copy = pltpu.make_async_copy(
        projector_ref.at[pl.ds(pl.multiple_of(core * half, GROUP), half), :],
        mine_ref.at[pl.ds(INFO, half), :],
        sem.at[2],
    )
    copy.start()
    for c in reads:
        c.wait()
    atom_dev = natoms // nslab
    below = lax.rem(lax.axis_index("slab") + nslab - 1, nslab) * atom_dev
    atom = atom_ref[...]
    slots = atom.shape[1]
    relative = atom - below
    relative = jnp.where(relative < 0, relative + natoms, relative)
    column = jnp.where(relative < atom_dev, relative, relative + (lanes - atom_dev))
    live = jnp.sum(jnp.where(atom >= 0, 1.0, 0.0), axis=1, keepdims=True)
    info_ref[...] = jnp.zeros(info_ref.shape, jnp.float32)
    info_ref[0:1, 0:slots] = box_ref[...].astype(jnp.float32)
    info_ref[1:2, 0:slots] = jnp.broadcast_to(live, (1, slots))
    info_ref[2:3, 0:slots] = jnp.where(atom >= 0, column, -1).astype(jnp.float32)
    head = pltpu.make_async_copy(info_ref, mine_ref.at[pl.ds(0, INFO), :], sem.at[0])
    head.start()
    head.wait()
    copy.wait()


def begin(slot_atom, slot_box, projectors, natoms, lanes):
    slots, depth = projectors.shape
    return pl.pallas_call(
        functools.partial(begin_kernel, natoms, lanes),
        out_shape=[
            jax.ShapeDtypeStruct((INFO, depth), jnp.float32),
            jax.ShapeDtypeStruct((INFO + slots // 2, depth), jnp.float32),
        ],
        in_specs=[ANY, ANY, ANY],
        out_specs=[VMEM, ANY],
        scratch_shapes=[
            pltpu.VMEM((1, slots), jnp.int32),
            pltpu.VMEM((1, slots), jnp.int32),
            pltpu.SemaphoreType.DMA((3,)),
        ],
        compiler_params=params(8 * MIB),
        name="begin",
    )(
        pltpu.with_memory_space_constraint(slot_atom.reshape(1, slots), pltpu.HBM),
        pltpu.with_memory_space_constraint(slot_box.reshape(1, slots), pltpu.HBM),
        pltpu.with_memory_space_constraint(projectors, pltpu.HBM),
    )


def scalar_row(info, first):
    return jnp.concatenate([info[0:1, :] + first, info[1:2, 0:128]], axis=1).astype(jnp.int32)


def project_kernel(pieces, infos, place_ref, x_ref, *refs):
    arrays = refs[: -len(pieces) - 4]
    outs = refs[-len(pieces) - 4 : -4]
    whole, proj, table, sem = refs[-4:]
    for k, index in enumerate(infos):
        whole[k : k + 1, :] = scalar_row(arrays[index][0:INFO, :], 0)
    copy = pltpu.make_async_copy(whole, table, sem)
    copy.start()
    rows = x_ref.shape[1]
    slots = arrays[infos[0]].shape[1]
    width = proj.shape[3]
    chunk = width // GROUP
    lane_block = lax.broadcasted_iota(jnp.int32, (rows, width), 1) // GROUP
    low_half = lax.broadcasted_iota(jnp.int32, (GROUP, 128), 1) < BOXPTS
    lane_slot = lax.broadcasted_iota(jnp.int32, (rows, width), 1) % GROUP
    proj[...] = jnp.zeros(proj.shape, jnp.float32)
    copy.wait()
    for which, p in enumerate(pieces):
        array = arrays[p.array]
        start = place_ref[3 * p.index + 1]
        box_base = place_ref[3 * p.index + 2]
        info = infos.index(p.info)
        count = live_groups(table[info, slots], start, p.rows)

        def step(block, carry):
            groups = [block * UNROLL + u for u in range(UNROLL)]
            weights, patches = [], []
            for g in groups:
                first = pl.multiple_of(p.offset + g * GROUP, 8)
                weights.append(slot_weights(array[pl.ds(first, GROUP), :], low_half, 1))
                boxes = [table[info, start + g * GROUP + s] for s in range(GROUP)]
                patches.append(jnp.concatenate([x_ref[box_base + b] for b in boxes], axis=0))
            totals = []
            for w, p_ in zip(weights, patches):
                product = lax.dot_general(
                    p_, w, (((1,), (1,)), ((), ())), preferred_element_type=jnp.float32
                )
                total = product[0:rows]
                for s in range(1, GROUP):
                    total = jnp.where(lane_slot == s, product[s * rows : (s + 1) * rows], total)
                totals.append(total)
            for g, total in zip(groups, totals):
                proj[which, g] = total
            return carry

        lax.fori_loop(0, lax.div(count + (UNROLL - 1), UNROLL), step, 0)

    for which, (p, out) in enumerate(zip(pieces, outs)):
        start = place_ref[3 * p.index + 1]
        columns = arrays[p.info][2:3, :]
        columns = pltpu.roll(columns, lax.rem(columns.shape[1] - start, columns.shape[1]), 1)
        nchunk = (p.rows // GROUP + chunk - 1) // chunk
        value = jnp.concatenate(
            [
                jnp.concatenate(
                    swap_blocks(
                        [proj[which, k * chunk + i] for i in range(chunk)], lane_block, width
                    ),
                    axis=0,
                )
                for k in range(nchunk)
            ],
            axis=1,
        )
        both = lax.dot_general(
            stacked_split(value),
            selector(columns[:, : nchunk * width], out.shape[1]),
            (((1,), (1,)), ((), ())),
            preferred_element_type=jnp.float32,
        )
        half = both.shape[0] // 2
        out[...] = both[:half] + both[half:]


def project(arrays, pieces, place, x, lanes):
    channel = arrays[0].shape[1] // BOXPTS
    used = sorted({p.array for p in pieces} | {p.info for p in pieces})
    local = [
        p._replace(array=used.index(p.array), info=used.index(p.info)) for p in pieces
    ]
    infos = sorted({p.info for p in local})
    shapes = [
        jax.ShapeDtypeStruct((channel * x.shape[1], 2 * lanes), jnp.float32) for p in pieces
    ]
    size = sum(p.rows for p in pieces) * arrays[0].shape[1]
    table = (round_up(len(infos), 8), arrays[0].shape[1] + 128)
    groups = round_up(max(p.rows for p in pieces), channel * GROUP) // GROUP
    return pl.pallas_call(
        functools.partial(project_kernel, local, infos),
        out_shape=shapes,
        in_specs=[SMEM, VMEM] + [VMEM] * len(used),
        out_specs=[VMEM] * len(pieces),
        scratch_shapes=[
            pltpu.VMEM(table, jnp.int32),
            pltpu.VMEM((len(pieces), groups, x.shape[1], channel * GROUP), jnp.float32),
            pltpu.SMEM(table, jnp.int32),
            pltpu.SemaphoreType.DMA(()),
        ],
        compiler_params=params(40 * MIB),
        cost_estimate=pl.CostEstimate(
            flops=2 * 16 * 16 * size, bytes_accessed=4 * size + 2 * x.size, transcendentals=0
        ),
        name="project",
    )(place, x, *[arrays[i] for i in used])


def swap_blocks(tiles, lane_block, width):
    tiles = list(tiles)
    bit = 1
    while bit < len(tiles):
        upper = (lane_block & bit) != 0
        for i in range(len(tiles)):
            if not i & bit:
                a, b = tiles[i], tiles[i | bit]
                tiles[i] = jnp.where(upper, pltpu.roll(b, GROUP * bit, 1), a)
                tiles[i | bit] = jnp.where(upper, b, pltpu.roll(a, width - GROUP * bit, 1))
        bit *= 2
    return tiles


def selector(columns, count):
    shape = (count, columns.shape[1])
    row = lax.broadcasted_iota(jnp.int32, shape, 0).astype(jnp.float32)
    return jnp.where(jnp.broadcast_to(columns, shape) == row, 1.0, 0.0).astype(jnp.bfloat16)


def stacked_split(value):
    high = value.astype(jnp.bfloat16)
    low = (value - high.astype(jnp.float32)).astype(jnp.bfloat16)
    return jnp.concatenate([high, low], axis=0)


def apply_kernel(nslab, slots, nsum, pieces, infos, place_ref, coupling_ref, *refs):
    npiece = len(pieces)
    proj, loaded, parts, beta, done, masks, info, whole, table = refs[-13:-4]
    sums = refs[-13 - nsum : -13]
    beta_sem, proj_sem, info_sem, out_sem = refs[-4:]
    base = len(refs) - 14 - nsum
    out_ref = refs[base]
    projections = refs[base - npiece : base]
    arrays = refs[: base - npiece]
    groups = slots // GROUP
    rows, width = proj.shape[1], proj.shape[2]
    channel = width // GROUP
    lanes = parts.shape[2] // 2
    boxes = out_ref.shape[1] // BOXPTS // nslab
    chunk = width // GROUP
    info_copies, copies, beta_copies = [], [], []
    for i, (array, index) in enumerate(infos):
        slab = place_ref[3 * index]
        info_copies.append(
            pltpu.make_async_copy(arrays[array].at[0:INFO, :], info.at[slab], info_sem.at[i])
        )
    for i, p in enumerate(pieces):
        slab, start = place_ref[3 * p.index], place_ref[3 * p.index + 1]
        j = i % loaded.shape[0]
        copies.append(
            pltpu.make_async_copy(projections[i], loaded.at[j], proj_sem.at[i])
        )
        first = pl.multiple_of(slab * slots + start, GROUP)
        beta_copies.append(
            pltpu.make_async_copy(
                arrays[p.array].at[p.offset : p.offset + p.rows, :],
                beta.at[pl.ds(first, p.rows), :],
                beta_sem.at[i],
            )
        )
    for c in info_copies + copies[: loaded.shape[0]]:
        c.start()
    lane_slot = lax.broadcasted_iota(jnp.int32, (rows, width), 1) % GROUP
    for s in range(GROUP):
        masks[s] = jnp.where(lane_slot == s, 1.0, 0.0).astype(jnp.bfloat16)
    for total in sums:
        total[...] = jnp.zeros(total.shape, jnp.float32)
    parts[...] = jnp.zeros(parts.shape, jnp.float32)
    for c in info_copies:
        c.wait()
    for slab in range(nslab):
        whole[slab : slab + 1, :] = scalar_row(info[slab], float(slab * boxes))
    to_scalars = pltpu.make_async_copy(whole, table, info_sem.at[0])
    to_scalars.start()
    for first in range(0, npiece, loaded.shape[0]):
        wave = range(first, min(first + loaded.shape[0], npiece))
        for i in wave:
            if first > 0:
                copies[i].start()
        for i in wave:
            copies[i].wait()
        for i in wave:
            slab = place_ref[3 * pieces[i].index]
            parts[slab] = parts[slab] + loaded[i % loaded.shape[0]]

    lane_block = lax.broadcasted_iota(jnp.int32, (rows, width), 1) // GROUP
    for c in beta_copies:
        c.start()

    def couple(slab, carry):
        following = lax.rem(slab + 1, nslab)
        total = parts[slab, :, lanes:] + parts[following, :, :lanes]
        for c in range(channel):
            mixed = jnp.zeros((rows, lanes), jnp.float32)
            for e in range(channel):
                factor = coupling_ref[slab, pl.ds(c * channel + e, 1), :]
                mixed = mixed + factor * total[e * rows : (e + 1) * rows]
            parts[slab, c * rows : (c + 1) * rows, lanes:] = mixed
        return carry

    lax.fori_loop(0, nslab, couple, 0)

    def spread(slab, carry):
        below = lax.rem(slab + nslab - 1, nslab)
        value = jnp.concatenate([parts[below, :, lanes:], parts[slab, :, lanes:]], axis=1)
        value = stacked_split(value)

        both = jnp.dot(
            value, selector(info[slab, 2:3, 0:slots], 2 * lanes), preferred_element_type=jnp.float32
        )
        half = both.shape[0] // 2
        both = both[:half] + both[half:]
        for k in range(groups // chunk):
            tiles = [
                both[c * rows : (c + 1) * rows, k * width : (k + 1) * width]
                for c in range(channel)
            ]
            for i, tile in enumerate(swap_blocks(tiles, lane_block, width)):
                proj[slab * groups + k * chunk + i] = tile
        return carry

    lax.fori_loop(0, nslab, spread, 0, unroll=4 if nsum > 1 else 1)
    to_scalars.wait()

    for c in beta_copies:
        c.wait()

    low_half = lax.broadcasted_iota(jnp.int32, (GROUP, 128), 1) < BOXPTS
    pair_half = lax.broadcasted_iota(jnp.int32, (rows, 128), 1) < BOXPTS
    span = boxes * BOXPTS

    def leaving(slab):
        slot = lax.rem(slab, 2)
        return pltpu.make_async_copy(
            done.at[slot],
            out_ref.at[:, pl.ds(pl.multiple_of(slab * span, 128), span)],
            out_sem.at[slot],
        )

    def slab_step(slab, carry):
        def step(block, inner):
            products = []
            for u in range(UNROLL):
                g = block * UNROLL + u
                slot_base = pl.multiple_of(slab * slots + g * GROUP, GROUP)
                weights = slot_weights(beta[pl.ds(slot_base, GROUP), :], low_half, 0)
                c = proj[slab * groups + g]
                high = c.astype(jnp.bfloat16)
                low = (c - high.astype(jnp.float32)).astype(jnp.bfloat16)
                left = jnp.concatenate(
                    [
                        jnp.concatenate([high * masks[s], low * masks[s]], axis=1)
                        for s in range(GROUP)
                    ],
                    axis=0,
                )
                products.append((slot_base, jnp.dot(left, weights, preferred_element_type=jnp.float32)))
            for u, (slot_base, product) in enumerate(products):
                for s in range(GROUP):
                    box = table[slab, block * (UNROLL * GROUP) + u * GROUP + s]
                    j = (u * GROUP + s) % nsum
                    sums[j][box] = sums[j][box] + product[s * rows : (s + 1) * rows]
            return inner

        count = live_groups(table[slab, info.shape[2]], 0, slots)
        lax.fori_loop(0, lax.div(count + (UNROLL - 1), UNROLL), step, 0)

        @pl.when(slab >= 2)
        def _():
            leaving(slab - 2).wait()

        def finish(pair, inner):
            folded = []
            for i in range(2):
                box = slab * boxes + 2 * pair + i
                value = sums[0][box]
                for j in range(1, nsum):
                    value = value + sums[j][box]
                folded.append(value + pltpu.roll(value, BOXPTS, 1))
            done[lax.rem(slab, 2), :, pl.ds(pl.multiple_of(pair * 128, 128), 128)] = jnp.where(
                pair_half, folded[0], folded[1]
            )
            return inner

        lax.fori_loop(0, span // 128, finish, 0, unroll=min(32, span // 128))
        leaving(slab).start()
        return carry

    lax.fori_loop(0, nslab, slab_step, 0)
    for slab in range(max(nslab - 2, 0), nslab):
        leaving(slab).wait()


def apply(arrays, pieces, infos, projections, place, coupling, nslab, slots, rows, ngrid):
    width = projections[0].shape[0] // rows * GROUP
    lanes = coupling.shape[2]
    depth = arrays[0].shape[1]
    one_sum = ngrid // BOXPTS * rows * 128 * 4
    nsum = 2 if one_sum <= 8 * MIB else 1
    buffers = [pltpu.VMEM((ngrid // BOXPTS, rows, 128), jnp.float32) for _ in range(nsum)]
    buffers += [
        pltpu.VMEM((nslab * slots // GROUP, rows, width), jnp.float32),
        pltpu.VMEM((len(pieces) if len(pieces) <= 24 else 1,) + projections[0].shape, jnp.float32),
        pltpu.VMEM((nslab,) + projections[0].shape, jnp.float32),
        pltpu.VMEM((nslab * slots, depth), jnp.float32),
        pltpu.VMEM((2, rows, ngrid // nslab), jnp.float32),
        pltpu.VMEM((GROUP, rows, width), jnp.bfloat16),
        pltpu.VMEM((nslab, INFO, depth), jnp.float32),
        pltpu.VMEM((nslab, depth + 128), jnp.int32),
    ]
    need = sum(math.prod(b.shape) * b.dtype.itemsize for b in buffers)
    scratch = buffers + [
        pltpu.SMEM((nslab, depth + 128), jnp.int32),
        pltpu.SemaphoreType.DMA((len(pieces),)),
        pltpu.SemaphoreType.DMA((len(pieces),)),
        pltpu.SemaphoreType.DMA((len(infos),)),
        pltpu.SemaphoreType.DMA((2,)),
    ]
    return pl.pallas_call(
        functools.partial(apply_kernel, nslab, slots, nsum, pieces, infos),
        out_shape=jax.ShapeDtypeStruct((rows, ngrid), jnp.float32),
        in_specs=[SMEM, VMEM] + [ANY] * (len(arrays) + len(pieces)),
        out_specs=ANY,
        scratch_shapes=scratch,
        compiler_params=params(min(need + 4 * MIB, 63 * MIB)),
        name="apply",
    )(place, coupling, *arrays, *projections)


Piece = collections.namedtuple("Piece", ["array", "offset", "rows", "info", "index"])


def gather_and_project(projectors, described, mine, split, lanes, nband, nslab):
    slots = projectors.shape[0]
    order, at = cycle_tables(nslab)
    half = slots // 2
    quarter = half // 2
    reach = nslab // 2
    onward = [
        (b * nslab + order[i], b * nslab + order[(i + 1) % nslab])
        for b in range(nband)
        for i in range(nslab)
    ]
    backward = [(d, s) for s, d in onward]
    sibling = [(b * nslab + s, (b ^ 1) * nslab + s) for b in range(nband) for s in range(nslab)]

    where = [(0, 0, None)]
    for step in range(1, reach):
        where += [(-step, 0, False), (step, 0, False), (-step, 0, True), (step, 0, True)]
    where += [(reach, 0, False), (reach, quarter, False), (reach, 0, True), (reach, quarter, True)]
    boxes = split.shape[0] // nslab

    def entry(core, slab, distance, start, other):
        there = order[(at[slab] + distance) % nslab]
        if other is not None:
            start += half * ((1 - core) if other else core)
        return there, start, there * boxes

    table = [[entry(b % 2, s, *w) for w in where] for b in range(nband) for s in range(nslab)]
    me = lax.axis_index("band") * nslab + lax.axis_index("slab")
    place = lax.dynamic_index_in_dim(
        jnp.asarray(np.array(table, np.int32)), me, 0, keepdims=False
    ).reshape(-1)

    arrays, pieces, infos, projections = [described, projectors], [], [(0, 0)], []

    def add(array, info=None):
        arrays.append(array)
        own = len(arrays) - 1
        offset = INFO if info is None else 0
        pieces.append(
            Piece(own, offset, array.shape[0] - offset, own if info is None else info, len(pieces))
        )
        return own

    pieces.append(Piece(1, 0, slots, 0, 0))
    up = lax.ppermute(mine, AXES, onward)
    down = lax.ppermute(mine, AXES, backward)
    done = 0

    def project_new():
        nonlocal done
        projections.extend(project(arrays, pieces[done:], place, split, lanes))
        done = len(pieces)

    project_new()
    up, down, projections, place = lax.optimization_barrier((up, down, projections, place))
    projections = list(projections)
    for step in range(1, reach + 1):
        last = step == reach
        for array in (up,) if last else (up, down):
            infos.append((add(array), len(pieces) - 1))
        if last:
            add(down, len(arrays) - 1)
        near = [up, down]
        if last:
            near = [lax.ppermute(x, AXES, sibling) for x in near]
        if step + 1 < reach:
            up = lax.ppermute(up, AXES, onward)
            down = lax.ppermute(down, AXES, backward)
        elif not last:
            up = lax.ppermute(up[: INFO + quarter], AXES, onward)
            down = lax.ppermute(down[INFO + quarter :], AXES, backward)
        project_new()
        near, projections = lax.optimization_barrier((near, projections))
        near, projections = list(near), list(projections)
        if not last:
            near = [lax.ppermute(x, AXES, sibling) for x in near]
        add(near[0])
        add(near[1], len(arrays) - 1 if last else None)
        project_new()
        if not last:
            up, down, projections = lax.optimization_barrier((up, down, projections))
            projections = list(projections)
    return arrays, pieces, infos, projections, place


def body(bands, projectors, slot_atom, slot_box, channels, coupling):
    nblock, band_local, ngrid = bands.shape
    nband, nslab = lax.axis_size("band"), lax.axis_size("slab")
    natoms = channels.shape[0]
    atom_dev = natoms // nslab
    slots = slot_atom.shape[0]
    lanes = round_up(atom_dev, 128)

    described, mine = begin(slot_atom, slot_box, projectors, natoms, lanes)
    rows = nblock * band_local
    padded = round_up(rows, GROUP)
    x = bands.reshape(rows, ngrid)
    if padded != rows:
        x = jnp.pad(x, ((0, padded - rows), (0, 0)))
    split, masked = split_bands(x, coupling, channels, nslab, lanes)
    arrays, pieces, infos, projections, place = gather_and_project(
        projectors, described, mine, split, lanes, nband, nslab
    )
    out = apply(arrays, pieces, infos, projections, place, masked, nslab, slots, padded, ngrid)
    return out[:rows].reshape(nblock, band_local, ngrid)


def solution(mesh):
    in_specs = (P(None, ("band", "slab"), None), P("slab", None), P("slab"), P("slab"), P(), P())
    out_specs = P(None, ("band", "slab"), None)
    return jax.shard_map(body, mesh=mesh, in_specs=in_specs, out_specs=out_specs, check_vma=False)
```

```python
import collections
import functools
import math

import jax
import jax.numpy as jnp
import numpy as np
from jax import lax
from jax.experimental import pallas as pl
from jax.experimental.pallas import tpu as pltpu
from jax.sharding import PartitionSpec as P

BOXPTS = 64
GROUP = 16
INFO = 8
UNROLL = 8
AXES = ("band", "slab")
MIB = 1 << 20


def round_up(value, step):
    return (value + step - 1) // step * step


def cycle_tables(nslab):
    order = list(range(0, nslab, 2)) + list(range(nslab - 1 - nslab % 2, 0, -2))
    place = {s: i for i, s in enumerate(order)}
    return order, place


def params(limit):
    return pltpu.CompilerParams(vmem_limit_bytes=limit)


VMEM = pl.BlockSpec(memory_space=pltpu.VMEM)
SMEM = pl.BlockSpec(memory_space=pltpu.SMEM)
ANY = pl.BlockSpec(memory_space=pl.ANY)


def split_bands_kernel(atom_dev, x_ref, coupling_ref, channels_ref, out_ref, masked_ref, whole):
    @pl.when(pl.program_id(0) == 0)
    def _():
        channel = channels_ref.shape[0]
        natoms = channels_ref.shape[1]
        number = lax.broadcasted_iota(jnp.int32, (channel, natoms), 0)
        mask = jnp.where(number < channels_ref[...], 1.0, 0.0)
        for c in range(channel):
            own = slice(c * channel, (c + 1) * channel)
            whole[own, :] = coupling_ref[own, :] * mask * mask[c : c + 1, :]
        lanes = masked_ref.shape[2]
        for slab in range(masked_ref.shape[0]):
            base = slab * atom_dev // 128 * 128
            part = whole[:, base : min(base + lanes + 128, natoms)]
            if part.shape[1] < lanes:
                part = jnp.concatenate([part, part[:, : lanes - part.shape[1]]], axis=1)
            if slab * atom_dev != base:
                part = pltpu.roll(part, part.shape[1] - (slab * atom_dev - base), 1)
            masked_ref[slab] = part[:, :lanes]

    rows = x_ref.shape[0]
    low_half = lax.broadcasted_iota(jnp.int32, (rows, 128), 1) < BOXPTS
    zero = jnp.zeros((rows, 128), jnp.float32)

    def step(pair, carry):
        x = x_ref[:, pl.ds(pl.multiple_of(pair * 128, 128), 128)]
        high = x.astype(jnp.bfloat16).astype(jnp.float32)
        low = x - high
        high_turned = pltpu.roll(high, BOXPTS, 1)
        low_turned = pltpu.roll(low, BOXPTS, 1)
        out_ref[2 * pair, :, 0:128] = jnp.where(low_half, high, high_turned).astype(jnp.bfloat16)
        out_ref[2 * pair, :, 128:256] = jnp.where(low_half, low, zero).astype(jnp.bfloat16)
        out_ref[2 * pair + 1, :, 0:128] = jnp.where(low_half, high_turned, high).astype(jnp.bfloat16)
        out_ref[2 * pair + 1, :, 128:256] = jnp.where(low_half, low_turned, zero).astype(jnp.bfloat16)
        return carry

    lax.fori_loop(0, x_ref.shape[1] // 128, step, 0, unroll=4)


def split_bands(x, coupling, channels, nslab, lanes):
    rows, ngrid = x.shape
    channel, natoms = coupling.shape[1:]
    span = ngrid // nslab
    boxes = span // BOXPTS
    return pl.pallas_call(
        functools.partial(split_bands_kernel, natoms // nslab),
        grid=(nslab,),
        out_shape=[
            jax.ShapeDtypeStruct((ngrid // BOXPTS, rows, 256), jnp.bfloat16),
            jax.ShapeDtypeStruct((nslab, channel * channel, lanes), jnp.float32),
        ],
        in_specs=[
            pl.BlockSpec((rows, span), lambda i: (0, i)),
            pl.BlockSpec((channel * channel, natoms), lambda i: (0, 0)),
            pl.BlockSpec((channel, natoms), lambda i: (0, 0)),
        ],
        out_specs=[
            pl.BlockSpec((boxes, rows, 256), lambda i: (i, 0, 0)),
            pl.BlockSpec((nslab, channel * channel, lanes), lambda i: (0, 0, 0)),
        ],
        scratch_shapes=[pltpu.VMEM((channel * channel, natoms), jnp.float32)],
        compiler_params=params(16 * MIB),
        cost_estimate=pl.CostEstimate(
            flops=8 * x.size, bytes_accessed=12 * x.size, transcendentals=0
        ),
        name="split_bands",
    )(
        pltpu.with_memory_space_constraint(x, pltpu.HBM),
        coupling.reshape(channel * channel, natoms),
        jnp.broadcast_to(channels[None, :], (channel, natoms)),
    )


def slot_weights(values, low_half, axis):
    full, top = [], []
    for t in range(values.shape[1] // 128):
        x = values[:, t * 128 : (t + 1) * 128]
        high = x.astype(jnp.bfloat16).astype(jnp.float32)
        low = x - high
        turned = pltpu.roll(high, BOXPTS, 1)
        full.append(jnp.where(low_half, high, pltpu.roll(low, BOXPTS, 1)).astype(jnp.bfloat16))
        full.append(jnp.where(low_half, turned, low).astype(jnp.bfloat16))
        top.append(jnp.where(low_half, high, 0.0).astype(jnp.bfloat16))
        top.append(jnp.where(low_half, turned, 0.0).astype(jnp.bfloat16))
    return jnp.concatenate(
        [jnp.concatenate(full, axis=0), jnp.concatenate(top, axis=0)], axis=axis
    )


def live_groups(live, start, length):
    return lax.div(jnp.clip(live - start, 0, length) + (GROUP - 1), GROUP)


def begin_kernel(
    natoms, lanes, atom_hbm, box_hbm, projector_ref, info_ref, mine_ref, atom_ref, box_ref, sem
):
    reads = [
        pltpu.make_async_copy(atom_hbm, atom_ref, sem.at[0]),
        pltpu.make_async_copy(box_hbm, box_ref, sem.at[1]),
    ]
    for c in reads:
        c.start()
    nslab = lax.axis_size("slab")
    half = mine_ref.shape[0] - INFO
    core = lax.rem(lax.axis_index("band"), 2)
    copy = pltpu.make_async_copy(
        projector_ref.at[pl.ds(pl.multiple_of(core * half, GROUP), half), :],
        mine_ref.at[pl.ds(INFO, half), :],
        sem.at[2],
    )
    copy.start()
    for c in reads:
        c.wait()
    atom_dev = natoms // nslab
    below = lax.rem(lax.axis_index("slab") + nslab - 1, nslab) * atom_dev
    atom = atom_ref[...]
    slots = atom.shape[1]
    relative = atom - below
    relative = jnp.where(relative < 0, relative + natoms, relative)
    column = jnp.where(relative < atom_dev, relative, relative + (lanes - atom_dev))
    live = jnp.sum(jnp.where(atom >= 0, 1.0, 0.0), axis=1, keepdims=True)
    info_ref[...] = jnp.zeros(info_ref.shape, jnp.float32)
    info_ref[0:1, 0:slots] = box_ref[...].astype(jnp.float32)
    info_ref[1:2, 0:slots] = jnp.broadcast_to(live, (1, slots))
    info_ref[2:3, 0:slots] = jnp.where(atom >= 0, column, -1).astype(jnp.float32)
    head = pltpu.make_async_copy(info_ref, mine_ref.at[pl.ds(0, INFO), :], sem.at[0])
    head.start()
    head.wait()
    copy.wait()


def begin(slot_atom, slot_box, projectors, natoms, lanes):
    slots, depth = projectors.shape
    return pl.pallas_call(
        functools.partial(begin_kernel, natoms, lanes),
        out_shape=[
            jax.ShapeDtypeStruct((INFO, depth), jnp.float32),
            jax.ShapeDtypeStruct((INFO + slots // 2, depth), jnp.float32),
        ],
        in_specs=[ANY, ANY, ANY],
        out_specs=[VMEM, ANY],
        scratch_shapes=[
            pltpu.VMEM((1, slots), jnp.int32),
            pltpu.VMEM((1, slots), jnp.int32),
            pltpu.SemaphoreType.DMA((3,)),
        ],
        compiler_params=params(8 * MIB),
        name="begin",
    )(
        pltpu.with_memory_space_constraint(slot_atom.reshape(1, slots), pltpu.HBM),
        pltpu.with_memory_space_constraint(slot_box.reshape(1, slots), pltpu.HBM),
        pltpu.with_memory_space_constraint(projectors, pltpu.HBM),
    )


def scalar_row(info, first):
    return jnp.concatenate([info[0:1, :] + first, info[1:2, 0:128]], axis=1).astype(jnp.int32)


def project_kernel(pieces, infos, place_ref, x_ref, *refs):
    arrays = refs[: -len(pieces) - 4]
    outs = refs[-len(pieces) - 4 : -4]
    whole, proj, table, sem = refs[-4:]
    for k, index in enumerate(infos):
        whole[k : k + 1, :] = scalar_row(arrays[index][0:INFO, :], 0)
    copy = pltpu.make_async_copy(whole, table, sem)
    copy.start()
    rows = x_ref.shape[1]
    slots = arrays[infos[0]].shape[1]
    width = proj.shape[3]
    chunk = width // GROUP
    lane_block = lax.broadcasted_iota(jnp.int32, (rows, width), 1) // GROUP
    low_half = lax.broadcasted_iota(jnp.int32, (GROUP, 128), 1) < BOXPTS
    lane_slot = lax.broadcasted_iota(jnp.int32, (rows, width), 1) % GROUP
    proj[...] = jnp.zeros(proj.shape, jnp.float32)
    copy.wait()
    for which, p in enumerate(pieces):
        array = arrays[p.array]
        start = place_ref[3 * p.index + 1]
        box_base = place_ref[3 * p.index + 2]
        info = infos.index(p.info)
        count = live_groups(table[info, slots], start, p.rows)

        def step(block, carry):
            groups = [block * UNROLL + u for u in range(UNROLL)]
            weights, patches = [], []
            for g in groups:
                first = pl.multiple_of(p.offset + g * GROUP, 8)
                weights.append(slot_weights(array[pl.ds(first, GROUP), :], low_half, 1))
                boxes = [table[info, start + g * GROUP + s] for s in range(GROUP)]
                patches.append(jnp.concatenate([x_ref[box_base + b] for b in boxes], axis=0))
            totals = []
            for w, p_ in zip(weights, patches):
                product = lax.dot_general(
                    p_, w, (((1,), (1,)), ((), ())), preferred_element_type=jnp.float32
                )
                total = product[0:rows]
                for s in range(1, GROUP):
                    total = jnp.where(lane_slot == s, product[s * rows : (s + 1) * rows], total)
                totals.append(total)
            for g, total in zip(groups, totals):
                proj[which, g] = total
            return carry

        lax.fori_loop(0, lax.div(count + (UNROLL - 1), UNROLL), step, 0)

    for which, (p, out) in enumerate(zip(pieces, outs)):
        start = place_ref[3 * p.index + 1]
        columns = arrays[p.info][2:3, :]
        columns = pltpu.roll(columns, lax.rem(columns.shape[1] - start, columns.shape[1]), 1)
        nchunk = (p.rows // GROUP + chunk - 1) // chunk
        value = jnp.concatenate(
            [
                jnp.concatenate(
                    swap_blocks(
                        [proj[which, k * chunk + i] for i in range(chunk)], lane_block, width
                    ),
                    axis=0,
                )
                for k in range(nchunk)
            ],
            axis=1,
        )
        both = lax.dot_general(
            stacked_split(value),
            selector(columns[:, : nchunk * width], out.shape[1]),
            (((1,), (1,)), ((), ())),
            preferred_element_type=jnp.float32,
        )
        half = both.shape[0] // 2
        out[...] = both[:half] + both[half:]


def project(arrays, pieces, place, x, lanes):
    channel = arrays[0].shape[1] // BOXPTS
    used = sorted({p.array for p in pieces} | {p.info for p in pieces})
    local = [
        p._replace(array=used.index(p.array), info=used.index(p.info)) for p in pieces
    ]
    infos = sorted({p.info for p in local})
    shapes = [
        jax.ShapeDtypeStruct((channel * x.shape[1], 2 * lanes), jnp.float32) for p in pieces
    ]
    size = sum(p.rows for p in pieces) * arrays[0].shape[1]
    table = (round_up(len(infos), 8), arrays[0].shape[1] + 128)
    groups = round_up(max(p.rows for p in pieces), channel * GROUP) // GROUP
    return pl.pallas_call(
        functools.partial(project_kernel, local, infos),
        out_shape=shapes,
        in_specs=[SMEM, VMEM] + [VMEM] * len(used),
        out_specs=[VMEM] * len(pieces),
        scratch_shapes=[
            pltpu.VMEM(table, jnp.int32),
            pltpu.VMEM((len(pieces), groups, x.shape[1], channel * GROUP), jnp.float32),
            pltpu.SMEM(table, jnp.int32),
            pltpu.SemaphoreType.DMA(()),
        ],
        compiler_params=params(40 * MIB),
        cost_estimate=pl.CostEstimate(
            flops=2 * 16 * 16 * size, bytes_accessed=4 * size + 2 * x.size, transcendentals=0
        ),
        name="project",
    )(place, x, *[arrays[i] for i in used])


def swap_blocks(tiles, lane_block, width):
    tiles = list(tiles)
    bit = 1
    while bit < len(tiles):
        upper = (lane_block & bit) != 0
        for i in range(len(tiles)):
            if not i & bit:
                a, b = tiles[i], tiles[i | bit]
                tiles[i] = jnp.where(upper, pltpu.roll(b, GROUP * bit, 1), a)
                tiles[i | bit] = jnp.where(upper, b, pltpu.roll(a, width - GROUP * bit, 1))
        bit *= 2
    return tiles


def selector(columns, count):
    shape = (count, columns.shape[1])
    row = lax.broadcasted_iota(jnp.int32, shape, 0).astype(jnp.float32)
    return jnp.where(jnp.broadcast_to(columns, shape) == row, 1.0, 0.0).astype(jnp.bfloat16)


def stacked_split(value):
    high = value.astype(jnp.bfloat16)
    low = (value - high.astype(jnp.float32)).astype(jnp.bfloat16)
    return jnp.concatenate([high, low], axis=0)


def apply_kernel(nslab, slots, nsum, pieces, infos, place_ref, coupling_ref, *refs):
    npiece = len(pieces)
    proj, loaded, parts, beta, done, masks, info, whole, table = refs[-13:-4]
    sums = refs[-13 - nsum : -13]
    beta_sem, proj_sem, info_sem, out_sem = refs[-4:]
    base = len(refs) - 14 - nsum
    out_ref = refs[base]
    projections = refs[base - npiece : base]
    arrays = refs[: base - npiece]
    groups = slots // GROUP
    rows, width = proj.shape[1], proj.shape[2]
    channel = width // GROUP
    lanes = parts.shape[2] // 2
    boxes = out_ref.shape[1] // BOXPTS // nslab
    chunk = width // GROUP
    info_copies, copies, beta_copies = [], [], []
    for i, (array, index) in enumerate(infos):
        slab = place_ref[3 * index]
        info_copies.append(
            pltpu.make_async_copy(arrays[array].at[0:INFO, :], info.at[slab], info_sem.at[i])
        )
    for i, p in enumerate(pieces):
        slab, start = place_ref[3 * p.index], place_ref[3 * p.index + 1]
        j = i % loaded.shape[0]
        copies.append(
            pltpu.make_async_copy(projections[i], loaded.at[j], proj_sem.at[i])
        )
        first = pl.multiple_of(slab * slots + start, GROUP)
        beta_copies.append(
            pltpu.make_async_copy(
                arrays[p.array].at[p.offset : p.offset + p.rows, :],
                beta.at[pl.ds(first, p.rows), :],
                beta_sem.at[i],
            )
        )
    for c in info_copies + copies[: loaded.shape[0]]:
        c.start()
    lane_slot = lax.broadcasted_iota(jnp.int32, (rows, width), 1) % GROUP
    for s in range(GROUP):
        masks[s] = jnp.where(lane_slot == s, 1.0, 0.0).astype(jnp.bfloat16)
    for total in sums:
        total[...] = jnp.zeros(total.shape, jnp.float32)
    parts[...] = jnp.zeros(parts.shape, jnp.float32)
    for c in info_copies:
        c.wait()
    for slab in range(nslab):
        whole[slab : slab + 1, :] = scalar_row(info[slab], float(slab * boxes))
    to_scalars = pltpu.make_async_copy(whole, table, info_sem.at[0])
    to_scalars.start()
    for first in range(0, npiece, loaded.shape[0]):
        wave = range(first, min(first + loaded.shape[0], npiece))
        for i in wave:
            if first > 0:
                copies[i].start()
        for i in wave:
            copies[i].wait()
        for i in wave:
            slab = place_ref[3 * pieces[i].index]
            parts[slab] = parts[slab] + loaded[i % loaded.shape[0]]

    lane_block = lax.broadcasted_iota(jnp.int32, (rows, width), 1) // GROUP
    for c in beta_copies:
        c.start()

    def couple(slab, carry):
        following = lax.rem(slab + 1, nslab)
        total = parts[slab, :, lanes:] + parts[following, :, :lanes]
        for c in range(channel):
            mixed = jnp.zeros((rows, lanes), jnp.float32)
            for e in range(channel):
                factor = coupling_ref[slab, pl.ds(c * channel + e, 1), :]
                mixed = mixed + factor * total[e * rows : (e + 1) * rows]
            parts[slab, c * rows : (c + 1) * rows, lanes:] = mixed
        return carry

    lax.fori_loop(0, nslab, couple, 0)

    def spread(slab, carry):
        below = lax.rem(slab + nslab - 1, nslab)
        value = jnp.concatenate([parts[below, :, lanes:], parts[slab, :, lanes:]], axis=1)
        value = stacked_split(value)

        both = jnp.dot(
            value, selector(info[slab, 2:3, 0:slots], 2 * lanes), preferred_element_type=jnp.float32
        )
        half = both.shape[0] // 2
        both = both[:half] + both[half:]
        for k in range(groups // chunk):
            tiles = [
                both[c * rows : (c + 1) * rows, k * width : (k + 1) * width]
                for c in range(channel)
            ]
            for i, tile in enumerate(swap_blocks(tiles, lane_block, width)):
                proj[slab * groups + k * chunk + i] = tile
        return carry

    lax.fori_loop(0, nslab, spread, 0, unroll=4 if nsum > 1 else 1)
    to_scalars.wait()

    for c in beta_copies:
        c.wait()

    low_half = lax.broadcasted_iota(jnp.int32, (GROUP, 128), 1) < BOXPTS
    pair_half = lax.broadcasted_iota(jnp.int32, (rows, 128), 1) < BOXPTS
    span = boxes * BOXPTS

    def leaving(slab):
        slot = lax.rem(slab, 2)
        return pltpu.make_async_copy(
            done.at[slot],
            out_ref.at[:, pl.ds(pl.multiple_of(slab * span, 128), span)],
            out_sem.at[slot],
        )

    def slab_step(slab, carry):
        def step(block, inner):
            products = []
            for u in range(UNROLL):
                g = block * UNROLL + u
                slot_base = pl.multiple_of(slab * slots + g * GROUP, GROUP)
                weights = slot_weights(beta[pl.ds(slot_base, GROUP), :], low_half, 0)
                c = proj[slab * groups + g]
                high = c.astype(jnp.bfloat16)
                low = (c - high.astype(jnp.float32)).astype(jnp.bfloat16)
                left = jnp.concatenate(
                    [
                        jnp.concatenate([high * masks[s], low * masks[s]], axis=1)
                        for s in range(GROUP)
                    ],
                    axis=0,
                )
                products.append((slot_base, jnp.dot(left, weights, preferred_element_type=jnp.float32)))
            for u, (slot_base, product) in enumerate(products):
                for s in range(GROUP):
                    box = table[slab, block * (UNROLL * GROUP) + u * GROUP + s]
                    j = (u * GROUP + s) % nsum
                    sums[j][box] = sums[j][box] + product[s * rows : (s + 1) * rows]
            return inner

        count = live_groups(table[slab, info.shape[2]], 0, slots)
        lax.fori_loop(0, lax.div(count + (UNROLL - 1), UNROLL), step, 0)

        @pl.when(slab >= 2)
        def _():
            leaving(slab - 2).wait()

        def finish(pair, inner):
            folded = []
            for i in range(2):
                box = slab * boxes + 2 * pair + i
                value = sums[0][box]
                for j in range(1, nsum):
                    value = value + sums[j][box]
                folded.append(value + pltpu.roll(value, BOXPTS, 1))
            done[lax.rem(slab, 2), :, pl.ds(pl.multiple_of(pair * 128, 128), 128)] = jnp.where(
                pair_half, folded[0], folded[1]
            )
            return inner

        lax.fori_loop(0, span // 128, finish, 0, unroll=min(32, span // 128))
        leaving(slab).start()
        return carry

    lax.fori_loop(0, nslab, slab_step, 0)
    for slab in range(max(nslab - 2, 0), nslab):
        leaving(slab).wait()


def apply(arrays, pieces, infos, projections, place, coupling, nslab, slots, rows, ngrid):
    width = projections[0].shape[0] // rows * GROUP
    lanes = coupling.shape[2]
    depth = arrays[0].shape[1]
    one_sum = ngrid // BOXPTS * rows * 128 * 4
    nsum = 2 if one_sum <= 8 * MIB else 1
    buffers = [pltpu.VMEM((ngrid // BOXPTS, rows, 128), jnp.float32) for _ in range(nsum)]
    buffers += [
        pltpu.VMEM((nslab * slots // GROUP, rows, width), jnp.float32),
        pltpu.VMEM((len(pieces) if len(pieces) <= 24 else 1,) + projections[0].shape, jnp.float32),
        pltpu.VMEM((nslab,) + projections[0].shape, jnp.float32),
        pltpu.VMEM((nslab * slots, depth), jnp.float32),
        pltpu.VMEM((2, rows, ngrid // nslab), jnp.float32),
        pltpu.VMEM((GROUP, rows, width), jnp.bfloat16),
        pltpu.VMEM((nslab, INFO, depth), jnp.float32),
        pltpu.VMEM((nslab, depth + 128), jnp.int32),
    ]
    need = sum(math.prod(b.shape) * b.dtype.itemsize for b in buffers)
    scratch = buffers + [
        pltpu.SMEM((nslab, depth + 128), jnp.int32),
        pltpu.SemaphoreType.DMA((len(pieces),)),
        pltpu.SemaphoreType.DMA((len(pieces),)),
        pltpu.SemaphoreType.DMA((len(infos),)),
        pltpu.SemaphoreType.DMA((2,)),
    ]
    return pl.pallas_call(
        functools.partial(apply_kernel, nslab, slots, nsum, pieces, infos),
        out_shape=jax.ShapeDtypeStruct((rows, ngrid), jnp.float32),
        in_specs=[SMEM, VMEM] + [ANY] * (len(arrays) + len(pieces)),
        out_specs=ANY,
        scratch_shapes=scratch,
        compiler_params=params(min(need + 4 * MIB, 63 * MIB)),
        name="apply",
    )(place, coupling, *arrays, *projections)


Piece = collections.namedtuple("Piece", ["array", "offset", "rows", "info", "index"])


def gather_and_project(projectors, described, mine, split, lanes, nband, nslab):
    slots = projectors.shape[0]
    order, at = cycle_tables(nslab)
    half = slots // 2
    quarter = half // 2
    reach = nslab // 2
    onward = [
        (b * nslab + order[i], b * nslab + order[(i + 1) % nslab])
        for b in range(nband)
        for i in range(nslab)
    ]
    backward = [(d, s) for s, d in onward]
    sibling = [(b * nslab + s, (b ^ 1) * nslab + s) for b in range(nband) for s in range(nslab)]

    where = [(0, 0, None)]
    for step in range(1, reach):
        where += [(1 - step, 0, True), (step - 1, 0, True)] if step > 1 else []
        where += [(-step, 0, False), (step, 0, False)]
    where += [(1 - reach, 0, True), (reach - 1, 0, True)]
    where += [(reach, 0, False), (reach, quarter, False), (reach, 0, True), (reach, quarter, True)]
    boxes = split.shape[0] // nslab

    def entry(core, slab, distance, start, other):
        there = order[(at[slab] + distance) % nslab]
        if other is not None:
            start += half * ((1 - core) if other else core)
        return there, start, there * boxes

    table = [[entry(b % 2, s, *w) for w in where] for b in range(nband) for s in range(nslab)]
    me = lax.axis_index("band") * nslab + lax.axis_index("slab")
    place = lax.dynamic_index_in_dim(
        jnp.asarray(np.array(table, np.int32)), me, 0, keepdims=False
    ).reshape(-1)

    arrays, pieces, infos, projections = [described, projectors], [], [(0, 0)], []

    def add(array, info=None):
        arrays.append(array)
        own = len(arrays) - 1
        offset = INFO if info is None else 0
        pieces.append(
            Piece(own, offset, array.shape[0] - offset, own if info is None else info, len(pieces))
        )
        return own

    pieces.append(Piece(1, 0, slots, 0, 0))
    up = lax.ppermute(mine, AXES, onward)
    down = lax.ppermute(mine, AXES, backward)
    done = 0

    def project_new():
        nonlocal done
        projections.extend(project(arrays, pieces[done:], place, split, lanes))
        done = len(pieces)

    project_new()
    up, down, projections, place = lax.optimization_barrier((up, down, projections, place))
    projections = list(projections)
    near = []
    for step in range(1, reach + 1):
        last = step == reach
        for array in near:
            add(array)
        for array in (up,) if last else (up, down):
            infos.append((add(array), len(pieces) - 1))
        if last:
            add(down, len(arrays) - 1)
        near = [lax.ppermute(up, AXES, sibling), lax.ppermute(down, AXES, sibling)]
        if step + 1 < reach:
            up = lax.ppermute(up, AXES, onward)
            down = lax.ppermute(down, AXES, backward)
        elif not last:
            up = lax.ppermute(up[: INFO + quarter], AXES, onward)
            down = lax.ppermute(down[INFO + quarter :], AXES, backward)
        project_new()
        up, down, near, projections = lax.optimization_barrier((up, down, near, projections))
        near, projections = list(near), list(projections)
    add(near[0])
    add(near[1], len(arrays) - 1)
    project_new()
    return arrays, pieces, infos, projections, place


def body(bands, projectors, slot_atom, slot_box, channels, coupling):
    nblock, band_local, ngrid = bands.shape
    nband, nslab = lax.axis_size("band"), lax.axis_size("slab")
    natoms = channels.shape[0]
    atom_dev = natoms // nslab
    slots = slot_atom.shape[0]
    lanes = round_up(atom_dev, 128)

    described, mine = begin(slot_atom, slot_box, projectors, natoms, lanes)
    rows = nblock * band_local
    padded = round_up(rows, GROUP)
    x = bands.reshape(rows, ngrid)
    if padded != rows:
        x = jnp.pad(x, ((0, padded - rows), (0, 0)))
    split, masked = split_bands(x, coupling, channels, nslab, lanes)
    arrays, pieces, infos, projections, place = gather_and_project(
        projectors, described, mine, split, lanes, nband, nslab
    )
    out = apply(arrays, pieces, infos, projections, place, masked, nslab, slots, padded, ngrid)
    return out[:rows].reshape(nblock, band_local, ngrid)


def solution(mesh):
    in_specs = (P(None, ("band", "slab"), None), P("slab", None), P("slab"), P("slab"), P(), P())
    out_specs = P(None, ("band", "slab"), None)
    return jax.shard_map(body, mesh=mesh, in_specs=in_specs, out_specs=out_specs, check_vma=False)
```

```python
import collections
import functools
import math

import jax
import jax.numpy as jnp
import numpy as np
from jax import lax
from jax.experimental import pallas as pl
from jax.experimental.pallas import tpu as pltpu
from jax.sharding import PartitionSpec as P

BOXPTS = 64
GROUP = 16
INFO = 8
UNROLL = 8
AXES = ("band", "slab")
MIB = 1 << 20


def round_up(value, step):
    return (value + step - 1) // step * step


def cycle_tables(nslab):
    order = list(range(0, nslab, 2)) + list(range(nslab - 1 - nslab % 2, 0, -2))
    place = {s: i for i, s in enumerate(order)}
    return order, place


def params(limit):
    return pltpu.CompilerParams(vmem_limit_bytes=limit)


VMEM = pl.BlockSpec(memory_space=pltpu.VMEM)
SMEM = pl.BlockSpec(memory_space=pltpu.SMEM)
ANY = pl.BlockSpec(memory_space=pl.ANY)


def split_bands_kernel(atom_dev, x_ref, coupling_ref, channels_ref, out_ref, masked_ref, whole):
    @pl.when(pl.program_id(0) == 0)
    def _():
        channel = channels_ref.shape[0]
        natoms = channels_ref.shape[1]
        number = lax.broadcasted_iota(jnp.int32, (channel, natoms), 0)
        mask = jnp.where(number < channels_ref[...], 1.0, 0.0)
        for c in range(channel):
            own = slice(c * channel, (c + 1) * channel)
            whole[own, :] = coupling_ref[own, :] * mask * mask[c : c + 1, :]
        lanes = masked_ref.shape[2]
        for slab in range(masked_ref.shape[0]):
            base = slab * atom_dev // 128 * 128
            part = whole[:, base : min(base + lanes + 128, natoms)]
            if part.shape[1] < lanes:
                part = jnp.concatenate([part, part[:, : lanes - part.shape[1]]], axis=1)
            if slab * atom_dev != base:
                part = pltpu.roll(part, part.shape[1] - (slab * atom_dev - base), 1)
            masked_ref[slab] = part[:, :lanes]

    rows = x_ref.shape[0]
    low_half = lax.broadcasted_iota(jnp.int32, (rows, 128), 1) < BOXPTS
    zero = jnp.zeros((rows, 128), jnp.float32)

    def step(pair, carry):
        x = x_ref[:, pl.ds(pl.multiple_of(pair * 128, 128), 128)]
        high = x.astype(jnp.bfloat16).astype(jnp.float32)
        low = x - high
        high_turned = pltpu.roll(high, BOXPTS, 1)
        low_turned = pltpu.roll(low, BOXPTS, 1)
        out_ref[2 * pair, :, 0:128] = jnp.where(low_half, high, high_turned).astype(jnp.bfloat16)
        out_ref[2 * pair, :, 128:256] = jnp.where(low_half, low, zero).astype(jnp.bfloat16)
        out_ref[2 * pair + 1, :, 0:128] = jnp.where(low_half, high_turned, high).astype(jnp.bfloat16)
        out_ref[2 * pair + 1, :, 128:256] = jnp.where(low_half, low_turned, zero).astype(jnp.bfloat16)
        return carry

    lax.fori_loop(0, x_ref.shape[1] // 128, step, 0, unroll=4)


def split_bands(x, coupling, channels, nslab, lanes):
    rows, ngrid = x.shape
    channel, natoms = coupling.shape[1:]
    span = ngrid // nslab
    boxes = span // BOXPTS
    return pl.pallas_call(
        functools.partial(split_bands_kernel, natoms // nslab),
        grid=(nslab,),
        out_shape=[
            jax.ShapeDtypeStruct((ngrid // BOXPTS, rows, 256), jnp.bfloat16),
            jax.ShapeDtypeStruct((nslab, channel * channel, lanes), jnp.float32),
        ],
        in_specs=[
            pl.BlockSpec((rows, span), lambda i: (0, i)),
            pl.BlockSpec((channel * channel, natoms), lambda i: (0, 0)),
            pl.BlockSpec((channel, natoms), lambda i: (0, 0)),
        ],
        out_specs=[
            pl.BlockSpec((boxes, rows, 256), lambda i: (i, 0, 0)),
            pl.BlockSpec((nslab, channel * channel, lanes), lambda i: (0, 0, 0)),
        ],
        scratch_shapes=[pltpu.VMEM((channel * channel, natoms), jnp.float32)],
        compiler_params=params(16 * MIB),
        cost_estimate=pl.CostEstimate(
            flops=8 * x.size, bytes_accessed=12 * x.size, transcendentals=0
        ),
        name="split_bands",
    )(
        pltpu.with_memory_space_constraint(x, pltpu.HBM),
        coupling.reshape(channel * channel, natoms),
        jnp.broadcast_to(channels[None, :], (channel, natoms)),
    )


def slot_weights(values, low_half, axis):
    full, top = [], []
    for t in range(values.shape[1] // 128):
        x = values[:, t * 128 : (t + 1) * 128]
        high = x.astype(jnp.bfloat16).astype(jnp.float32)
        low = x - high
        turned = pltpu.roll(high, BOXPTS, 1)
        full.append(jnp.where(low_half, high, pltpu.roll(low, BOXPTS, 1)).astype(jnp.bfloat16))
        full.append(jnp.where(low_half, turned, low).astype(jnp.bfloat16))
        top.append(jnp.where(low_half, high, 0.0).astype(jnp.bfloat16))
        top.append(jnp.where(low_half, turned, 0.0).astype(jnp.bfloat16))
    return jnp.concatenate(
        [jnp.concatenate(full, axis=0), jnp.concatenate(top, axis=0)], axis=axis
    )


def live_groups(live, start, length):
    return lax.div(jnp.clip(live - start, 0, length) + (GROUP - 1), GROUP)


def begin_kernel(
    natoms, lanes, atom_hbm, box_hbm, projector_ref, info_ref, mine_ref, atom_ref, box_ref, sem
):
    reads = [
        pltpu.make_async_copy(atom_hbm, atom_ref, sem.at[0]),
        pltpu.make_async_copy(box_hbm, box_ref, sem.at[1]),
    ]
    for c in reads:
        c.start()
    nslab = lax.axis_size("slab")
    half = mine_ref.shape[0] - INFO
    core = lax.rem(lax.axis_index("band"), 2)
    copy = pltpu.make_async_copy(
        projector_ref.at[pl.ds(pl.multiple_of(core * half, GROUP), half), :],
        mine_ref.at[pl.ds(INFO, half), :],
        sem.at[2],
    )
    copy.start()
    for c in reads:
        c.wait()
    atom_dev = natoms // nslab
    below = lax.rem(lax.axis_index("slab") + nslab - 1, nslab) * atom_dev
    atom = atom_ref[...]
    slots = atom.shape[1]
    relative = atom - below
    relative = jnp.where(relative < 0, relative + natoms, relative)
    column = jnp.where(relative < atom_dev, relative, relative + (lanes - atom_dev))
    live = jnp.sum(jnp.where(atom >= 0, 1.0, 0.0), axis=1, keepdims=True)
    info_ref[...] = jnp.zeros(info_ref.shape, jnp.float32)
    info_ref[0:1, 0:slots] = box_ref[...].astype(jnp.float32)
    info_ref[1:2, 0:slots] = jnp.broadcast_to(live, (1, slots))
    info_ref[2:3, 0:slots] = jnp.where(atom >= 0, column, -1).astype(jnp.float32)
    head = pltpu.make_async_copy(info_ref, mine_ref.at[pl.ds(0, INFO), :], sem.at[0])
    head.start()
    head.wait()
    copy.wait()


def begin(slot_atom, slot_box, projectors, natoms, lanes):
    slots, depth = projectors.shape
    return pl.pallas_call(
        functools.partial(begin_kernel, natoms, lanes),
        out_shape=[
            jax.ShapeDtypeStruct((INFO, depth), jnp.float32),
            jax.ShapeDtypeStruct((INFO + slots // 2, depth), jnp.float32),
        ],
        in_specs=[ANY, ANY, ANY],
        out_specs=[VMEM, ANY],
        scratch_shapes=[
            pltpu.VMEM((1, slots), jnp.int32),
            pltpu.VMEM((1, slots), jnp.int32),
            pltpu.SemaphoreType.DMA((3,)),
        ],
        compiler_params=params(8 * MIB),
        name="begin",
    )(
        pltpu.with_memory_space_constraint(slot_atom.reshape(1, slots), pltpu.HBM),
        pltpu.with_memory_space_constraint(slot_box.reshape(1, slots), pltpu.HBM),
        pltpu.with_memory_space_constraint(projectors, pltpu.HBM),
    )


def scalar_row(info, first):
    return jnp.concatenate([info[0:1, :] + first, info[1:2, 0:128]], axis=1).astype(jnp.int32)


def project_kernel(pieces, infos, place_ref, x_ref, *refs):
    arrays = refs[: -len(pieces) - 4]
    outs = refs[-len(pieces) - 4 : -4]
    whole, proj, table, sem = refs[-4:]
    for k, index in enumerate(infos):
        whole[k : k + 1, :] = scalar_row(arrays[index][0:INFO, :], 0)
    copy = pltpu.make_async_copy(whole, table, sem)
    copy.start()
    rows = x_ref.shape[1]
    slots = arrays[infos[0]].shape[1]
    width = proj.shape[3]
    chunk = width // GROUP
    lane_block = lax.broadcasted_iota(jnp.int32, (rows, width), 1) // GROUP
    low_half = lax.broadcasted_iota(jnp.int32, (GROUP, 128), 1) < BOXPTS
    lane_slot = lax.broadcasted_iota(jnp.int32, (rows, width), 1) % GROUP
    proj[...] = jnp.zeros(proj.shape, jnp.float32)
    copy.wait()
    for which, p in enumerate(pieces):
        array = arrays[p.array]
        start = place_ref[3 * p.index + 1]
        box_base = place_ref[3 * p.index + 2]
        info = infos.index(p.info)
        count = live_groups(table[info, slots], start, p.rows)

        def step(block, carry):
            groups = [block * UNROLL + u for u in range(UNROLL)]
            weights, patches = [], []
            for g in groups:
                first = pl.multiple_of(p.offset + g * GROUP, 8)
                weights.append(slot_weights(array[pl.ds(first, GROUP), :], low_half, 1))
                boxes = [table[info, start + g * GROUP + s] for s in range(GROUP)]
                patches.append(jnp.concatenate([x_ref[box_base + b] for b in boxes], axis=0))
            totals = []
            for w, p_ in zip(weights, patches):
                product = lax.dot_general(
                    p_, w, (((1,), (1,)), ((), ())), preferred_element_type=jnp.float32
                )
                total = product[0:rows]
                for s in range(1, GROUP):
                    total = jnp.where(lane_slot == s, product[s * rows : (s + 1) * rows], total)
                totals.append(total)
            for g, total in zip(groups, totals):
                proj[which, g] = total
            return carry

        lax.fori_loop(0, lax.div(count + (UNROLL - 1), UNROLL), step, 0)

    for which, (p, out) in enumerate(zip(pieces, outs)):
        start = place_ref[3 * p.index + 1]
        columns = arrays[p.info][2:3, :]
        columns = pltpu.roll(columns, lax.rem(columns.shape[1] - start, columns.shape[1]), 1)
        nchunk = (p.rows // GROUP + chunk - 1) // chunk
        value = jnp.concatenate(
            [
                jnp.concatenate(
                    swap_blocks(
                        [proj[which, k * chunk + i] for i in range(chunk)], lane_block, width
                    ),
                    axis=0,
                )
                for k in range(nchunk)
            ],
            axis=1,
        )
        both = lax.dot_general(
            stacked_split(value),
            selector(columns[:, : nchunk * width], out.shape[1]),
            (((1,), (1,)), ((), ())),
            preferred_element_type=jnp.float32,
        )
        half = both.shape[0] // 2
        out[...] = both[:half] + both[half:]


def project(arrays, pieces, place, x, lanes):
    channel = arrays[0].shape[1] // BOXPTS
    used = sorted({p.array for p in pieces} | {p.info for p in pieces})
    local = [
        p._replace(array=used.index(p.array), info=used.index(p.info)) for p in pieces
    ]
    infos = sorted({p.info for p in local})
    shapes = [
        jax.ShapeDtypeStruct((channel * x.shape[1], 2 * lanes), jnp.float32) for p in pieces
    ]
    size = sum(p.rows for p in pieces) * arrays[0].shape[1]
    table = (round_up(len(infos), 8), arrays[0].shape[1] + 128)
    groups = round_up(max(p.rows for p in pieces), channel * GROUP) // GROUP
    return pl.pallas_call(
        functools.partial(project_kernel, local, infos),
        out_shape=shapes,
        in_specs=[SMEM, VMEM] + [VMEM] * len(used),
        out_specs=[VMEM] * len(pieces),
        scratch_shapes=[
            pltpu.VMEM(table, jnp.int32),
            pltpu.VMEM((len(pieces), groups, x.shape[1], channel * GROUP), jnp.float32),
            pltpu.SMEM(table, jnp.int32),
            pltpu.SemaphoreType.DMA(()),
        ],
        compiler_params=params(40 * MIB),
        cost_estimate=pl.CostEstimate(
            flops=2 * 16 * 16 * size, bytes_accessed=4 * size + 2 * x.size, transcendentals=0
        ),
        name="project",
    )(place, x, *[arrays[i] for i in used])


def swap_blocks(tiles, lane_block, width):
    tiles = list(tiles)
    bit = 1
    while bit < len(tiles):
        upper = (lane_block & bit) != 0
        for i in range(len(tiles)):
            if not i & bit:
                a, b = tiles[i], tiles[i | bit]
                tiles[i] = jnp.where(upper, pltpu.roll(b, GROUP * bit, 1), a)
                tiles[i | bit] = jnp.where(upper, b, pltpu.roll(a, width - GROUP * bit, 1))
        bit *= 2
    return tiles


def selector(columns, count):
    shape = (count, columns.shape[1])
    row = lax.broadcasted_iota(jnp.int32, shape, 0).astype(jnp.float32)
    return jnp.where(jnp.broadcast_to(columns, shape) == row, 1.0, 0.0).astype(jnp.bfloat16)


def stacked_split(value):
    high = value.astype(jnp.bfloat16)
    low = (value - high.astype(jnp.float32)).astype(jnp.bfloat16)
    return jnp.concatenate([high, low], axis=0)


def apply_kernel(nslab, slots, nsum, pieces, infos, place_ref, coupling_ref, *refs):
    npiece = len(pieces)
    proj, loaded, parts, beta, done, masks, info, whole, table = refs[-13:-4]
    sums = refs[-13 - nsum : -13]
    beta_sem, proj_sem, info_sem, out_sem = refs[-4:]
    base = len(refs) - 14 - nsum
    out_ref = refs[base]
    projections = refs[base - npiece : base]
    arrays = refs[: base - npiece]
    groups = slots // GROUP
    rows, width = proj.shape[1], proj.shape[2]
    channel = width // GROUP
    lanes = parts.shape[2] // 2
    boxes = out_ref.shape[1] // BOXPTS // nslab
    chunk = width // GROUP
    info_copies, copies, beta_copies = [], [], []
    for i, (array, index) in enumerate(infos):
        slab = place_ref[3 * index]
        info_copies.append(
            pltpu.make_async_copy(arrays[array].at[0:INFO, :], info.at[slab], info_sem.at[i])
        )
    for i, p in enumerate(pieces):
        slab, start = place_ref[3 * p.index], place_ref[3 * p.index + 1]
        j = i % loaded.shape[0]
        copies.append(
            pltpu.make_async_copy(projections[i], loaded.at[j], proj_sem.at[i])
        )
        first = pl.multiple_of(slab * slots + start, GROUP)
        beta_copies.append(
            pltpu.make_async_copy(
                arrays[p.array].at[p.offset : p.offset + p.rows, :],
                beta.at[pl.ds(first, p.rows), :],
                beta_sem.at[i],
            )
        )
    for c in info_copies + copies[: loaded.shape[0]]:
        c.start()
    lane_slot = lax.broadcasted_iota(jnp.int32, (rows, width), 1) % GROUP
    for s in range(GROUP):
        masks[s] = jnp.where(lane_slot == s, 1.0, 0.0).astype(jnp.bfloat16)
    for total in sums:
        total[...] = jnp.zeros(total.shape, jnp.float32)
    parts[...] = jnp.zeros(parts.shape, jnp.float32)
    for c in info_copies:
        c.wait()
    for slab in range(nslab):
        whole[slab : slab + 1, :] = scalar_row(info[slab], float(slab * boxes))
    to_scalars = pltpu.make_async_copy(whole, table, info_sem.at[0])
    to_scalars.start()
    for first in range(0, npiece, loaded.shape[0]):
        wave = range(first, min(first + loaded.shape[0], npiece))
        for i in wave:
            if first > 0:
                copies[i].start()
        for i in wave:
            copies[i].wait()
        for i in wave:
            slab = place_ref[3 * pieces[i].index]
            parts[slab] = parts[slab] + loaded[i % loaded.shape[0]]

    lane_block = lax.broadcasted_iota(jnp.int32, (rows, width), 1) // GROUP
    for c in beta_copies:
        c.start()

    def couple(slab, carry):
        following = lax.rem(slab + 1, nslab)
        total = parts[slab, :, lanes:] + parts[following, :, :lanes]
        for c in range(channel):
            mixed = jnp.zeros((rows, lanes), jnp.float32)
            for e in range(channel):
                factor = coupling_ref[slab, pl.ds(c * channel + e, 1), :]
                mixed = mixed + factor * total[e * rows : (e + 1) * rows]
            parts[slab, c * rows : (c + 1) * rows, lanes:] = mixed
        return carry

    lax.fori_loop(0, nslab, couple, 0)

    def spread(slab, carry):
        below = lax.rem(slab + nslab - 1, nslab)
        value = jnp.concatenate([parts[below, :, lanes:], parts[slab, :, lanes:]], axis=1)
        value = stacked_split(value)

        both = jnp.dot(
            value, selector(info[slab, 2:3, 0:slots], 2 * lanes), preferred_element_type=jnp.float32
        )
        half = both.shape[0] // 2
        both = both[:half] + both[half:]
        for k in range(groups // chunk):
            tiles = [
                both[c * rows : (c + 1) * rows, k * width : (k + 1) * width]
                for c in range(channel)
            ]
            for i, tile in enumerate(swap_blocks(tiles, lane_block, width)):
                proj[slab * groups + k * chunk + i] = tile
        return carry

    lax.fori_loop(0, nslab, spread, 0, unroll=4 if nsum > 1 else 1)
    to_scalars.wait()

    for c in beta_copies:
        c.wait()

    low_half = lax.broadcasted_iota(jnp.int32, (GROUP, 128), 1) < BOXPTS
    pair_half = lax.broadcasted_iota(jnp.int32, (rows, 128), 1) < BOXPTS
    span = boxes * BOXPTS

    def leaving(slab):
        slot = lax.rem(slab, 2)
        return pltpu.make_async_copy(
            done.at[slot],
            out_ref.at[:, pl.ds(pl.multiple_of(slab * span, 128), span)],
            out_sem.at[slot],
        )

    def slab_step(slab, carry):
        def step(block, inner):
            products = []
            for u in range(UNROLL):
                g = block * UNROLL + u
                slot_base = pl.multiple_of(slab * slots + g * GROUP, GROUP)
                weights = slot_weights(beta[pl.ds(slot_base, GROUP), :], low_half, 0)
                c = proj[slab * groups + g]
                high = c.astype(jnp.bfloat16)
                low = (c - high.astype(jnp.float32)).astype(jnp.bfloat16)
                left = jnp.concatenate(
                    [
                        jnp.concatenate([high * masks[s], low * masks[s]], axis=1)
                        for s in range(GROUP)
                    ],
                    axis=0,
                )
                products.append((slot_base, jnp.dot(left, weights, preferred_element_type=jnp.float32)))
            for u, (slot_base, product) in enumerate(products):
                for s in range(GROUP):
                    box = table[slab, block * (UNROLL * GROUP) + u * GROUP + s]
                    j = (u * GROUP + s) % nsum
                    sums[j][box] = sums[j][box] + product[s * rows : (s + 1) * rows]
            return inner

        count = live_groups(table[slab, info.shape[2]], 0, slots)
        lax.fori_loop(0, lax.div(count + (UNROLL - 1), UNROLL), step, 0)

        @pl.when(slab >= 2)
        def _():
            leaving(slab - 2).wait()

        def finish(pair, inner):
            folded = []
            for i in range(2):
                box = slab * boxes + 2 * pair + i
                value = sums[0][box]
                for j in range(1, nsum):
                    value = value + sums[j][box]
                folded.append(value + pltpu.roll(value, BOXPTS, 1))
            done[lax.rem(slab, 2), :, pl.ds(pl.multiple_of(pair * 128, 128), 128)] = jnp.where(
                pair_half, folded[0], folded[1]
            )
            return inner

        lax.fori_loop(0, span // 128, finish, 0, unroll=min(32, span // 128))
        leaving(slab).start()
        return carry

    lax.fori_loop(0, nslab, slab_step, 0)
    for slab in range(max(nslab - 2, 0), nslab):
        leaving(slab).wait()


def apply(arrays, pieces, infos, projections, place, coupling, nslab, slots, rows, ngrid):
    width = projections[0].shape[0] // rows * GROUP
    lanes = coupling.shape[2]
    depth = arrays[0].shape[1]
    one_sum = ngrid // BOXPTS * rows * 128 * 4
    nsum = 2 if one_sum <= 8 * MIB else 1
    buffers = [pltpu.VMEM((ngrid // BOXPTS, rows, 128), jnp.float32) for _ in range(nsum)]
    buffers += [
        pltpu.VMEM((nslab * slots // GROUP, rows, width), jnp.float32),
        pltpu.VMEM((len(pieces) if len(pieces) <= 24 else 1,) + projections[0].shape, jnp.float32),
        pltpu.VMEM((nslab,) + projections[0].shape, jnp.float32),
        pltpu.VMEM((nslab * slots, depth), jnp.float32),
        pltpu.VMEM((2, rows, ngrid // nslab), jnp.float32),
        pltpu.VMEM((GROUP, rows, width), jnp.bfloat16),
        pltpu.VMEM((nslab, INFO, depth), jnp.float32),
        pltpu.VMEM((nslab, depth + 128), jnp.int32),
    ]
    need = sum(math.prod(b.shape) * b.dtype.itemsize for b in buffers)
    scratch = buffers + [
        pltpu.SMEM((nslab, depth + 128), jnp.int32),
        pltpu.SemaphoreType.DMA((len(pieces),)),
        pltpu.SemaphoreType.DMA((len(pieces),)),
        pltpu.SemaphoreType.DMA((len(infos),)),
        pltpu.SemaphoreType.DMA((2,)),
    ]
    return pl.pallas_call(
        functools.partial(apply_kernel, nslab, slots, nsum, pieces, infos),
        out_shape=jax.ShapeDtypeStruct((rows, ngrid), jnp.float32),
        in_specs=[SMEM, VMEM] + [ANY] * (len(arrays) + len(pieces)),
        out_specs=ANY,
        scratch_shapes=scratch,
        compiler_params=params(min(need + 4 * MIB, 63 * MIB)),
        name="apply",
    )(place, coupling, *arrays, *projections)


Piece = collections.namedtuple("Piece", ["array", "offset", "rows", "info", "index"])


def gather_and_project(projectors, described, mine, split, lanes, nband, nslab):
    slots = projectors.shape[0]
    order, at = cycle_tables(nslab)
    half = slots // 2
    quarter = half // 2
    reach = nslab // 2
    onward = [
        (b * nslab + order[i], b * nslab + order[(i + 1) % nslab])
        for b in range(nband)
        for i in range(nslab)
    ]
    backward = [(d, s) for s, d in onward]
    sibling = [(b * nslab + s, (b ^ 1) * nslab + s) for b in range(nband) for s in range(nslab)]

    where = [(0, 0, None)]
    for step in range(1, reach):
        where += [(1 - step, 0, True), (step - 1, 0, True)] if step > 1 else []
        where += [(-step, 0, False), (step, 0, False)]
    where += [(1 - reach, 0, True), (reach - 1, 0, True)]
    where += [(reach, 0, False), (reach, quarter, False), (reach, 0, True), (reach, quarter, True)]
    boxes = split.shape[0] // nslab

    def entry(core, slab, distance, start, other):
        there = order[(at[slab] + distance) % nslab]
        if other is not None:
            start += half * ((1 - core) if other else core)
        return there, start, there * boxes

    table = [[entry(b % 2, s, *w) for w in where] for b in range(nband) for s in range(nslab)]
    me = lax.axis_index("band") * nslab + lax.axis_index("slab")
    place = lax.dynamic_index_in_dim(
        jnp.asarray(np.array(table, np.int32)), me, 0, keepdims=False
    ).reshape(-1)

    arrays, pieces, infos, projections = [described, projectors], [], [(0, 0)], []

    def add(array, info=None):
        arrays.append(array)
        own = len(arrays) - 1
        offset = INFO if info is None else 0
        pieces.append(
            Piece(own, offset, array.shape[0] - offset, own if info is None else info, len(pieces))
        )
        return own

    pieces.append(Piece(1, 0, slots, 0, 0))
    up = lax.ppermute(mine, AXES, onward)
    down = lax.ppermute(mine, AXES, backward)
    done = 0

    def project_new():
        nonlocal done
        projections.extend(project(arrays, pieces[done:], place, split, lanes))
        done = len(pieces)

    project_new()
    up, down, projections, place = lax.optimization_barrier((up, down, projections, place))
    projections = list(projections)
    near = []
    for step in range(1, reach + 1):
        last = step == reach
        for array in near:
            add(array)
        for array in (up,) if last else (up, down):
            infos.append((add(array), len(pieces) - 1))
        if last:
            add(down, len(arrays) - 1)
        near = [lax.ppermute(up, AXES, sibling), lax.ppermute(down, AXES, sibling)]
        if step + 1 < reach:
            up = lax.ppermute(up, AXES, onward)
            down = lax.ppermute(down, AXES, backward)
        elif not last:
            up = lax.ppermute(up[: INFO + quarter], AXES, onward)
            down = lax.ppermute(down[INFO + quarter :], AXES, backward)
        project_new()
        if step + 1 == reach:
            for array in near:
                add(array)
            near = []
            project_new()
        up, down, near, projections = lax.optimization_barrier((up, down, near, projections))
        near, projections = list(near), list(projections)
    add(near[0])
    add(near[1], len(arrays) - 1)
    project_new()
    return arrays, pieces, infos, projections, place


def body(bands, projectors, slot_atom, slot_box, channels, coupling):
    nblock, band_local, ngrid = bands.shape
    nband, nslab = lax.axis_size("band"), lax.axis_size("slab")
    natoms = channels.shape[0]
    atom_dev = natoms // nslab
    slots = slot_atom.shape[0]
    lanes = round_up(atom_dev, 128)

    described, mine = begin(slot_atom, slot_box, projectors, natoms, lanes)
    rows = nblock * band_local
    padded = round_up(rows, GROUP)
    x = bands.reshape(rows, ngrid)
    if padded != rows:
        x = jnp.pad(x, ((0, padded - rows), (0, 0)))
    split, masked = split_bands(x, coupling, channels, nslab, lanes)
    arrays, pieces, infos, projections, place = gather_and_project(
        projectors, described, mine, split, lanes, nband, nslab
    )
    out = apply(arrays, pieces, infos, projections, place, masked, nslab, slots, padded, ngrid)
    return out[:rows].reshape(nblock, band_local, ngrid)


def solution(mesh):
    in_specs = (P(None, ("band", "slab"), None), P("slab", None), P("slab"), P("slab"), P(), P())
    out_specs = P(None, ("band", "slab"), None)
    return jax.shard_map(body, mesh=mesh, in_specs=in_specs, out_specs=out_specs, check_vma=False)
```
